32 devices in a mesh: dp: 8 (over z, y), seq: 4 (over x, core).
Axes of the slice: x: 2, y: 2, z: 4, core: 2. Of those that a mesh axis runs over, the one named last changes fastest.
Arguments:
- tokens: bfloat16 [8, 512, 1088], P('dp', 'seq'), may hold values from -6 to 6
- order: int32 [8, 512], P('dp'), may hold values from 0 to 511, as said below
- cotangent: bfloat16 [8, 512, 1088], P('dp', 'seq'), may hold values from -6 to 6
- qkv_weight: bfloat16 [3551232], P(('dp', 'seq')), may hold values from -0.1875 to 0.1875
- out_weight: bfloat16 [1183744], P(('dp', 'seq')), may hold values from -0.75 to 0.75
- up_weight: bfloat16 [4734976], P(('dp', 'seq')), may hold values from -0.1875 to 0.1875
- down_weight: bfloat16 [4734976], P(('dp', 'seq')), may hold values from -0.09375 to 0.09375
- small_params: bfloat16 [13056], P(('dp', 'seq')), may hold values from -0.6 to 1.4, as said below
Outputs:
- mixed: bfloat16 [8, 512, 1088], P('dp', 'seq')
- input_grad: bfloat16 [8, 512, 1088], P('dp', 'seq')
- qkv_grad: float32 [3551232], P(('dp', 'seq'))
- out_grad: float32 [1183744], P(('dp', 'seq'))
- up_grad: float32 [4734976], P(('dp', 'seq'))
- down_grad: float32 [4734976], P(('dp', 'seq'))
- small_grad: float32 [13056], P(('dp', 'seq'))
The draws below stay inside these ranges and needn't reach their ends.
Inputs may be any that keep to these rules, and one draw needn't show every extreme that they name: Each row is a permutation of the positions. Its slots form 2 * 4 runs of 64 consecutive positions; the slots of index i of seq hold stretches c and 7 - c in either order, with c drawn per sequence. `small_params`: the two norm gains lie in 0.6 to 1.4.
All inputs are finite; a program needn't handle non-finite values.
Results may differ from the reference program's by a relative error of at most 0.015.
Values may be sent and summed in bfloat16 or wider, within the bound.
No kernel may reach another device: no remote copies, remote signals or barrier semaphores. Data moves between devices by JAX's collectives and lax.ppermute only.
A program may use at most 384 MiB of HBM per device.

```python
import math
import jax
import jax.numpy as jnp
from jax import lax

D = 1088
FF = 4352
HD = 64
LEN = 512
SEQS = 8
PAIRS = 4
STRETCH = 64
SMALLP = 13056


def draw_order(key, part):
    key = jax.random.fold_in(key, 7)
    key_list = jax.random.split(key, SEQS + 1)
    pair_perm = jax.vmap(lambda one_key: jax.random.permutation(one_key, PAIRS))(key_list[:SEQS])
    flip_bits = jax.random.randint(key_list[SEQS], (SEQS, PAIRS), 0, 2)
    mirrored = 2 * PAIRS - 1 - pair_perm
    first_stretch = jnp.where(flip_bits == 1, mirrored, pair_perm)
    second_stretch = jnp.where(flip_bits == 1, pair_perm, mirrored)
    stretch_ids = jnp.stack([first_stretch, second_stretch], axis=2).reshape(SEQS, 2 * PAIRS)
    positions = stretch_ids[:, :, None] * STRETCH + jnp.arange(STRETCH, dtype=jnp.int32)[None, None, :]
    return positions.reshape(SEQS, LEN).astype(jnp.int32)


def draw_small_params(key, part):
    key = jax.random.fold_in(key, 13)
    gain_key, bias_key = jax.random.split(key)
    position = jnp.arange(SMALLP)
    is_gain = (position < D) | (position >= 5 * D) & (position < 6 * D)
    gains = jax.random.uniform(gain_key, (SMALLP,), jnp.float32, 0.6, 1.4)
    biases = jnp.clip(0.1 * jax.random.normal(bias_key, (SMALLP,), jnp.float32), -0.6, 0.6)
    return jnp.where(is_gain, gains, biases).astype(jnp.bfloat16)


def shard_levels(key, dims, shards, smallest, high):
    factor_of, own = 1.0, jax.random.fold_in(key, 6)
    for dim, parts in shards:
        heights = jnp.exp(jax.random.uniform(jax.random.fold_in(own, dim), (parts,), jnp.float32, smallest / len(shards), high / len(shards)))
        factor_of = factor_of * jnp.repeat(heights, dims[dim] // parts).reshape([-1 if axis == dim else 1 for axis in range(len(dims))])
    return factor_of


def noise(rng, dims, width, reach, cuts=(), kind=jnp.bfloat16):
    entries = jax.random.normal(rng, dims, jnp.float32) * width
    if len(cuts) > 0:
        entries = shard_levels(rng, dims, cuts, -0.22, 0.18) * entries
    return jnp.clip(entries, min=-reach, max=reach).astype(kind)


def setup_inputs(seed: int = 0) -> dict:
    seeds = jax.random.split(jax.random.key(seed), 9)
    tokens = noise(seeds[0], (SEQS, LEN, D), 1.0, 6.0, ((0, 8), (1, 4)))
    order = draw_order(jax.random.fold_in(seeds[8], 71), 0)
    cotangent = noise(seeds[2], (SEQS, LEN, D), 1.0, 6.0, ((0, 8), (1, 4)))
    qkv_weight = noise(seeds[3], (3 * D * D,), D ** -0.5, 0.1875, ((0, 32),))
    out_weight = noise(seeds[4], (D * D,), (D // 16) ** -0.5, 0.75, ((0, 32),))
    up_weight = noise(seeds[5], (D * FF,), D ** -0.5, 0.1875, ((0, 32),))
    down_weight = noise(seeds[6], (FF * D,), FF ** -0.5, 0.09375, ((0, 32),))
    small_params = draw_small_params(jax.random.fold_in(seeds[8], 71), 0)
    return {"tokens": tokens, "order": order, "cotangent": cotangent, "qkv_weight": qkv_weight, "out_weight": out_weight, "up_weight": up_weight, "down_weight": down_weight, "small_params": small_params}


@jax.custom_vjp
def low(v):
    return lax.optimization_barrier(v.astype(jnp.bfloat16)).astype(jnp.float32)

@jax.custom_vjp
def low_back(v):
    return v

def low_keep(v):
    return (low(v), None)

def low_pass(kept, grad):
    return (grad,)

def back_keep(v):
    return (v, None)

def back_low(kept, grad):
    return (low(grad),)
low.defvjp(low_keep, low_pass)
low_back.defvjp(back_keep, back_low)

def precise_dot(left, right):
    return jnp.dot(left, right, precision=lax.Precision.HIGHEST)

def layer_norm(values, scale_vec, shift_vec):
    row_mean = lax.optimization_barrier(jnp.mean(values, axis=-1, keepdims=True))
    centred = values - row_mean
    variance = lax.optimization_barrier(jnp.mean(centred * centred, axis=-1, keepdims=True))
    return centred * lax.rsqrt(variance + 1e-05) * scale_vec + shift_vec

def block_forward(inputs, w_qkv, w_out, w_up, w_down, small, positions):
    ln1_gain, ln1_bias = (small[0:D], small[D:2 * D])
    q_bias, v_bias, out_bias = (small[2 * D:3 * D], small[3 * D:4 * D], small[4 * D:5 * D])
    ln2_gain, ln2_bias = (small[5 * D:6 * D], small[6 * D:7 * D])
    up_bias = small[7 * D:7 * D + FF]
    down_bias = small[7 * D + FF:8 * D + FF]
    group = inputs.shape[0]
    input_rows = inputs.reshape(-1, D)
    a_one = low(layer_norm(input_rows, ln1_gain, ln1_bias))
    bias_qkv = jnp.concatenate([q_bias, jnp.zeros((D,), jnp.float32), v_bias])
    qkv_vals = low_back(low(precise_dot(a_one, w_qkv) + bias_qkv))
    queries = qkv_vals[:, :D].reshape(group, LEN, D // HD, HD)
    keys_all = qkv_vals[:, D:2 * D].reshape(group, LEN, D // HD, HD)
    values_all = qkv_vals[:, 2 * D:].reshape(group, LEN, D // HD, HD)
    scores = jnp.einsum('gqhd,gkhd->ghqk', queries, keys_all, precision=lax.Precision.HIGHEST) * 0.125
    causal_mask = positions[:, :, None] >= positions[:, None, :]
    scores = low_back(jnp.where(causal_mask[:, None], scores, -1e+30))
    attn_probs = low(jax.nn.softmax(scores, axis=-1))
    context = jnp.einsum('ghqk,gkhd->gqhd', attn_probs, values_all, precision=lax.Precision.HIGHEST)
    context = low_back(low(context.reshape(-1, D)))
    attn_out = low_back(precise_dot(context, w_out) + out_bias)
    residual = input_rows + attn_out
    a_two = low(layer_norm(residual, ln2_gain, ln2_bias))
    pre_act = low_back(precise_dot(a_two, w_up) + up_bias)
    act_low = low(jax.nn.gelu(pre_act, approximate=False))
    result = residual + precise_dot(act_low, w_down) + down_bias
    return result.reshape(inputs.shape)

def reference(tokens, order, cotangent, qkv_weight, out_weight, up_weight, down_weight, small_params):
    w_qkv = qkv_weight.astype(jnp.float32).reshape(D, 3 * D)
    w_out = out_weight.astype(jnp.float32).reshape(D, D)
    w_up = up_weight.astype(jnp.float32).reshape(D, FF)
    w_down = down_weight.astype(jnp.float32).reshape(FF, D)
    small = small_params.astype(jnp.float32)
    group = math.gcd(SEQS, 8)
    inputs = tokens.astype(jnp.float32).reshape(SEQS // group, group, LEN, D)
    grads_in = cotangent.astype(jnp.float32).reshape(SEQS // group, group, LEN, D)
    slot_pos = order.reshape(SEQS // group, group, LEN)
    params = (w_qkv, w_out, w_up, w_down, small)

    def scan_step(running, batch_item):
        block_in, positions, block_grad = batch_item

        def forward_only(block_x, p_qkv, p_out, p_up, p_down, p_small):
            return block_forward(block_x, p_qkv, p_out, p_up, p_down, p_small, positions)
        result, pull_back = jax.vjp(forward_only, block_in, *params)
        pulled = pull_back(block_grad)
        running = jax.tree.map(lambda a, b: a + b, running, tuple(pulled[1:]))
        return (running, (result.astype(jnp.bfloat16), pulled[0].astype(jnp.bfloat16)))
    start_sums = tuple((jnp.zeros_like(p) for p in params))
    sums, (outputs, input_grads) = lax.scan(scan_step, start_sums, (inputs, slot_pos, grads_in))
    mixed = outputs.reshape(SEQS, LEN, D)
    input_grad = input_grads.reshape(SEQS, LEN, D)
    return (mixed, input_grad, sums[0].reshape(-1), sums[1].reshape(-1), sums[2].reshape(-1), sums[3].reshape(-1), sums[4])
```

```python
from functools import partial

import jax
import jax.numpy as jnp
from jax import lax
from jax.sharding import PartitionSpec as P

D = 1088
FF = 4352
HD = 64
HEADS = D // HD
LEN = 512
F32 = jnp.float32
BF16 = jnp.bfloat16

CORE_SWAP = [(0, 1), (1, 0), (2, 3), (3, 2)]
CHIP_SWAP = [(0, 2), (2, 0), (1, 3), (3, 1)]
DIAG_SWAP = [(0, 3), (3, 0), (1, 2), (2, 1)]


def mm(left, right):
    return jnp.dot(left, right, preferred_element_type=F32)


def inner_rows(left, right):
    return lax.dot_general(left, right, (((0,), (0,)), ((), ())), preferred_element_type=F32)


def times_transposed(left, right):
    return lax.dot_general(left, right, (((1,), (1,)), ((), ())), preferred_element_type=F32)


def seq_gather(rows):
    other = lax.ppermute(rows, "seq", CHIP_SWAP)
    pair = jnp.stack([rows, other])
    across = lax.ppermute(pair, "seq", CORE_SWAP)
    return jnp.stack([pair[0], across[0], pair[1], across[1]])


def seq_reduce(blocks):
    low = blocks.astype(BF16)
    across = lax.ppermute(jnp.stack([low[1], low[3]]), "seq", CORE_SWAP).astype(F32)
    far = (blocks[2] + across[1]).astype(BF16)
    got = lax.ppermute(far, "seq", CHIP_SWAP).astype(F32)
    return blocks[0] + across[0] + got


def seq_exchange(blocks, me):
    pick = lambda r: lax.dynamic_index_in_dim(blocks, me ^ r, 0, False)
    rel = [
        pick(0),
        lax.ppermute(pick(1), "seq", CORE_SWAP),
        lax.ppermute(pick(2), "seq", CHIP_SWAP),
        lax.ppermute(pick(3), "seq", DIAG_SWAP),
    ]
    out = jnp.zeros_like(blocks)
    for r in range(4):
        out = lax.dynamic_update_index_in_dim(out, rel[r], me ^ r, 0)
    return out


class Ring:
    def __init__(self, size):
        self.size = size
        half = size // 2
        walk = [2 * i for i in range(half)] + [2 * i + 1 for i in range(half)][::-1]
        self.ahead = [(walk[i], walk[(i + 1) % size]) for i in range(size)]
        self.back = [(b, a) for a, b in self.ahead]
        index = lax.axis_index("dp")
        self.place = jnp.where(index % 2 == 0, index // 2, size - 1 - index // 2)

    def member(self, step):
        place = (self.place + step + self.size) % self.size
        return jnp.where(place < self.size // 2, 2 * place, 2 * (self.size - 1 - place) + 1)

    def gather(self, chunk):
        half = self.size // 2
        cut = (chunk.shape[0] // 2 + 7) // 8 * 8
        out = jnp.zeros((self.size,) + chunk.shape, chunk.dtype)
        put = lambda out, part, step, row: lax.dynamic_update_slice(
            out, part[None], (self.member(step), row, 0)
        )
        out = put(out, chunk, 0, 0)
        ahead = back = chunk
        for step in range(1, half):
            ahead = lax.ppermute(ahead, "dp", self.ahead)
            back = lax.ppermute(back, "dp", self.back)
            out = put(out, ahead, -step, 0)
            out = put(out, back, step, 0)
        out = put(out, lax.ppermute(ahead[:cut], "dp", self.ahead), half, 0)
        out = put(out, lax.ppermute(back[cut:], "dp", self.back), half, cut)
        return out

    def reduce(self, parts):
        half = self.size // 2
        cut = (parts.shape[1] // 2 + 7) // 8 * 8
        own = lambda step: lax.dynamic_index_in_dim(parts, self.member(step), 0, False).astype(F32)
        far = lax.dynamic_index_in_dim(parts, self.member(half), 0, False)
        ahead = lax.ppermute(far[:cut], "dp", self.ahead).astype(F32)
        back = lax.ppermute(far[cut:], "dp", self.back).astype(F32)
        mine = own(half - 1)
        ahead = jnp.concatenate([mine[:cut] + ahead, mine[cut:]])
        mine = own(1 - half)
        back = jnp.concatenate([mine[:cut], mine[cut:] + back])
        for step in range(half - 1, 0, -1):
            if step < half - 1:
                ahead = own(step) + ahead
                back = own(-step) + back
            ahead = lax.ppermute(ahead.astype(BF16), "dp", self.ahead).astype(F32)
            back = lax.ppermute(back.astype(BF16), "dp", self.back).astype(F32)
        return own(0) + ahead + back


class Whole:
    def gather(self, chunk):
        return lax.all_gather(chunk, "dp", axis=0)

    def reduce(self, parts):
        return lax.psum_scatter(parts, "dp", scatter_dimension=0, tiled=True)[0].astype(F32)


def split_rows(flat, width, cols_of, me):
    if flat.shape[0] % width == 0:
        rows = flat.reshape(-1, width)
        got = seq_exchange(cols_of(rows), me)
        return got.reshape(-1, got.shape[-1])
    rows = lax.all_gather(flat, "seq", axis=0, tiled=True).reshape(-1, width)
    return lax.dynamic_index_in_dim(cols_of(rows), me, 0, False)


def join_rows(rows, width, join_cols, me):
    share = rows.shape[0] * width // 4
    low = rows.astype(BF16)
    if share % width == 0:
        got = seq_exchange(low.reshape(4, rows.shape[0] // 4, -1), me)
        return join_cols(got).astype(F32).reshape(-1)
    got = join_cols(lax.all_gather(low, "seq", axis=0)).reshape(-1)
    return lax.dynamic_slice_in_dim(got, me * share, share, 0).astype(F32)


STARTS = (0, 5, 9, 12)
WINDOW = 5


def head_cols(rows):
    three = rows.reshape(-1, 3, D)
    return jnp.stack(
        [three[:, :, s * HD : (s + WINDOW) * HD].reshape(-1, 3 * WINDOW * HD) for s in STARTS]
    )


def join_windows(four, axis):
    size = WINDOW * HD
    cut = lambda part, lo, hi: lax.slice_in_dim(part, lo, hi, axis=axis)
    return jnp.concatenate(
        [four[0], cut(four[1], 0, size - HD), cut(four[2], 0, size - HD), cut(four[3], HD, size)],
        axis=axis,
    )


def join_head_cols(got):
    return join_windows(got.reshape(4, -1, 3, WINDOW * HD), 2).reshape(-1, 3 * D)


def norm_stats(values):
    mean = jnp.mean(values, axis=-1, keepdims=True)
    centred = values - mean
    scale = lax.rsqrt(jnp.mean(centred * centred, axis=-1, keepdims=True) + 1e-05)
    return centred * scale, scale


def norm_back(unit, scale, gain, grad):
    lifted = grad * gain
    return scale * (
        lifted
        - jnp.mean(lifted, axis=-1, keepdims=True)
        - unit * jnp.mean(lifted * unit, axis=-1, keepdims=True)
    )


def body(tokens, order, cotangent, qkv_weight, out_weight, up_weight, down_weight, small_params):
    slots = tokens.shape[1]
    dp_count = lax.axis_size("dp")
    me = lax.axis_index("seq")
    units = FF // (dp_count * 4)
    block_rows = D // dp_count
    own_cols = D // 4
    ring = Ring(dp_count) if dp_count == 8 else Whole()
    start = jnp.where(me == 0, 0, jnp.where(me == 3, 12, 4 * me + 1)) * HD

    small_len = small_params.shape[0]
    w = 3 * WINDOW * HD
    qkv_rows = split_rows(qkv_weight, 3 * D, head_cols, me)
    small_rows = seq_exchange(
        jnp.broadcast_to(jnp.pad(small_params, (0, w - small_len))[None], (4, w)), me
    )
    tail = 8 + (-block_rows) % 8
    qkv_chunk = jnp.concatenate([qkv_rows, small_rows, jnp.zeros((tail - 4, w), BF16)])
    qkv_all = ring.gather(qkv_chunk)
    w_qkv = qkv_all[:, :block_rows].reshape(D, w)
    small_full = qkv_all[:, block_rows : block_rows + 4, :small_len].reshape(-1).astype(F32)

    out_rows = split_rows(
        out_weight, D, lambda r: jnp.swapaxes(r.reshape(-1, 4, own_cols), 0, 1), me
    )
    out_cols = ring.gather(out_rows).reshape(D, own_cols)
    out_got = seq_exchange(jnp.stack([out_cols[s * HD : (s + WINDOW) * HD] for s in STARTS]), me)
    w_out = jnp.swapaxes(out_got, 0, 1).reshape(WINDOW * HD, D)
    row_head = jnp.arange(WINDOW * HD) // HD
    repeated = jnp.where(me == 0, WINDOW, jnp.where(me == 3, 0, WINDOW - 1))
    w_out = jnp.where((row_head == repeated)[:, None], 0, w_out).astype(BF16)

    up_rows = split_rows(
        up_weight,
        FF,
        lambda r: jnp.transpose(r.reshape(-1, dp_count, 4, units), (2, 0, 1, 3)).reshape(
            4, r.shape[0], D
        ),
        me,
    )
    w_up = ring.gather(up_rows).reshape(D, D)
    w_down = ring.gather(down_weight.reshape(-1, D)).reshape(D, D)

    at = lambda i: small_full[i * D : (i + 1) * D]
    ln1_gain, ln1_bias, q_bias, v_bias, out_bias, ln2_gain, ln2_bias = [at(i) for i in range(7)]
    up_bias = small_full[7 * D : 7 * D + FF]
    down_bias = small_full[7 * D + FF : 8 * D + FF]

    own_tokens = tokens.reshape(-1, D)
    own_grad = cotangent.reshape(-1, D)
    all_tokens = seq_gather(own_tokens).reshape(-1, D).astype(F32)
    grad_all = seq_gather(own_grad).reshape(-1, D)
    order_four = order.reshape(4, slots)
    positions = jnp.concatenate(
        [lax.dynamic_index_in_dim(order_four, me ^ r, 0, False) for r in range(4)]
    )
    causal = positions[:, None] >= positions[None, :]

    unit_one, _ = norm_stats(all_tokens)
    a_one = (unit_one * ln1_gain + ln1_bias).astype(BF16)
    window = lambda v: lax.dynamic_slice_in_dim(v, start, WINDOW * HD, 0)
    bias_qkv = jnp.concatenate([window(q_bias), jnp.zeros((WINDOW * HD,), F32), window(v_bias)])
    qkv_vals = (mm(a_one, w_qkv) + bias_qkv).astype(BF16)
    heads = qkv_vals.reshape(-1, 3, WINDOW, HD)
    queries, keys, values = heads[:, 0], heads[:, 1], heads[:, 2]
    scores = jnp.einsum("qhd,khd->hqk", queries, keys, preferred_element_type=F32) * 0.125
    scores = jnp.where(causal[None], scores, -1e30)
    peak = jnp.max(scores, axis=-1, keepdims=True)
    exps = jnp.exp(scores - peak)
    probs = exps / jnp.sum(exps, axis=-1, keepdims=True)
    probs_low = probs.astype(BF16)
    context = jnp.einsum("hqk,khd->qhd", probs_low, values, preferred_element_type=F32)
    context = context.reshape(-1, WINDOW * HD).astype(BF16)
    attn_out = seq_reduce(mm(context, w_out).reshape(4, slots, D))
    residual = own_tokens.astype(F32) + attn_out + out_bias
    unit_two, scale_two = norm_stats(residual)
    a_two = (unit_two * ln2_gain + ln2_bias).astype(BF16)
    a_two_all = seq_gather(a_two).reshape(-1, D)
    up_bias_own = lax.dynamic_index_in_dim(
        up_bias.reshape(dp_count, 4, units), me, 1, False
    ).reshape(-1)
    pre_act = mm(a_two_all, w_up) + up_bias_own
    act_low = jax.nn.gelu(pre_act, approximate=False).astype(BF16)
    mlp_out = seq_reduce(mm(act_low, w_down).reshape(4, slots, D))
    mixed = (residual + mlp_out + down_bias).astype(BF16).reshape(tokens.shape)

    own_grad32 = own_grad.astype(F32)
    down_bias_grad = jnp.sum(own_grad32, axis=0)
    down_grad = inner_rows(act_low, grad_all)
    down_sum = ring.reduce(down_grad.astype(BF16).reshape(dp_count, units, D))
    act_grad = times_transposed(grad_all, w_down)
    _, gelu_pull = jax.vjp(partial(jax.nn.gelu, approximate=False), pre_act)
    pre_low = gelu_pull(act_grad)[0].astype(BF16)
    up_grad = inner_rows(a_two_all, pre_low)
    up_sum = ring.reduce(up_grad.astype(BF16).reshape(dp_count, block_rows, D))
    bias_cols = jnp.sum(pre_low.astype(F32), axis=0)
    norm_two_in = seq_reduce(times_transposed(pre_low, w_up).reshape(4, slots, D))
    ln2_gain_grad = jnp.sum(norm_two_in * unit_two, axis=0)
    ln2_bias_grad = jnp.sum(norm_two_in, axis=0)
    residual_grad = own_grad32 + norm_back(unit_two, scale_two, ln2_gain, norm_two_in)

    resid_low = residual_grad.astype(BF16)
    out_bias_grad = jnp.sum(resid_low.astype(F32), axis=0)
    resid_all = seq_gather(resid_low).reshape(-1, D)
    out_grad = inner_rows(context, resid_all).astype(BF16)
    out_back = seq_exchange(jnp.swapaxes(out_grad.reshape(WINDOW * HD, 4, own_cols), 0, 1), me)
    out_back = join_windows(out_back, 0)
    out_sum = ring.reduce(out_back.reshape(dp_count, block_rows, own_cols))
    context_grad = times_transposed(resid_all, w_out).astype(BF16).reshape(-1, WINDOW, HD)
    prob_grad = jnp.einsum("qhd,khd->hqk", context_grad, values, preferred_element_type=F32)
    values_grad = jnp.einsum("hqk,qhd->khd", probs_low, context_grad, preferred_element_type=F32)
    score_grad = probs * (prob_grad - jnp.sum(probs * prob_grad, axis=-1, keepdims=True))
    score_low = score_grad.astype(BF16)
    query_grad = jnp.einsum("hqk,khd->qhd", score_low, keys, preferred_element_type=F32) * 0.125
    keys_grad = jnp.einsum("hqk,qhd->khd", score_low, queries, preferred_element_type=F32) * 0.125
    qkv_low = jnp.concatenate(
        [g.reshape(-1, WINDOW * HD) for g in (query_grad, keys_grad, values_grad)], axis=1
    ).astype(BF16)
    bias_sums = jnp.sum(qkv_low.astype(F32), axis=0)
    placed = lambda v: lax.dynamic_update_slice(jnp.zeros((D,), F32), v, (start,))
    q_bias_grad = placed(bias_sums[: WINDOW * HD])
    v_bias_grad = placed(bias_sums[2 * WINDOW * HD :])
    norm_one_part = times_transposed(qkv_low, w_qkv)
    ln1_gain_grad = jnp.sum(norm_one_part * unit_one, axis=0)
    ln1_bias_grad = jnp.sum(norm_one_part, axis=0)
    qkv_grad = inner_rows(a_one, qkv_low).astype(BF16)

    up_bias_grad = lax.dynamic_update_slice(
        jnp.zeros((dp_count, 4, units), F32), bias_cols.reshape(dp_count, 1, units), (0, me, 0)
    ).reshape(-1)
    small_grad = jnp.concatenate(
        [
            ln1_gain_grad,
            ln1_bias_grad,
            q_bias_grad,
            v_bias_grad,
            out_bias_grad,
            ln2_gain_grad,
            ln2_bias_grad,
            up_bias_grad,
            down_bias_grad,
            jnp.zeros((small_full.shape[0] - 8 * D - FF,), F32),
        ]
    ).astype(BF16)
    small_grad = jnp.pad(
        small_grad.reshape(dp_count, 4, small_len), ((0, 0), (0, tail - 4), (0, w - small_len))
    )
    qkv_parts = jnp.concatenate([qkv_grad.reshape(dp_count, block_rows, w), small_grad], axis=1)
    qkv_sum = ring.reduce(qkv_parts)
    small_got = seq_exchange(qkv_sum[block_rows : block_rows + 4].astype(BF16), me)
    small_part = jnp.sum(small_got.astype(F32), axis=0)[:small_len]
    qkv_part = join_rows(qkv_sum[:block_rows], 3 * D, join_head_cols, me)

    norm_one_in = seq_reduce(norm_one_part.reshape(4, slots, D))
    own_unit, own_scale = norm_stats(own_tokens.astype(F32))
    input_grad = residual_grad + norm_back(own_unit, own_scale, ln1_gain, norm_one_in)
    input_grad = input_grad.astype(BF16).reshape(tokens.shape)

    out_part = join_rows(out_sum, D, lambda g: jnp.swapaxes(g, 0, 1).reshape(-1, D), me)
    up_part = join_rows(
        up_sum,
        FF,
        lambda g: jnp.transpose(g.reshape(4, -1, dp_count, units), (1, 2, 0, 3)).reshape(-1, FF),
        me,
    )
    down_part = down_sum.reshape(-1)
    return (mixed, input_grad, qkv_part, out_part, up_part, down_part, small_part)


def solution(mesh):
    rows, flat = P("dp", "seq", None), P(("dp", "seq"))
    return jax.shard_map(
        body,
        mesh=mesh,
        in_specs=(rows, P("dp", None), rows, flat, flat, flat, flat, flat),
        out_specs=(rows, rows, flat, flat, flat, flat, flat),
        check_vma=False,
    )
```

```python
import jax
import jax.numpy as jnp
from jax import lax
from jax.experimental import pallas as pl
from jax.experimental.pallas import tpu as pltpu
from jax.sharding import PartitionSpec as P

D = 1088
FF = 4352
HD = 64
HEADS = D // HD
LEN = 512
F32 = jnp.float32
BF16 = jnp.bfloat16

CORE_SWAP = [(0, 1), (1, 0), (2, 3), (3, 2)]
CHIP_SWAP = [(0, 2), (2, 0), (1, 3), (3, 1)]
DIAG_SWAP = [(0, 3), (3, 0), (1, 2), (2, 1)]


def mm(left, right):
    return jnp.dot(left, right, preferred_element_type=F32)


def inner_rows(left, right):
    return lax.dot_general(left, right, (((0,), (0,)), ((), ())), preferred_element_type=F32)


def times_transposed(left, right):
    return lax.dot_general(left, right, (((1,), (1,)), ((), ())), preferred_element_type=F32)


def xor_order(four, me):
    core, chip = me % 2 == 1, me // 2 == 1
    a = [four[0], four[1], four[2], four[3]]
    a = [jnp.where(core, a[i ^ 1], a[i]) for i in range(4)]
    return [jnp.where(chip, a[i ^ 2], a[i]) for i in range(4)]


def seq_gather(rows):
    other = lax.ppermute(rows, "seq", CHIP_SWAP)
    return core_gather(jnp.stack([rows, other]))


def core_gather(pair):
    across = lax.ppermute(pair, "seq", CORE_SWAP)
    return jnp.stack([pair[0], across[0], pair[1], across[1]])


def core_reduce(blocks):
    low = blocks.astype(BF16)
    across = lax.ppermute(jnp.stack([low[1], low[3]]), "seq", CORE_SWAP).astype(F32)
    return blocks[0] + across[0], blocks[2] + across[1]


def seq_reduce(blocks):
    near, far = core_reduce(blocks)
    return near + lax.ppermute(far.astype(BF16), "seq", CHIP_SWAP).astype(F32)


def pair_reduce(blocks):
    near, far = core_reduce(blocks)
    pair = jnp.stack([near, far]).astype(BF16)
    got = lax.ppermute(pair, "seq", CHIP_SWAP).astype(F32)
    return pair.astype(F32) + jnp.stack([got[1], got[0]])


def seq_exchange(blocks, me):
    rel = xor_order(blocks, me)
    rel = [
        rel[0],
        lax.ppermute(rel[1], "seq", CORE_SWAP),
        lax.ppermute(rel[2], "seq", CHIP_SWAP),
        lax.ppermute(rel[3], "seq", DIAG_SWAP),
    ]
    return xor_order(rel, me)


def tied(*values):
    return lax.optimization_barrier(values)


class Ring:
    def __init__(self, size):
        self.size = size
        half = size // 2
        walk = [2 * i for i in range(half)] + [2 * i + 1 for i in range(half)][::-1]
        self.ahead = [(walk[i], walk[(i + 1) % size]) for i in range(size)]
        self.back = [(b, a) for a, b in self.ahead]
        index = lax.axis_index("dp")
        self.place = jnp.where(index % 2 == 0, index // 2, size - 1 - index // 2)

    def member(self, step):
        place = (self.place + step + self.size) % self.size
        return jnp.where(place < self.size // 2, 2 * place, 2 * (self.size - 1 - place) + 1)

    def gather(self, chunk, windows):
        return Gather(self, chunk, windows)

    def gather_two(self, first, second):
        return GatherTwo(self, first, second)

    def reduce(self, parts):
        return Reduce(self, parts)

    def reduce_two(self, first, second):
        return ReduceTwo(self, first, second)


class Steps:
    def step(self, count=1):
        for _ in range(count):
            self.done += 1
            self.move(self.done)

    def tie(self, value):
        value, self.flight = tied(value, self.flight)
        return value

    def finish(self):
        self.step(self.ring.size // 2 - self.done)
        return self.result()


class Gather(Steps):
    def __init__(self, ring, chunk, windows):
        self.ring, self.windows, self.done = ring, windows, 0
        self.outs = [jnp.zeros((ring.size, w[1], w[3]), chunk.dtype) for w in windows]
        self.put(chunk, 0, 0)
        self.flight = (chunk, chunk)

    def put(self, part, step, first):
        for i, (row, rows, col, cols) in enumerate(self.windows):
            lo, hi = max(row, first), min(row + rows, first + part.shape[0])
            if lo < hi:
                self.outs[i] = lax.dynamic_update_slice(
                    self.outs[i],
                    part[None, lo - first : hi - first, col : col + cols],
                    (self.ring.member(step), lo - row, 0),
                )

    def move(self, step):
        ring, (ahead, back) = self.ring, self.flight
        cut = 0
        if step == ring.size // 2:
            cut = (ahead.shape[0] // 2 + 7) // 8 * 8
            ahead, back = ahead[:cut], back[cut:]
        ahead = lax.ppermute(ahead, "dp", ring.ahead)
        back = lax.ppermute(back, "dp", ring.back)
        self.put(ahead, -step, 0)
        self.put(back, step, cut)
        self.flight = (ahead, back)

    def result(self):
        return self.outs


def place_two(ids, chunks, halves, size):
    shape = halves[0].shape
    last = len(chunks)

    def kernel(ids_ref, *refs):
        sources, outs = refs[: last + 2], refs[last + 2 :]
        for k in range(last):
            for half in range(2):
                outs[half][ids_ref[k]] = sources[k][half]
        for half in range(2):
            outs[half][ids_ref[last]] = sources[last + half][...]

    return pl.pallas_call(
        kernel,
        out_shape=[jax.ShapeDtypeStruct((size,) + shape, halves[0].dtype)] * 2,
        in_specs=[pl.BlockSpec(memory_space=pltpu.SMEM)]
        + [pl.BlockSpec(memory_space=pltpu.VMEM)] * (last + 2),
        out_specs=[pl.BlockSpec(memory_space=pltpu.VMEM)] * 2,
        compiler_params=pltpu.CompilerParams(vmem_limit_bytes=32 * 2**20),
        cost_estimate=pl.CostEstimate(
            flops=0, bytes_accessed=4 * size * shape[0] * shape[1] * 2, transcendentals=0
        ),
    )(ids, *chunks, *halves)


class GatherTwo(Steps):
    def __init__(self, ring, first, second):
        self.ring, self.done = ring, 0
        chunk = jnp.stack([first, second])
        self.flight = (chunk, chunk)
        self.chunks, self.order = [chunk], [0]

    def move(self, step):
        ring, (ahead, back) = self.ring, self.flight
        last = step == ring.size // 2
        if last:
            ahead, back = ahead[0], back[1]
        ahead = lax.ppermute(ahead, "dp", ring.ahead)
        back = lax.ppermute(back, "dp", ring.back)
        self.flight = (ahead, back)
        if not last:
            self.chunks += [ahead, back]
            self.order += [-step, step]

    def result(self):
        ids = jnp.stack([self.ring.member(k) for k in self.order + [self.ring.size // 2]])
        return place_two(ids.astype(jnp.int32), self.chunks, self.flight, self.ring.size)


class ReduceTwo(Steps):
    def __init__(self, ring, first, second):
        self.ring, self.parts, self.done = ring, (first, second), 0
        far = [lax.dynamic_index_in_dim(p, ring.member(ring.size // 2), 0, False) for p in self.parts]
        self.flight = tuple(far)

    def own(self, step):
        return [
            lax.dynamic_index_in_dim(p, self.ring.member(step), 0, False).astype(F32)
            for p in self.parts
        ]

    def move(self, step):
        ring, (ahead, back) = self.ring, self.flight
        left = ring.size // 2 - step + 1
        if step == 2:
            mine, other = self.own(left), self.own(-left)
            ahead = jnp.stack([mine[0] + ahead.astype(F32), mine[1]])
            back = jnp.stack([other[0], other[1] + back.astype(F32)])
        elif step > 2:
            ahead = jnp.stack(self.own(left)) + ahead.astype(F32)
            back = jnp.stack(self.own(-left)) + back.astype(F32)
        ahead = lax.ppermute(ahead.astype(BF16), "dp", ring.ahead)
        back = lax.ppermute(back.astype(BF16), "dp", ring.back)
        self.flight = (ahead, back)

    def result(self):
        ahead, back = self.flight
        mine = self.own(0)
        return [mine[i] + ahead[i].astype(F32) + back[i].astype(F32) for i in range(2)]


class Reduce(Steps):
    def __init__(self, ring, parts):
        self.ring, self.parts, self.done = ring, parts, 0
        self.cut = (parts.shape[1] // 2 + 7) // 8 * 8
        far = lax.dynamic_index_in_dim(parts, ring.member(ring.size // 2), 0, False)
        self.flight = (far[: self.cut], far[self.cut :])

    def own(self, step):
        return lax.dynamic_index_in_dim(self.parts, self.ring.member(step), 0, False).astype(F32)

    def move(self, step):
        ring, cut, (ahead, back) = self.ring, self.cut, self.flight
        left = ring.size // 2 - step + 1
        if step == 2:
            mine, other = self.own(left), self.own(-left)
            ahead = jnp.concatenate([mine[:cut] + ahead.astype(F32), mine[cut:]])
            back = jnp.concatenate([other[:cut], other[cut:] + back.astype(F32)])
        elif step > 2:
            ahead = self.own(left) + ahead.astype(F32)
            back = self.own(-left) + back.astype(F32)
        ahead = lax.ppermute(ahead.astype(BF16), "dp", ring.ahead)
        back = lax.ppermute(back.astype(BF16), "dp", ring.back)
        self.flight = (ahead, back)

    def result(self):
        ahead, back = self.flight
        return self.own(0) + ahead.astype(F32) + back.astype(F32)


class Whole:
    def gather(self, chunk, windows):
        got = lax.all_gather(chunk, "dp", axis=0)
        return Whole.Ready([got[:, r : r + n, c : c + m] for r, n, c, m in windows], chunk)

    def gather_two(self, first, second):
        got = lax.all_gather(jnp.stack([first, second]), "dp", axis=0)
        return Whole.Ready([got[:, 0], got[:, 1]], first)

    def reduce_two(self, first, second):
        got = lax.psum_scatter(
            jnp.stack([first, second], axis=1), "dp", scatter_dimension=0, tiled=True
        )[0].astype(F32)
        return Whole.Ready([got[0], got[1]], got)

    def reduce(self, parts):
        got = lax.psum_scatter(parts, "dp", scatter_dimension=0, tiled=True)[0]
        return Whole.Ready(got.astype(F32), got)

    class Ready(Steps):
        def __init__(self, value, flight):
            self.value, self.flight = value, flight

        def step(self, count=1):
            pass

        def finish(self):
            return self.value


STARTS = (0, 5, 9, 12)
WINDOW = 5


SPAN = WINDOW * HD


def join_windows(four, axis):
    cut = lambda part, lo, hi: lax.slice_in_dim(part, lo, hi, axis=axis)
    return jnp.concatenate(
        [
            four[0],
            cut(four[1], 0, SPAN - HD),
            cut(four[2], 0, SPAN - HD),
            cut(four[3], HD, SPAN),
        ],
        axis=axis,
    )


def head_cols(rows):
    piece = lambda s, b: rows[:, b * D + s * HD : b * D + s * HD + SPAN]
    return [jnp.concatenate([piece(s, b) for b in range(3)], axis=1) for s in STARTS]


def join_head_cols(four):
    block = lambda b: join_windows([f[:, b * SPAN : (b + 1) * SPAN] for f in four], 1)
    return jnp.concatenate([block(b) for b in range(3)], axis=1)


def own_cols(rows):
    return [rows[:, s * (D // 4) : (s + 1) * (D // 4)] for s in range(4)]


def unit_cols(rows, dp_count):
    four = rows.reshape(rows.shape[0], dp_count, 4, -1)
    return [four[:, :, s].reshape(rows.shape[0], D) for s in range(4)]


def join_unit_cols(four, dp_count):
    parts = [f.reshape(f.shape[0], dp_count, 1, -1) for f in four]
    return jnp.concatenate(parts, axis=2).reshape(four[0].shape[0], FF)


def split_rows(flats, widths, cols_of, me):
    if all(flat.shape[0] % width == 0 for flat, width in zip(flats, widths)):
        rows = [flat.reshape(-1, width) for flat, width in zip(flats, widths)]
        return jnp.concatenate(seq_exchange(cols_of(rows), me))
    rows = [
        lax.all_gather(flat, "seq", axis=0, tiled=True).reshape(-1, width)
        for flat, width in zip(flats, widths)
    ]
    return xor_order(cols_of(rows), me)[0]


def join_rows(rows, shares, widths, join_cols, me):
    low = rows.astype(BF16)
    count = rows.shape[0] // 4
    if all(share % width == 0 for share, width in zip(shares, widths)):
        got = seq_exchange([low[m * count : (m + 1) * count] for m in range(4)], me)
        return [part.astype(F32).reshape(-1) for part in join_cols(got)]
    got = join_cols(list(lax.all_gather(low, "seq", axis=0)))
    return [
        lax.dynamic_slice_in_dim(part.reshape(-1), me * share, share, 0).astype(F32)
        for part, share in zip(got, shares)
    ]


def norm_stats(values):
    mean = jnp.mean(values, axis=-1, keepdims=True)
    centred = values - mean
    scale = lax.rsqrt(jnp.mean(centred * centred, axis=-1, keepdims=True) + 1e-05)
    return centred * scale, scale


def norm_back(unit, scale, gain, grad):
    lifted = grad * gain
    return scale * (
        lifted
        - jnp.mean(lifted, axis=-1, keepdims=True)
        - unit * jnp.mean(lifted * unit, axis=-1, keepdims=True)
    )


def body(tokens, order, cotangent, qkv_weight, out_weight, up_weight, down_weight, small_params):
    slots = tokens.shape[1]
    dp_count = lax.axis_size("dp")
    me = lax.axis_index("seq")
    units = FF // (dp_count * 4)
    block_rows = D // dp_count
    ring = Ring(dp_count) if dp_count == 8 else Whole()
    start = jnp.where(me == 0, 0, jnp.where(me == 3, 12, 4 * me + 1)) * HD

    small_len = small_params.shape[0]
    tail = 8 + (-block_rows) % 8
    wide = 3 * SPAN + D // 4

    attn_rows = split_rows(
        [qkv_weight, out_weight],
        [3 * D, D],
        lambda r: [
            jnp.concatenate([q, o], axis=1) for q, o in zip(head_cols(r[0]), own_cols(r[1]))
        ],
        me,
    )
    small_row = jnp.pad(small_params.reshape(1, -1), ((0, 0), (0, wide - small_len)))
    small_rows = xor_order(list(seq_gather(small_row)), me)
    attn_chunk = jnp.concatenate([attn_rows] + small_rows + [jnp.zeros((tail - 4, wide), BF16)])
    attn_chunk, up_flat = tied(attn_chunk, up_weight)
    attn_ring = ring.gather(
        attn_chunk,
        [
            (0, block_rows, 0, 3 * SPAN),
            (0, block_rows, 3 * SPAN, D // 4),
            (block_rows, tail, 0, wide),
        ],
    )
    attn_ring.step()
    up_rows = split_rows([up_flat], [FF], lambda r: unit_cols(r[0], dp_count), me)
    positions = jnp.concatenate(xor_order(order.reshape(4, slots), me))
    causal = attn_ring.tie(positions[:, None] >= positions[None, :])
    attn_ring.step()
    tokens_four = seq_gather(tokens.reshape(-1, D)).astype(F32)
    unit_one, scale_one = norm_stats(tokens_four.reshape(-1, D))
    unit_one, scale_one, up_rows = attn_ring.tie((unit_one, scale_one, up_rows))
    own_grad = attn_ring.tie(cotangent.reshape(-1, D))
    attn_ring.step()
    mlp_rows = attn_ring.tie((up_rows, down_weight.reshape(-1, D)))
    mlp_ring = ring.gather_two(*mlp_rows)
    grad_all = seq_gather(own_grad).reshape(-1, D)
    w_qkv, out_cols, small_all = attn_ring.finish()
    mlp_ring.step()
    w_qkv = w_qkv.reshape(D, 3 * SPAN)
    out_cols = out_cols.reshape(D, D // 4)
    small_full = small_all[:, :4, :small_len].reshape(-1).astype(F32)
    out_got = seq_exchange([out_cols[s * HD : s * HD + SPAN] for s in STARTS], me)
    w_out = jnp.concatenate(out_got, axis=1)
    row_head = jnp.arange(SPAN) // HD
    repeated = jnp.where(me == 0, WINDOW, jnp.where(me == 3, 0, WINDOW - 1))
    w_out = jnp.where((row_head == repeated)[:, None], 0, w_out).astype(BF16)

    at = lambda i: small_full[i * D : (i + 1) * D]
    ln1_gain, ln1_bias, q_bias, v_bias, out_bias, ln2_gain, ln2_bias = [at(i) for i in range(7)]
    up_bias = small_full[7 * D : 7 * D + FF]
    down_bias = small_full[7 * D + FF : 8 * D + FF]

    a_one = (unit_one * ln1_gain + ln1_bias).astype(BF16)
    window = lambda v: lax.dynamic_slice_in_dim(v, start, SPAN, 0)
    bias_qkv = jnp.concatenate([window(q_bias), jnp.zeros((SPAN,), F32), window(v_bias)])
    qkv_vals = (mm(a_one, w_qkv) + bias_qkv).astype(BF16)
    qkv_vals = mlp_ring.tie(qkv_vals)
    mlp_ring.step()
    heads = qkv_vals.reshape(-1, 3, WINDOW, HD)
    queries, keys, values = heads[:, 0], heads[:, 1], heads[:, 2]
    scores = jnp.einsum("qhd,khd->hqk", queries, keys, preferred_element_type=F32) * 0.125
    scores = jnp.where(causal[None], scores, -1e30)
    peak = jnp.max(scores, axis=-1, keepdims=True)
    exps = jnp.exp(scores - peak)
    probs = exps / jnp.sum(exps, axis=-1, keepdims=True)
    probs_low = mlp_ring.tie(probs.astype(BF16))
    mlp_ring.step()
    context = jnp.einsum("hqk,khd->qhd", probs_low, values, preferred_element_type=F32)
    context = context.reshape(-1, SPAN).astype(BF16)
    attn_part, grad_all = mlp_ring.tie((mm(context, w_out), grad_all))
    w_up, w_down = (w.reshape(D, D) for w in mlp_ring.finish())
    attn_out = pair_reduce(attn_part.reshape(4, slots, D))
    tokens_pair = jnp.stack([tokens_four[0], tokens_four[2]])
    residual = tokens_pair + attn_out + out_bias
    unit_two, scale_two = norm_stats(residual)
    a_two = (unit_two * ln2_gain + ln2_bias).astype(BF16)
    a_two_all = core_gather(a_two).reshape(-1, D)
    up_bias_own = lax.dynamic_index_in_dim(
        up_bias.reshape(dp_count, 4, units), me, 1, False
    ).reshape(-1)
    pre_act = mm(a_two_all, w_up) + up_bias_own
    below = 0.5 * (1.0 + lax.erf(pre_act * 0.7071067811865476))
    act_low = (pre_act * below).astype(BF16)
    slope = below + pre_act * jnp.exp(-0.5 * pre_act * pre_act) * 0.3989422804014327
    down_grad = inner_rows(act_low, grad_all)
    down_grad = down_grad.astype(BF16)

    own_grad32 = own_grad.astype(F32)
    down_bias_grad = jnp.sum(own_grad32, axis=0)
    pre_low = (times_transposed(grad_all, w_down) * slope).astype(BF16)
    norm_two_part = times_transposed(pre_low, w_up)
    up_grad = inner_rows(a_two_all, pre_low).astype(BF16)
    norm_two_part, up_grad, down_grad = tied(norm_two_part, up_grad, down_grad)
    mlp_back = ring.reduce_two(
        down_grad.reshape(dp_count, units, D), up_grad.reshape(dp_count, block_rows, D)
    )
    mlp_back.step()
    norm_two_in = mlp_back.tie(pair_reduce(norm_two_part.reshape(4, slots, D)))
    mlp_back.step()
    bias_cols = jnp.sum(pre_low.astype(F32), axis=0)
    ln2_gain_grad = jnp.sum(norm_two_in[0] * unit_two[0], axis=0)
    ln2_bias_grad = jnp.sum(norm_two_in[0], axis=0)
    grad_pair = jnp.stack([grad_all[:slots], grad_all[2 * slots : 3 * slots]]).astype(F32)
    residual_grad = grad_pair + norm_back(unit_two, scale_two, ln2_gain, norm_two_in)

    resid_low = residual_grad.astype(BF16)
    out_bias_grad = jnp.sum(resid_low[0].astype(F32), axis=0)
    resid_all = core_gather(resid_low).reshape(-1, D)
    context_grad = mlp_back.tie(times_transposed(resid_all, w_out).astype(BF16))
    mlp_back.step()
    context_grad = context_grad.reshape(-1, WINDOW, HD)
    prob_grad = jnp.einsum("qhd,khd->hqk", context_grad, values, preferred_element_type=F32)
    values_grad = jnp.einsum("hqk,qhd->khd", probs_low, context_grad, preferred_element_type=F32)
    score_grad = probs * (prob_grad - jnp.sum(probs * prob_grad, axis=-1, keepdims=True))
    score_low = mlp_back.tie(score_grad.astype(BF16))
    query_grad = jnp.einsum("hqk,khd->qhd", score_low, keys, preferred_element_type=F32) * 0.125
    keys_grad = jnp.einsum("hqk,qhd->khd", score_low, queries, preferred_element_type=F32) * 0.125
    qkv_low = jnp.concatenate(
        [g.reshape(-1, SPAN) for g in (query_grad, keys_grad, values_grad)], axis=1
    ).astype(BF16)
    down_sum, up_sum = mlp_back.finish()
    out_grad = inner_rows(context, resid_all).astype(BF16)
    out_back = join_windows(seq_exchange(own_cols(out_grad), me), 0)
    bias_sums = jnp.sum(qkv_low.astype(F32), axis=0)
    placed = lambda v: lax.dynamic_update_slice(jnp.zeros((D,), F32), v, (start,))
    q_bias_grad = placed(bias_sums[:SPAN])
    v_bias_grad = placed(bias_sums[2 * SPAN :])
    norm_one_part = times_transposed(qkv_low, w_qkv)
    ln1_gain_grad = jnp.sum(norm_one_part * unit_one, axis=0)
    ln1_bias_grad = jnp.sum(norm_one_part, axis=0)
    qkv_grad = inner_rows(a_one, qkv_low).astype(BF16)

    up_bias_grad = lax.dynamic_update_slice(
        jnp.zeros((dp_count, 4, units), F32), bias_cols.reshape(dp_count, 1, units), (0, me, 0)
    ).reshape(-1)
    small_grad = jnp.concatenate(
        [
            ln1_gain_grad,
            ln1_bias_grad,
            q_bias_grad,
            v_bias_grad,
            out_bias_grad,
            ln2_gain_grad,
            ln2_bias_grad,
            up_bias_grad,
            down_bias_grad,
            jnp.zeros((small_full.shape[0] - 8 * D - FF,), F32),
        ]
    ).astype(BF16)
    small_grad = jnp.pad(
        small_grad.reshape(dp_count, 4, small_len), ((0, 0), (0, tail - 4), (0, wide - small_len))
    )
    attn_parts = jnp.concatenate(
        [
            qkv_grad.reshape(dp_count, block_rows, 3 * SPAN),
            out_back.reshape(dp_count, block_rows, D // 4),
        ],
        axis=2,
    )
    attn_sum = ring.reduce(jnp.concatenate([attn_parts, small_grad], axis=1)).finish()
    small_got = seq_exchange(
        [attn_sum[block_rows + m : block_rows + m + 1, :small_len].astype(BF16) for m in range(4)],
        me,
    )
    small_part = sum(g.astype(F32) for g in small_got).reshape(-1)
    qkv_part, out_part = join_rows(
        attn_sum[:block_rows],
        [qkv_weight.shape[0], out_weight.shape[0]],
        [3 * D, D],
        lambda four: (
            join_head_cols([f[:, : 3 * SPAN] for f in four]),
            jnp.concatenate([f[:, 3 * SPAN :] for f in four], axis=1),
        ),
        me,
    )

    norm_one_in = seq_reduce(norm_one_part.reshape(4, slots, D))
    input_grad = residual_grad[0] + norm_back(
        unit_one[:slots], scale_one[:slots], ln1_gain, norm_one_in
    )
    input_grad = input_grad.astype(BF16).reshape(tokens.shape)

    (up_part,) = join_rows(
        up_sum, [up_weight.shape[0]], [FF], lambda four: (join_unit_cols(four, dp_count),), me
    )
    down_part = down_sum.reshape(-1)
    act_tied, _ = tied(act_low, resid_all)
    mlp_abs = jnp.concatenate(xor_order(mm(act_tied, w_down).astype(BF16).reshape(4, slots, D), me))
    mlp_out = lax.psum_scatter(mlp_abs, "seq", scatter_dimension=0, tiled=True).astype(F32)
    mixed = (residual[0] + mlp_out + down_bias).astype(BF16).reshape(tokens.shape)
    return (mixed, input_grad, qkv_part, out_part, up_part, down_part, small_part)


def solution(mesh):
    rows, flat = P("dp", "seq", None), P(("dp", "seq"))
    return jax.shard_map(
        body,
        mesh=mesh,
        in_specs=(rows, P("dp", None), rows, flat, flat, flat, flat, flat),
        out_specs=(rows, rows, flat, flat, flat, flat, flat),
        check_vma=False,
    )
```

```python
import jax
import jax.numpy as jnp
from jax import lax
from jax.experimental import pallas as pl
from jax.experimental.pallas import tpu as pltpu
from jax.sharding import PartitionSpec as P

D = 1088
FF = 4352
LANES = 1152
MIB = 16
HD = 64
HEADS = D // HD
LEN = 512
F32 = jnp.float32
BF16 = jnp.bfloat16

STARTS = (0, 5, 9, 12)
WINDOW = 5
SPAN = WINDOW * HD

CORE_SWAP = [(0, 1), (1, 0), (2, 3), (3, 2)]
CHIP_SWAP = [(0, 2), (2, 0), (1, 3), (3, 1)]
DIAG_SWAP = [(0, 3), (3, 0), (1, 2), (2, 1)]


def mm(left, right):
    return jnp.dot(left, right, preferred_element_type=F32)


def inner_rows(left, right):
    return lax.dot_general(left, right, (((0,), (0,)), ((), ())), preferred_element_type=F32)


def times_transposed(left, right):
    return lax.dot_general(left, right, (((1,), (1,)), ((), ())), preferred_element_type=F32)


def xor_order(four, me):
    core, chip = me % 2 == 1, me // 2 == 1
    a = [four[0], four[1], four[2], four[3]]
    a = [jnp.where(core, a[i ^ 1], a[i]) for i in range(4)]
    return [jnp.where(chip, a[i ^ 2], a[i]) for i in range(4)]


def seq_blocks(rows):
    other = lax.ppermute(rows, "seq", CHIP_SWAP)
    return other, lax.ppermute(jnp.stack([rows, other]), "seq", CORE_SWAP)


def seq_gather(rows):
    other, across = seq_blocks(rows)
    return jnp.stack([rows, across[0], other, across[1]])


def core_gather(pair):
    across = lax.ppermute(pair, "seq", CORE_SWAP)
    return jnp.stack([pair[0], across[0], pair[1], across[1]])


def core_reduce(blocks):
    low = blocks.astype(BF16)
    across = lax.ppermute(jnp.stack([low[1], low[3]]), "seq", CORE_SWAP).astype(F32)
    return blocks[0] + across[0], blocks[2] + across[1]


def seq_reduce(blocks):
    near, far = core_reduce(blocks)
    return near + lax.ppermute(far.astype(BF16), "seq", CHIP_SWAP).astype(F32)


def pair_reduce(blocks):
    near, far = core_reduce(blocks)
    pair = jnp.stack([near, far]).astype(BF16)
    got = lax.ppermute(pair, "seq", CHIP_SWAP).astype(F32)
    return pair.astype(F32) + jnp.stack([got[1], got[0]])


def seq_exchange(blocks, me):
    return xor_order(rel_exchange(xor_order(blocks, me)), me)


def rel_exchange(rel):
    return [
        rel[0],
        lax.ppermute(rel[1], "seq", CORE_SWAP),
        lax.ppermute(rel[2], "seq", CHIP_SWAP),
        lax.ppermute(rel[3], "seq", DIAG_SWAP),
    ]


def tied(*values):
    return lax.optimization_barrier(values)


class Ring:
    def __init__(self, size):
        self.size = size
        half = size // 2
        walk = [2 * i for i in range(half)] + [2 * i + 1 for i in range(half)][::-1]
        self.ahead = [(walk[i], walk[(i + 1) % size]) for i in range(size)]
        self.back = [(b, a) for a, b in self.ahead]
        index = lax.axis_index("dp")
        self.place = jnp.where(index % 2 == 0, index // 2, size - 1 - index // 2)

    def member(self, step):
        place = (self.place + step + self.size) % self.size
        return jnp.where(place < self.size // 2, 2 * place, 2 * (self.size - 1 - place) + 1)

    def gather_attn(self, chunk):
        return GatherAttn(self, chunk)

    def gather_two(self, first, second):
        return GatherTwo(self, first, second)

    def reduce(self, *parts, cut=None):
        return Reduce(self, parts, cut)


class Steps:
    def step(self, count=1):
        for _ in range(count):
            self.done += 1
            self.move(self.done)

    def tie(self, value):
        value, self.flight = tied(value, self.flight)
        return value

    def finish(self):
        self.step(self.ring.size // 2 - self.done)
        return self.result()


def quick(body, outs, ins, smem=0, scratch=(), mib=MIB):
    spec = lambda space: pl.BlockSpec(memory_space=space)
    return pl.pallas_call(
        body,
        out_shape=[jax.ShapeDtypeStruct(shape, kind) for shape, kind in outs],
        in_specs=[spec(pltpu.SMEM if i < smem else pltpu.VMEM) for i in range(len(ins))],
        out_specs=[spec(pltpu.VMEM)] * len(outs),
        scratch_shapes=list(scratch),
        compiler_params=pltpu.CompilerParams(vmem_limit_bytes=mib * 2**20),
        cost_estimate=pl.CostEstimate(flops=1000, bytes_accessed=1000, transcendentals=0),
    )(*ins)


def place_two(ids, chunks, halves, size):
    last = len(chunks)

    def kernel(ids_ref, *refs):
        sources, outs = refs[: last + 2], refs[last + 2 :]
        for k in range(last):
            for half in range(2):
                outs[half][ids_ref[k]] = sources[k][half]
        for half in range(2):
            outs[half][ids_ref[last]] = sources[last + half][...]

    outs = [((size,) + halves[0].shape, halves[0].dtype)] * 2
    return quick(kernel, outs, [ids, *chunks, *halves], smem=1)


HEAD = 16
TAIL = 896


def place_attn(ids, chunks, halves, size, cut):
    last = len(chunks)
    rows, wide = chunks[0].shape
    rows -= HEAD

    def kernel(ids_ref, *refs):
        sources, (qkv, out, small) = refs[: last + 2], refs[last + 2 :]
        for k in range(last):
            qkv[ids_ref[k]] = sources[k][HEAD:, : 3 * SPAN]
            out[ids_ref[k]] = sources[k][HEAD:, TAIL:]
            small[ids_ref[k]] = sources[k][:HEAD, :]
        first, second, place = sources[last], sources[last + 1], ids_ref[last]
        qkv[place, : cut - HEAD] = first[HEAD:, : 3 * SPAN]
        qkv[place, cut - HEAD :] = second[:, : 3 * SPAN]
        out[place, : cut - HEAD] = first[HEAD:, TAIL:]
        out[place, cut - HEAD :] = second[:, TAIL:]
        small[place] = first[:HEAD, :]

    outs = [
        ((size, rows, 3 * SPAN), BF16),
        ((size, rows, wide - TAIL), BF16),
        ((size, HEAD, wide), BF16),
    ]
    return quick(kernel, outs, [ids, *chunks, *halves], smem=1)


def dot(left, right, left_dim, right_dim):
    return lax.dot_general(
        left, right, (((left_dim,), (right_dim,)), ((), ())), preferred_element_type=F32
    )


def qkv_kernel(unit, gain, shift, weight, bias):
    rows = unit.shape[0]

    def kernel(unit_ref, gain_ref, shift_ref, weight_ref, bias_ref, a_ref, qkv_ref):
        for at in range(0, rows, 128):
            part = slice(at, at + 128)
            a = (unit_ref[part, :] * gain_ref[...] + shift_ref[...]).astype(BF16)
            a_ref[part, :] = a
            qkv_ref[part, :] = (dot(a, weight_ref[...], 1, 0) + bias_ref[...]).astype(BF16)

    outs = [((rows, D), BF16), ((rows, 3 * SPAN), BF16)]
    row = lambda v: v.reshape(1, -1)
    return quick(kernel, outs, [unit, row(gain), row(shift), weight, row(bias)])


def put_rows(ref, at, rows):
    ref[at, :, :D] = rows
    ref[at, :, D:] = jnp.zeros((rows.shape[0], LANES - D), rows.dtype)


def put_block(block, product, send_ref, keep_ref):
    if block % 2 == 1:
        put_rows(send_ref, block // 2, product.astype(BF16))
    else:
        keep_ref[block // 2] = product


def halves(slots):
    return [((2, slots, LANES), BF16), ((2, slots, D), F32)]


def attention(qkv, positions, w_out):
    rows = qkv.shape[0]
    slots = rows // 4

    def kernel(
        qkv_ref, col_ref, row_ref, w_ref, context_ref, log_ref, send_ref, keep_ref
    ):
        for block in range(4):
            part = slice(block * slots, (block + 1) * slots)
            mask = col_ref[part, :] >= row_ref[...]
            heads = []
            for h in range(WINDOW):
                lo, hi = h * HD, (h + 1) * HD
                queries = qkv_ref[part, lo:hi]
                keys = qkv_ref[:, SPAN + lo : SPAN + hi]
                values = qkv_ref[:, 2 * SPAN + lo : 2 * SPAN + hi]
                scores = jnp.where(mask, dot(queries, keys, 1, 1) * 0.125, -1e30)
                peak = jnp.max(scores, axis=1, keepdims=True)
                exps = jnp.exp(scores - peak)
                total = jnp.sum(exps, axis=1, keepdims=True)
                heads.append(dot((exps * (1.0 / total)).astype(BF16), values, 1, 0))
                log_ref[part, h : h + 1] = peak + jnp.log(total)
            context = jnp.concatenate(heads, axis=1).astype(BF16)
            context_ref[part, :] = context
            put_block(block, dot(context, w_ref[...], 1, 0), send_ref, keep_ref)

    outs = [((rows, SPAN), BF16), ((rows, 8), F32)] + halves(slots)
    ins = [qkv, positions.reshape(-1, 1), positions.reshape(1, -1), w_out]
    return quick(kernel, outs, ins)


def widened(rows):
    return jnp.pad(rows, ((0, 0), (0, LANES - D)))


def row(vector):
    return vector.reshape(1, -1)


def norm(values):
    mean = jnp.mean(values, axis=-1, keepdims=True)
    centred = values - mean
    scale = lax.rsqrt(jnp.mean(centred * centred, axis=-1, keepdims=True) + 1e-05)
    return centred * scale, scale


def first_norm(own, other, across):
    slots = own.shape[0]

    def kernel(own_ref, other_ref, across_ref, unit_ref):
        for block, part in enumerate((own_ref, across_ref.at[0], other_ref, across_ref.at[1])):
            unit_ref[block * slots : (block + 1) * slots, :] = norm(part[:, :D].astype(F32))[0]

    return quick(kernel, [((4 * slots, D), F32)], [own, other, across])[0]


def join_blocks(own, other, across):
    slots = own.shape[0]

    def kernel(own_ref, other_ref, across_ref, out_ref):
        for block, part in enumerate((own_ref, across_ref.at[0], other_ref, across_ref.at[1])):
            out_ref[block * slots : (block + 1) * slots, :] = part[:, :D]

    return quick(kernel, [((4 * slots, D), own.dtype)], [own, other, across])[0]


def pair_sum(keep, across):
    def kernel(keep_ref, across_ref, out_ref):
        for i in range(2):
            put_rows(out_ref, i, (keep_ref[i] + across_ref[i, :, :D].astype(F32)).astype(BF16))

    return quick(kernel, [(across.shape, BF16)], [keep, across])[0]


def second_norm(pair, got, own, other, out_bias, gain, shift):
    slots = own.shape[0]

    def kernel(
        pair_ref, got_ref, own_ref, other_ref, bias_ref, gain_ref, shift_ref,
        residual_ref, unit_ref, scale_ref, a_ref,
    ):
        for i, part in enumerate((own_ref, other_ref)):
            attn = pair_ref[i, :, :D].astype(F32) + got_ref[1 - i, :, :D].astype(F32)
            residual = part[:, :D].astype(F32) + attn + bias_ref[...]
            if i == 0:
                residual_ref[...] = residual
            unit, scale = norm(residual)
            unit_ref[i] = unit
            scale_ref[i] = scale
            put_rows(a_ref, i, (unit * gain_ref[...] + shift_ref[...]).astype(BF16))

    two = (2, slots, D)
    outs = [((slots, D), F32), (two, F32), ((2, slots, 1), F32), (pair.shape, BF16)]
    return quick(
        kernel, outs, [pair, got, own, other, row(out_bias), row(gain), row(shift)]
    )


def mlp_up(pair, across, weight, bias):
    slots = pair.shape[1]

    def kernel(pair_ref, across_ref, weight_ref, bias_ref, all_ref, act_ref, slope_ref):
        for block in range(4):
            part = slice(block * slots, (block + 1) * slots)
            rows = (across_ref if block % 2 else pair_ref)[block // 2, :, :D]
            all_ref[part, :] = rows
            pre = dot(rows, weight_ref[...], 1, 0) + bias_ref[...]
            below = 0.5 * (1.0 + lax.erf(pre * 0.7071067811865476))
            act_ref[part, :] = (pre * below).astype(BF16)
            slope_ref[part, :] = below + pre * jnp.exp(-0.5 * pre * pre) * 0.3989422804014327

    shape = (4 * slots, D)
    outs = [(shape, BF16), (shape, BF16), (shape, F32)]
    return quick(kernel, outs, [pair, across, weight, row(bias)])


def mlp_down_back(grads, w_down, slope, w_up):
    rows = grads.shape[0]
    slots = rows // 4

    def kernel(
        grad_ref, down_ref, slope_ref, up_ref, low_ref, send_ref, keep_ref, sums_ref
    ):
        sums = jnp.zeros((1, D), F32)
        for block in range(4):
            part = slice(block * slots, (block + 1) * slots)
            pre = dot(grad_ref[part, :], down_ref[...], 1, 1) * slope_ref[part, :]
            low = pre.astype(BF16)
            low_ref[part, :] = low
            sums += jnp.sum(low.astype(F32), axis=0, keepdims=True)
            put_block(block, dot(low, up_ref[...], 1, 1), send_ref, keep_ref)
        sums_ref[...] = sums

    outs = [((rows, D), BF16)] + halves(slots) + [((1, D), F32)]
    return quick(kernel, outs, [grads, w_down, slope, w_up])


def norm_pull(unit, scale, gain, grad):
    lifted = grad * gain
    return scale * (
        lifted
        - jnp.mean(lifted, axis=-1, keepdims=True)
        - unit * jnp.mean(lifted * unit, axis=-1, keepdims=True)
    )


def second_norm_back(pair, got, unit, scale, gain, own_grad, other_grad):
    slots = own_grad.shape[0]

    def kernel(
        pair_ref, got_ref, unit_ref, scale_ref, gain_ref, own_ref, other_ref,
        resid_ref, low_ref, sums_ref,
    ):
        for i, part in enumerate((own_ref, other_ref)):
            grad = pair_ref[i, :, :D].astype(F32) + got_ref[1 - i, :, :D].astype(F32)
            back = norm_pull(unit_ref[i], scale_ref[i], gain_ref[...], grad)
            resid = part[:, :D].astype(F32) + back
            low = resid.astype(BF16)
            put_rows(low_ref, i, low)
            if i == 0:
                resid_ref[...] = resid
                sums_ref[0:1, :] = jnp.sum(grad * unit_ref[i], axis=0, keepdims=True)
                sums_ref[1:2, :] = jnp.sum(grad, axis=0, keepdims=True)
                sums_ref[2:3, :] = jnp.sum(low.astype(F32), axis=0, keepdims=True)
                sums_ref[3:4, :] = jnp.sum(part[...].astype(F32), axis=0, keepdims=True)

    outs = [((slots, D), F32), (pair.shape, BF16), ((8, D), F32)]
    return quick(kernel, outs, [pair, got, unit, scale, row(gain), own_grad, other_grad])


def first_norm_back(low, w_qkv, unit):
    rows = low.shape[0]
    slots = rows // 4

    def kernel(low_ref, w_ref, unit_ref, send_ref, keep_ref, sums_ref, bias_ref):
        gain = jnp.zeros((1, D), F32)
        shift = jnp.zeros((1, D), F32)
        bias = jnp.zeros((1, 3 * SPAN), F32)
        for block in range(4):
            part = slice(block * slots, (block + 1) * slots)
            low = low_ref[part, :]
            back = dot(low, w_ref[...], 1, 1)
            gain += jnp.sum(back * unit_ref[part, :], axis=0, keepdims=True)
            shift += jnp.sum(back, axis=0, keepdims=True)
            bias += jnp.sum(low.astype(F32), axis=0, keepdims=True)
            put_block(block, back, send_ref, keep_ref)
        sums_ref[0:1, :] = gain
        sums_ref[1:2, :] = shift
        bias_ref[...] = bias

    outs = halves(slots) + [((8, D), F32), ((1, 3 * SPAN), F32)]
    return quick(kernel, outs, [low, w_qkv, unit])


def attn_parts(a_one, low, out_back, small):
    count, rows = out_back.shape[0], D // out_back.shape[0]
    wide = 3 * SPAN + D // 4

    def kernel(a_ref, low_ref, out_ref, small_ref, parts_ref, total_ref):
        total_ref[...] = dot(a_ref[...], low_ref[...], 0, 0)
        for k in range(count):
            piece = total_ref[k * rows : (k + 1) * rows, :].astype(BF16)
            parts_ref[k, HEAD:, : 3 * SPAN] = piece
            parts_ref[k, HEAD:, 3 * SPAN :] = out_ref[k]
            parts_ref[k, :HEAD, :] = small_ref[k]

    scratch = [pltpu.VMEM((D, 3 * SPAN), F32)]
    outs = [((count, HEAD + rows, wide), BF16)]
    return quick(kernel, outs, [a_one, low, out_back, small], scratch=scratch)[0]


def core_sums(keep, across):
    def kernel(keep_ref, across_ref, near_ref, far_ref):
        near_ref[...] = keep_ref[0] + across_ref[0, :, :D].astype(F32)
        put_rows(far_ref, 0, (keep_ref[1] + across_ref[1, :, :D].astype(F32)).astype(BF16))

    outs = [(keep.shape[1:], F32), ((1,) + across.shape[1:], BF16)]
    return quick(kernel, outs, [keep, across])


def input_back(own, gain, near, got, resid):
    def kernel(own_ref, gain_ref, near_ref, got_ref, resid_ref, out_ref):
        unit, scale = norm(own_ref[...].astype(F32))
        grad = near_ref[...] + got_ref[0, :, :D].astype(F32)
        back = norm_pull(unit, scale, gain_ref[...], grad)
        out_ref[...] = (resid_ref[...] + back).astype(BF16)

    return quick(kernel, [(own.shape, BF16)], [own, row(gain), near, got, resid])[0]


def out_gradient(me, context, pair, across):
    slots, cols = pair.shape[1], D // 4

    def kernel(me_ref, context_ref, pair_ref, across_ref, *outs):
        total = jnp.zeros((SPAN, D), F32)
        for block in range(4):
            part = slice(block * slots, (block + 1) * slots)
            rows = (across_ref if block % 2 else pair_ref)[block // 2, :, :D]
            total += dot(context_ref[part, :], rows, 0, 0)
        low = total.astype(BF16)
        for m in range(4):

            @pl.when(me_ref[0] == m)
            def _():
                for r in range(4):
                    outs[r][...] = low[:, (m ^ r) * cols : ((m ^ r) + 1) * cols]

    ins = [me.reshape(1).astype(jnp.int32), context, pair, across]
    return quick(kernel, [((SPAN, cols), BF16)] * 4, ins, smem=1)


def attention_back(qkv, pair, across, w_out, logs, positions):
    rows = qkv.shape[0]
    slots = rows // 4

    def kernel(
        qkv_ref, pair_ref, across_ref, w_ref, log_ref, col_ref, row_ref, low_ref,
        keys_acc, values_acc,
    ):
        for block in range(4):
            part = slice(block * slots, (block + 1) * slots)
            mask = col_ref[part, :] >= row_ref[...]
            resid = (across_ref if block % 2 else pair_ref)[block // 2, :, :D]
            grads = dot(resid, w_ref[...], 1, 1).astype(BF16)
            heads = []
            for h in range(WINDOW):
                lo, hi = h * HD, (h + 1) * HD
                queries = qkv_ref[part, lo:hi]
                keys = qkv_ref[:, SPAN + lo : SPAN + hi]
                values = qkv_ref[:, 2 * SPAN + lo : 2 * SPAN + hi]
                grad = grads[:, lo:hi]
                scores = jnp.where(mask, dot(queries, keys, 1, 1) * 0.125, -1e30)
                probs = jnp.exp(scores - log_ref[part, h : h + 1])
                prob_grad = dot(grad, values, 1, 1)
                inner = jnp.sum(probs * prob_grad, axis=1, keepdims=True)
                score_low = (probs * (prob_grad - inner)).astype(BF16)
                heads.append(dot(score_low, keys, 1, 0) * 0.125)
                keys_grad = dot(score_low, queries, 0, 0) * 0.125
                values_grad = dot(probs.astype(BF16), grad, 0, 0)
                if block == 0:
                    keys_acc[h] = keys_grad
                    values_acc[h] = values_grad
                else:
                    keys_acc[h] += keys_grad
                    values_acc[h] += values_grad
            low_ref[part, :SPAN] = jnp.concatenate(heads, axis=1).astype(BF16)
        for i, acc in enumerate((keys_acc, values_acc)):
            joined = jnp.concatenate([acc[h] for h in range(WINDOW)], axis=1)
            low_ref[:, (i + 1) * SPAN : (i + 2) * SPAN] = joined.astype(BF16)

    scratch = [pltpu.VMEM((WINDOW, rows, HD), F32)] * 2
    ins = [qkv, pair, across, w_out, logs, positions.reshape(-1, 1), positions.reshape(1, -1)]
    return quick(kernel, [((rows, 3 * SPAN), BF16)], ins, scratch=scratch)[0]


def ring_add(ids, parts, flight, cut=None):
    count = len(parts)
    rows, cols = parts[0].shape[1:]
    half = flight[0].shape != (count, rows, cols)

    def kernel(ids_ref, *refs):
        ahead, back = refs[2 * count], refs[2 * count + 1]
        out_ahead, out_back = refs[2 * count + 2], refs[2 * count + 3]
        total = lambda a, b: (a.astype(F32) + b.astype(F32)).astype(BF16)
        mine = [refs[i][0] for i in range(2 * count)]
        if half and count == 2:
            out_ahead[0], out_ahead[1] = total(mine[0], ahead[...]), mine[1]
            out_back[0], out_back[1] = mine[2], total(mine[3], back[...])
        elif half:
            out_ahead[0, :cut] = total(mine[0][:cut], ahead[...])
            out_ahead[0, cut:] = mine[0][cut:]
            out_back[0, :cut] = mine[1][:cut]
            out_back[0, cut:] = total(mine[1][cut:], back[...])
        else:
            for i in range(count):
                out_ahead[i] = total(mine[i], ahead[i])
                out_back[i] = total(mine[count + i], back[i])

    pick = lambda n: pl.BlockSpec((1, rows, cols), lambda i, ids, n=n: (ids[n], 0, 0))
    whole = lambda v: pl.BlockSpec(v.shape, lambda i, ids, v=v: (0,) * v.ndim)
    out = jax.ShapeDtypeStruct((count, rows, cols), BF16)
    return pl.pallas_call(
        kernel,
        out_shape=[out] * 2,
        grid_spec=pltpu.PrefetchScalarGridSpec(
            num_scalar_prefetch=1,
            grid=(1,),
            in_specs=[pick(0)] * count + [pick(1)] * count + [whole(f) for f in flight],
            out_specs=[whole(out)] * 2,
        ),
        compiler_params=pltpu.CompilerParams(vmem_limit_bytes=MIB * 2**20),
        cost_estimate=pl.CostEstimate(flops=1000, bytes_accessed=1000, transcendentals=0),
    )(ids, *parts, *parts, *flight)


def ring_total(ids, parts, flight):
    count = len(parts)
    rows, cols = parts[0].shape[1:]

    def kernel(ids_ref, *refs):
        for i in range(count):
            mine = refs[i][0].astype(F32) + refs[count][i].astype(F32)
            refs[count + 2 + i][...] = mine + refs[count + 1][i].astype(F32)

    pick = pl.BlockSpec((1, rows, cols), lambda i, ids: (ids[0], 0, 0))
    whole = pl.BlockSpec((count, rows, cols), lambda i, ids: (0, 0, 0))
    return pl.pallas_call(
        kernel,
        out_shape=[jax.ShapeDtypeStruct((rows, cols), F32)] * count,
        grid_spec=pltpu.PrefetchScalarGridSpec(
            num_scalar_prefetch=1,
            grid=(1,),
            in_specs=[pick] * count + [whole] * 2,
            out_specs=[pl.BlockSpec((rows, cols), lambda i, ids: (0, 0))] * count,
        ),
        compiler_params=pltpu.CompilerParams(vmem_limit_bytes=MIB * 2**20),
        cost_estimate=pl.CostEstimate(flops=1000, bytes_accessed=1000, transcendentals=0),
    )(ids, *parts, *flight)


def split_units(me, rows, dp_count):
    width = FF // dp_count // 4

    def kernel(me_ref, rows_ref, *outs):
        value = rows_ref[...]
        cut = lambda d, s: value[:, (4 * d + s) * width : (4 * d + s + 1) * width]
        four = [jnp.concatenate([cut(d, s) for d in range(dp_count)], axis=1) for s in range(4)]
        for m in range(4):

            @pl.when(me_ref[0] == m)
            def _():
                for r in range(4):
                    outs[r][...] = four[m ^ r]

    outs = [((rows.shape[0], D), BF16)] * 4
    return quick(kernel, outs, [me.reshape(1).astype(jnp.int32), rows], smem=1)


def join_units(four):
    rows = four[0].shape[0]
    blocks = FF // 128

    def kernel(*refs):
        parts, out_ref = [r[...].astype(F32) for r in refs[:4]], refs[4]
        width = 136
        pieces = []
        for d in range(D // width):
            pieces += [p[:, d * width : (d + 1) * width] for p in parts]
        joined = jnp.concatenate(pieces, axis=1)
        for t in range(blocks):
            out_ref[pl.ds(t, rows, stride=blocks), :] = joined[:, t * 128 : (t + 1) * 128]

    out = quick(kernel, [((rows * blocks, 128), F32)], four)[0]
    return out.reshape(-1)


class GatherAttn(Steps):
    def __init__(self, ring, chunk):
        self.ring, self.done = ring, 0
        self.flight = (chunk, chunk)
        self.chunks, self.order = [chunk], [0]
        self.cut = 80

    def move(self, step):
        ring, (ahead, back) = self.ring, self.flight
        last = step == ring.size // 2
        if last:
            ahead, back = ahead[: self.cut], back[self.cut :]
        ahead = lax.ppermute(ahead, "dp", ring.ahead)
        back = lax.ppermute(back, "dp", ring.back)
        self.flight = (ahead, back)
        if not last:
            self.chunks += [ahead, back]
            self.order += [-step, step]

    def result(self):
        ids = jnp.stack([self.ring.member(k) for k in self.order + [self.ring.size // 2]])
        return place_attn(ids.astype(jnp.int32), self.chunks, self.flight, self.ring.size, self.cut)


class GatherTwo(Steps):
    def __init__(self, ring, first, second):
        self.ring, self.done = ring, 0
        chunk = jnp.stack([first, second])
        self.flight = (chunk, chunk)
        self.chunks, self.order = [chunk], [0]

    def move(self, step):
        ring, (ahead, back) = self.ring, self.flight
        last = step == ring.size // 2
        if last:
            ahead, back = ahead[0], back[1]
        ahead = lax.ppermute(ahead, "dp", ring.ahead)
        back = lax.ppermute(back, "dp", ring.back)
        self.flight = (ahead, back)
        if not last:
            self.chunks += [ahead, back]
            self.order += [-step, step]

    def result(self):
        ids = jnp.stack([self.ring.member(k) for k in self.order + [self.ring.size // 2]])
        return place_two(ids.astype(jnp.int32), self.chunks, self.flight, self.ring.size)


class Reduce(Steps):
    def __init__(self, ring, parts, cut=None):
        self.ring, self.parts, self.cut, self.done = ring, parts, cut, 0
        far = [
            lax.dynamic_index_in_dim(p, ring.member(ring.size // 2), 0, False) for p in parts
        ]
        self.flight = tuple(far) if cut is None else (far[0][:cut], far[0][cut:])

    def ids(self, *steps):
        return jnp.stack([self.ring.member(k) for k in steps]).astype(jnp.int32)

    def move(self, step):
        left = self.ring.size // 2 - step + 1
        ahead, back = self.flight
        if step > 1:
            ahead, back = ring_add(self.ids(left, -left), self.parts, self.flight, self.cut)
        self.flight = (
            lax.ppermute(ahead, "dp", self.ring.ahead),
            lax.ppermute(back, "dp", self.ring.back),
        )

    def result(self):
        return ring_total(self.ids(0), self.parts, self.flight)


class Whole:
    def gather_attn(self, chunk):
        got = lax.all_gather(chunk, "dp", axis=0)
        parts = [got[:, HEAD:, : 3 * SPAN], got[:, HEAD:, TAIL:], got[:, :HEAD]]
        return Whole.Ready(parts, chunk)

    def gather_two(self, first, second):
        got = lax.all_gather(jnp.stack([first, second]), "dp", axis=0)
        return Whole.Ready([got[:, 0], got[:, 1]], first)

    def reduce(self, *parts, cut=None):
        got = [lax.psum_scatter(p, "dp", scatter_dimension=0, tiled=True)[0] for p in parts]
        return Whole.Ready([g.astype(F32) for g in got], got[0])

    class Ready(Steps):
        def __init__(self, value, flight):
            self.value, self.flight = value, flight

        def step(self, count=1):
            pass

        def finish(self):
            return self.value


def join_windows(four, axis):
    cut = lambda part, lo, hi: lax.slice_in_dim(part, lo, hi, axis=axis)
    return jnp.concatenate(
        [
            four[0],
            cut(four[1], 0, SPAN - HD),
            cut(four[2], 0, SPAN - HD),
            cut(four[3], HD, SPAN),
        ],
        axis=axis,
    )


def head_cols(rows):
    piece = lambda s, b: rows[:, b * D + s * HD : b * D + s * HD + SPAN]
    return [jnp.concatenate([piece(s, b) for b in range(3)], axis=1) for s in STARTS]


def join_head_cols(four):
    block = lambda b: join_windows([f[:, b * SPAN : (b + 1) * SPAN] for f in four], 1)
    return jnp.concatenate([block(b) for b in range(3)], axis=1)


def own_cols(rows):
    return [rows[:, s * (D // 4) : (s + 1) * (D // 4)] for s in range(4)]


def unit_cols(rows, dp_count):
    four = rows.reshape(rows.shape[0], dp_count, 4, -1)
    return [four[:, :, s].reshape(rows.shape[0], D) for s in range(4)]


def join_unit_cols(four, dp_count):
    if FF // dp_count // 4 == 136:
        return join_units(four)
    parts = [f.reshape(f.shape[0], dp_count, 1, -1) for f in four]
    return jnp.concatenate(parts, axis=2).reshape(four[0].shape[0], FF)


def split_rows(flats, widths, cols_of, me):
    if all(flat.shape[0] % width == 0 for flat, width in zip(flats, widths)):
        rows = [flat.reshape(-1, width) for flat, width in zip(flats, widths)]
        return jnp.concatenate(seq_exchange(cols_of(rows), me))
    rows = [
        lax.all_gather(flat, "seq", axis=0, tiled=True).reshape(-1, width)
        for flat, width in zip(flats, widths)
    ]
    return xor_order(cols_of(rows), me)[0]


def join_rows(rows, shares, widths, join_cols, me):
    low = rows.astype(BF16)
    count = rows.shape[0] // 4
    if all(share % width == 0 for share, width in zip(shares, widths)):
        got = seq_exchange([low[m * count : (m + 1) * count] for m in range(4)], me)
        return [part.astype(F32).reshape(-1) for part in join_cols(got)]
    got = join_cols(list(lax.all_gather(low, "seq", axis=0)))
    return [
        lax.dynamic_slice_in_dim(part.reshape(-1), me * share, share, 0).astype(F32)
        for part, share in zip(got, shares)
    ]


def body(tokens, order, cotangent, qkv_weight, out_weight, up_weight, down_weight, small_params):
    slots = tokens.shape[1]
    dp_count = lax.axis_size("dp")
    me = lax.axis_index("seq")
    units = FF // (dp_count * 4)
    block_rows = D // dp_count
    ring = Ring(dp_count) if dp_count == 8 else Whole()
    start = jnp.where(me == 0, 0, jnp.where(me == 3, 12, 4 * me + 1)) * HD

    small_len = small_params.shape[0]
    wide = 3 * SPAN + D // 4

    attn_rows = split_rows(
        [qkv_weight, out_weight],
        [3 * D, D],
        lambda r: [
            jnp.concatenate([q, o], axis=1) for q, o in zip(head_cols(r[0]), own_cols(r[1]))
        ],
        me,
    )
    small_row = jnp.pad(small_params.reshape(1, -1), ((0, 0), (0, wide - small_len)))
    small_rows = xor_order(list(seq_gather(small_row)), me)
    blank = jnp.zeros((HEAD - 4, wide), BF16)
    attn_chunk = jnp.concatenate(small_rows + [blank, attn_rows])
    attn_chunk, up_flat = tied(attn_chunk, up_weight)
    attn_ring = ring.gather_attn(attn_chunk)
    attn_ring.step()
    if block_rows == 136:
        up_four = split_units(me, up_flat.reshape(-1, FF), dp_count)
        up_rows = jnp.concatenate(xor_order(rel_exchange(up_four), me))
    else:
        up_rows = split_rows([up_flat], [FF], lambda r: unit_cols(r[0], dp_count), me)
    positions = jnp.concatenate(xor_order(order.reshape(4, slots), me))
    positions = attn_ring.tie(positions)
    attn_ring.step()
    own_tokens = tokens.reshape(-1, D)
    other_tokens, across_tokens = seq_blocks(widened(own_tokens))
    unit_one = first_norm(own_tokens, other_tokens, across_tokens)
    unit_one, up_rows = attn_ring.tie((unit_one, up_rows))
    own_grad = attn_ring.tie(cotangent.reshape(-1, D))
    attn_ring.step()
    mlp_rows = attn_ring.tie((up_rows, down_weight.reshape(-1, D)))
    mlp_ring = ring.gather_two(*mlp_rows)
    other_grad, across_grad = seq_blocks(widened(own_grad))
    grad_all = join_blocks(own_grad, other_grad, across_grad)
    w_qkv, out_tail, small_all = attn_ring.finish()
    mlp_ring.step()
    w_qkv = w_qkv.reshape(D, 3 * SPAN)
    out_cols = out_tail[:, :, 3 * SPAN - TAIL :].reshape(D, D // 4)
    small_full = small_all[:, :4, :small_len].reshape(-1).astype(F32)
    out_got = seq_exchange([out_cols[s * HD : s * HD + SPAN] for s in STARTS], me)
    w_out = jnp.concatenate(out_got, axis=1)
    row_head = jnp.arange(SPAN) // HD
    repeated = jnp.where(me == 0, WINDOW, jnp.where(me == 3, 0, WINDOW - 1))
    w_out = jnp.where((row_head == repeated)[:, None], 0, w_out).astype(BF16)

    at = lambda i: small_full[i * D : (i + 1) * D]
    ln1_gain, ln1_bias, q_bias, v_bias, out_bias, ln2_gain, ln2_bias = [at(i) for i in range(7)]
    up_bias = small_full[7 * D : 7 * D + FF]
    down_bias = small_full[7 * D + FF : 8 * D + FF]

    window = lambda v: lax.dynamic_slice_in_dim(v, start, SPAN, 0)
    bias_qkv = jnp.concatenate([window(q_bias), jnp.zeros((SPAN,), F32), window(v_bias)])
    a_one, qkv_vals = qkv_kernel(unit_one, ln1_gain, ln1_bias, w_qkv, bias_qkv)
    a_one, qkv_vals = mlp_ring.tie((a_one, qkv_vals))
    mlp_ring.step()
    context, logs, send, keep = mlp_ring.tie(attention(qkv_vals, positions, w_out))
    mlp_ring.step()
    across = lax.ppermute(send, "seq", CORE_SWAP)
    pair, grad_all = tied(pair_sum(keep, across), grad_all)
    w_up, w_down = (w.reshape(D, D) for w in mlp_ring.finish())
    got = lax.ppermute(pair, "seq", CHIP_SWAP)
    residual, unit_two, scale_two, a_two = second_norm(
        pair, got, own_tokens, other_tokens, out_bias, ln2_gain, ln2_bias
    )
    a_across = lax.ppermute(a_two, "seq", CORE_SWAP)
    up_bias_own = lax.dynamic_index_in_dim(
        up_bias.reshape(dp_count, 4, units), me, 1, False
    ).reshape(-1)
    a_two_all, act_low, slope = mlp_up(a_two, a_across, w_up, up_bias_own)

    pre_low, send, keep, bias_cols = mlp_down_back(grad_all, w_down, slope, w_up)
    across = lax.ppermute(send, "seq", CORE_SWAP)
    down_grad = inner_rows(act_low, grad_all).astype(BF16)
    up_grad = inner_rows(a_two_all, pre_low).astype(BF16)
    pair, up_grad, down_grad = tied(pair_sum(keep, across), up_grad, down_grad)
    mlp_back = ring.reduce(
        down_grad.reshape(dp_count, units, D), up_grad.reshape(dp_count, block_rows, D)
    )
    mlp_back.step()
    got = mlp_back.tie(lax.ppermute(pair, "seq", CHIP_SWAP))
    mlp_back.step()
    resid, resid_low, sums_two = second_norm_back(
        pair, got, unit_two, scale_two, ln2_gain, own_grad, other_grad
    )

    resid_across = lax.ppermute(resid_low, "seq", CORE_SWAP)
    out_four = out_gradient(me, context, resid_low, resid_across)
    out_four, resid_low, resid_across = tied(out_four, resid_low, resid_across)
    out_back = join_windows(xor_order(rel_exchange(out_four), me), 0)
    qkv_low = attention_back(qkv_vals, resid_low, resid_across, w_out, logs, positions)
    qkv_low = mlp_back.tie(qkv_low)
    mlp_back.step()
    send, keep, sums_one, bias_sums = first_norm_back(qkv_low, w_qkv, unit_one)
    bias_sums = bias_sums.reshape(-1)
    placed = lambda v: lax.dynamic_update_slice(jnp.zeros((D,), F32), v, (start,))
    q_bias_grad = placed(bias_sums[:SPAN])
    v_bias_grad = placed(bias_sums[2 * SPAN :])

    up_bias_grad = lax.dynamic_update_slice(
        jnp.zeros((dp_count, 4, units), F32), bias_cols.reshape(dp_count, 1, units), (0, me, 0)
    ).reshape(-1)
    small_grad = jnp.concatenate(
        [
            sums_one[0],
            sums_one[1],
            q_bias_grad,
            v_bias_grad,
            sums_two[2],
            sums_two[0],
            sums_two[1],
            up_bias_grad,
            sums_two[3],
            jnp.zeros((small_full.shape[0] - 8 * D - FF,), F32),
        ]
    ).astype(BF16)
    small_grad = jnp.pad(
        small_grad.reshape(dp_count, 4, small_len), ((0, 0), (0, HEAD - 4), (0, wide - small_len))
    )
    out_back = out_back.reshape(dp_count, block_rows, D // 4)
    if block_rows == 136:
        parts = attn_parts(a_one, qkv_low, out_back, small_grad)
    else:
        qkv_grad = inner_rows(a_one, qkv_low).astype(BF16)
        parts = jnp.concatenate([qkv_grad.reshape(dp_count, block_rows, -1), out_back], axis=2)
        parts = jnp.concatenate([small_grad, parts], axis=1)
    attn_back = ring.reduce(parts, cut=80)
    attn_back.step()
    down_sum, up_sum = mlp_back.finish()
    down_sum, up_sum, send, keep = attn_back.tie((down_sum, up_sum, send, keep))
    attn_back.step()
    near, far = core_sums(keep, lax.ppermute(send, "seq", CORE_SWAP))
    got = lax.ppermute(far, "seq", CHIP_SWAP)
    input_grad = input_back(own_tokens, ln1_gain, near, got, resid).reshape(tokens.shape)
    (up_part,) = join_rows(
        up_sum, [up_weight.shape[0]], [FF], lambda four: (join_unit_cols(four, dp_count),), me
    )
    (attn_sum,) = attn_back.finish()
    small_got = seq_exchange(
        [attn_sum[m : m + 1, :small_len].astype(BF16) for m in range(4)],
        me,
    )
    small_part = sum(g.astype(F32) for g in small_got).reshape(-1)
    qkv_part, out_part = join_rows(
        attn_sum[HEAD:],
        [qkv_weight.shape[0], out_weight.shape[0]],
        [3 * D, D],
        lambda four: (
            join_head_cols([f[:, : 3 * SPAN] for f in four]),
            jnp.concatenate([f[:, 3 * SPAN :] for f in four], axis=1),
        ),
        me,
    )

    down_part = down_sum.reshape(-1)
    act_tied, _ = tied(act_low, qkv_low)
    mlp_abs = jnp.concatenate(xor_order(mm(act_tied, w_down).astype(BF16).reshape(4, slots, D), me))
    mlp_out = lax.psum_scatter(mlp_abs, "seq", scatter_dimension=0, tiled=True).astype(F32)
    mixed = (residual + mlp_out + down_bias).astype(BF16).reshape(tokens.shape)
    return (mixed, input_grad, qkv_part, out_part, up_part, down_part, small_part)


def solution(mesh):
    rows, flat = P("dp", "seq", None), P(("dp", "seq"))
    return jax.shard_map(
        body,
        mesh=mesh,
        in_specs=(rows, P("dp", None), rows, flat, flat, flat, flat, flat),
        out_specs=(rows, rows, flat, flat, flat, flat, flat),
        check_vma=False,
    )
```

```python
import jax
import jax.numpy as jnp
from jax import lax
from jax.experimental import pallas as pl
from jax.experimental.pallas import tpu as pltpu
from jax.sharding import PartitionSpec as P

D = 1088
FF = 4352
LANES = 1152
MIB = 16
HD = 64
HEADS = D // HD
LEN = 512
F32 = jnp.float32
BF16 = jnp.bfloat16

STARTS = (0, 5, 9, 12)
WINDOW = 5
SPAN = WINDOW * HD

CORE_SWAP = [(0, 1), (1, 0), (2, 3), (3, 2)]
CHIP_SWAP = [(0, 2), (2, 0), (1, 3), (3, 1)]
DIAG_SWAP = [(0, 3), (3, 0), (1, 2), (2, 1)]


def mm(left, right):
    return jnp.dot(left, right, preferred_element_type=F32)


def inner_rows(left, right):
    return lax.dot_general(left, right, (((0,), (0,)), ((), ())), preferred_element_type=F32)


def times_transposed(left, right):
    return lax.dot_general(left, right, (((1,), (1,)), ((), ())), preferred_element_type=F32)


def xor_order(four, me):
    core, chip = me % 2 == 1, me // 2 == 1
    a = [four[0], four[1], four[2], four[3]]
    a = [jnp.where(core, a[i ^ 1], a[i]) for i in range(4)]
    return [jnp.where(chip, a[i ^ 2], a[i]) for i in range(4)]


def seq_blocks(rows):
    other = lax.ppermute(rows, "seq", CHIP_SWAP)
    return other, lax.ppermute(jnp.stack([rows, other]), "seq", CORE_SWAP)


def seq_gather(rows):
    other, across = seq_blocks(rows)
    return jnp.stack([rows, across[0], other, across[1]])


def core_gather(pair):
    across = lax.ppermute(pair, "seq", CORE_SWAP)
    return jnp.stack([pair[0], across[0], pair[1], across[1]])


def core_reduce(blocks):
    low = blocks.astype(BF16)
    across = lax.ppermute(jnp.stack([low[1], low[3]]), "seq", CORE_SWAP).astype(F32)
    return blocks[0] + across[0], blocks[2] + across[1]


def seq_reduce(blocks):
    near, far = core_reduce(blocks)
    return near + lax.ppermute(far.astype(BF16), "seq", CHIP_SWAP).astype(F32)


def pair_reduce(blocks):
    near, far = core_reduce(blocks)
    pair = jnp.stack([near, far]).astype(BF16)
    got = lax.ppermute(pair, "seq", CHIP_SWAP).astype(F32)
    return pair.astype(F32) + jnp.stack([got[1], got[0]])


def seq_exchange(blocks, me):
    return xor_order(rel_exchange(xor_order(blocks, me)), me)


def rel_exchange(rel):
    return [
        rel[0],
        lax.ppermute(rel[1], "seq", CORE_SWAP),
        lax.ppermute(rel[2], "seq", CHIP_SWAP),
        lax.ppermute(rel[3], "seq", DIAG_SWAP),
    ]


def tied(*values):
    return lax.optimization_barrier(values)


class Ring:
    def __init__(self, size):
        self.size = size
        half = size // 2
        walk = [2 * i for i in range(half)] + [2 * i + 1 for i in range(half)][::-1]
        self.ahead = [(walk[i], walk[(i + 1) % size]) for i in range(size)]
        self.back = [(b, a) for a, b in self.ahead]
        index = lax.axis_index("dp")
        self.place = jnp.where(index % 2 == 0, index // 2, size - 1 - index // 2)

    def member(self, step):
        place = (self.place + step + self.size) % self.size
        return jnp.where(place < self.size // 2, 2 * place, 2 * (self.size - 1 - place) + 1)

    def gather_attn(self, chunk):
        return GatherAttn(self, chunk)

    def gather_two(self, first, second):
        return GatherTwo(self, first, second)

    def reduce(self, *parts, cut=None):
        return Reduce(self, parts, cut)


class Steps:
    def step(self, count=1):
        for _ in range(count):
            self.done += 1
            self.move(self.done)

    def tie(self, value):
        value, self.flight = tied(value, self.flight)
        return value

    def finish(self):
        self.step(self.ring.size // 2 - self.done)
        return self.result()


def quick(body, outs, ins, smem=0, scratch=(), mib=MIB):
    spec = lambda space: pl.BlockSpec(memory_space=space)
    return pl.pallas_call(
        body,
        out_shape=[jax.ShapeDtypeStruct(shape, kind) for shape, kind in outs],
        in_specs=[spec(pltpu.SMEM if i < smem else pltpu.VMEM) for i in range(len(ins))],
        out_specs=[spec(pltpu.VMEM)] * len(outs),
        scratch_shapes=list(scratch),
        compiler_params=pltpu.CompilerParams(vmem_limit_bytes=mib * 2**20),
        cost_estimate=pl.CostEstimate(flops=1000, bytes_accessed=1000, transcendentals=0),
    )(*ins)


def place_two(ids, chunks, halves, size):
    last = len(chunks)

    def kernel(ids_ref, *refs):
        sources, outs = refs[: last + 2], refs[last + 2 :]
        for k in range(last):
            for half in range(2):
                outs[half][ids_ref[k]] = sources[k][half]
        for half in range(2):
            outs[half][ids_ref[last]] = sources[last + half][...]

    outs = [((size,) + halves[0].shape, halves[0].dtype)] * 2
    return quick(kernel, outs, [ids, *chunks, *halves], smem=1)


HEAD = 16


def place_attn(ids, chunks, halves, size, cut):
    last = len(chunks)
    rows, cols = chunks[0].shape[0] - HEAD, D // 4

    def kernel(ids_ref, *refs):
        sources, (qkv, small, *sends, out) = refs[: last + 2], refs[last + 2 :]

        def put(place, lo, hi, part, head):
            qkv[place, lo:hi] = part[head:, : 3 * SPAN]
            at = pl.multiple_of(place * rows + lo, 8)
            out[pl.ds(at, hi - lo), :] = part[head:, 3 * SPAN :].astype(F32)

        for k in range(last):
            put(ids_ref[k], 0, rows, sources[k], HEAD)
            small[ids_ref[k]] = sources[k][:HEAD, :]
        place = ids_ref[last]
        put(place, 0, cut - HEAD, sources[last], HEAD)
        put(place, cut - HEAD, rows, sources[last + 1], 0)
        small[place] = sources[last][:HEAD, :]
        for m in range(4):

            @pl.when(ids_ref[last + 1] == m)
            def _():
                for r in range(4):
                    first = STARTS[m ^ r] * HD
                    sends[r][...] = out[first : first + SPAN, :].astype(BF16)

    outs = [((size, rows, 3 * SPAN), BF16), ((size, HEAD, chunks[0].shape[1]), BF16)]
    outs += [((SPAN, cols), BF16)] * 4
    scratch = [pltpu.VMEM((D, cols), F32)]
    got = quick(kernel, outs, [ids, *chunks, *halves], smem=1, scratch=scratch)
    return got[0], got[1], got[2:]


def cut_halves(ahead, back, cut):
    def kernel(ahead_ref, back_ref, first_ref, second_ref):
        if cut is None:
            first_ref[...], second_ref[...] = ahead_ref[0], back_ref[1]
        else:
            first_ref[...], second_ref[...] = ahead_ref[:cut, :], back_ref[cut:, :]

    rows, cols = ahead.shape[-2:]
    shapes = [(rows, cols)] * 2 if cut is None else [(cut, cols), (rows - cut, cols)]
    return quick(kernel, [(shape, BF16) for shape in shapes], [ahead, back])


def dot(left, right, left_dim, right_dim):
    return lax.dot_general(
        left, right, (((left_dim,), (right_dim,)), ((), ())), preferred_element_type=F32
    )


def qkv_kernel(unit, gain, shift, weight, bias):
    rows = unit.shape[0]

    def kernel(unit_ref, gain_ref, shift_ref, weight_ref, bias_ref, a_ref, qkv_ref):
        for at in range(0, rows, 128):
            part = slice(at, at + 128)
            a = (unit_ref[part, :] * gain_ref[...] + shift_ref[...]).astype(BF16)
            a_ref[part, :] = a
            qkv_ref[part, :] = (dot(a, weight_ref[...], 1, 0) + bias_ref[...]).astype(BF16)

    outs = [((rows, D), BF16), ((rows, 3 * SPAN), BF16)]
    row = lambda v: v.reshape(1, -1)
    return quick(kernel, outs, [unit, row(gain), row(shift), weight, row(bias)])


def put_rows(ref, at, rows):
    ref[at, :, :D] = rows
    ref[at, :, D:] = jnp.zeros((rows.shape[0], LANES - D), rows.dtype)


def put_block(block, product, send_ref, keep_ref):
    if block % 2 == 1:
        put_rows(send_ref, block // 2, product.astype(BF16))
    else:
        keep_ref[block // 2] = product


def halves(slots):
    return [((2, slots, LANES), BF16), ((2, slots, D), F32)]


def project(me, context, pieces):
    rows, cols = context.shape[0], D // 4
    slots = rows // 4

    def kernel(me_ref, context_ref, *refs):
        sources, (w_ref, send_ref, keep_ref) = refs[:4], refs[4:]
        for m in range(4):

            @pl.when(me_ref[0] == m)
            def _():
                for r in range(4):
                    w_ref[:, (m ^ r) * cols : ((m ^ r) + 1) * cols] = sources[r][...]
                if m > 0:
                    head = 0 if m == 3 else WINDOW - 1
                    w_ref[head * HD : (head + 1) * HD, :] = jnp.zeros((HD, D), BF16)

        for block in range(4):
            part = context_ref[block * slots : (block + 1) * slots, :]
            put_block(block, dot(part, w_ref[...], 1, 0), send_ref, keep_ref)

    ins = [me.reshape(1).astype(jnp.int32), context, *pieces]
    return quick(kernel, [((SPAN, D), BF16)] + halves(slots), ins, smem=1)


def attention(qkv, positions):
    rows = qkv.shape[0]
    slots = rows // 4

    def kernel(qkv_ref, col_ref, row_ref, context_ref, log_ref):
        for block in range(4):
            part = slice(block * slots, (block + 1) * slots)
            mask = col_ref[part, :] >= row_ref[...]
            heads = []
            for h in range(WINDOW):
                lo, hi = h * HD, (h + 1) * HD
                queries = qkv_ref[part, lo:hi]
                keys = qkv_ref[:, SPAN + lo : SPAN + hi]
                values = qkv_ref[:, 2 * SPAN + lo : 2 * SPAN + hi]
                scores = jnp.where(mask, dot(queries, keys, 1, 1) * 0.125, -1e30)
                peak = jnp.max(scores, axis=1, keepdims=True)
                exps = jnp.exp(scores - peak)
                total = jnp.sum(exps, axis=1, keepdims=True)
                heads.append(dot((exps * (1.0 / total)).astype(BF16), values, 1, 0))
                log_ref[part, h : h + 1] = peak + jnp.log(total)
            context_ref[part, :] = jnp.concatenate(heads, axis=1).astype(BF16)

    outs = [((rows, SPAN), BF16), ((rows, 8), F32)]
    return quick(kernel, outs, [qkv, positions.reshape(-1, 1), positions.reshape(1, -1)])


def widened(rows):
    return jnp.pad(rows, ((0, 0), (0, LANES - D)))


def row(vector):
    return vector.reshape(1, -1)


def norm(values):
    mean = jnp.mean(values, axis=-1, keepdims=True)
    centred = values - mean
    scale = lax.rsqrt(jnp.mean(centred * centred, axis=-1, keepdims=True) + 1e-05)
    return centred * scale, scale


def first_norm(own, other, across):
    slots = own.shape[0]

    def kernel(own_ref, other_ref, across_ref, unit_ref):
        for block, part in enumerate((own_ref, across_ref.at[0], other_ref, across_ref.at[1])):
            unit_ref[block * slots : (block + 1) * slots, :] = norm(part[:, :D].astype(F32))[0]

    return quick(kernel, [((4 * slots, D), F32)], [own, other, across])[0]


def join_blocks(own, other, across):
    slots = own.shape[0]

    def kernel(own_ref, other_ref, across_ref, out_ref):
        for block, part in enumerate((own_ref, across_ref.at[0], other_ref, across_ref.at[1])):
            out_ref[block * slots : (block + 1) * slots, :] = part[:, :D]

    return quick(kernel, [((4 * slots, D), own.dtype)], [own, other, across])[0]


def pair_sum(keep, across):
    def kernel(keep_ref, across_ref, out_ref):
        for i in range(2):
            put_rows(out_ref, i, (keep_ref[i] + across_ref[i, :, :D].astype(F32)).astype(BF16))

    return quick(kernel, [(across.shape, BF16)], [keep, across])[0]


def second_norm(pair, got, own, other, out_bias, gain, shift):
    slots = own.shape[0]

    def kernel(
        pair_ref, got_ref, own_ref, other_ref, bias_ref, gain_ref, shift_ref,
        residual_ref, unit_ref, scale_ref, a_ref,
    ):
        for i, part in enumerate((own_ref, other_ref)):
            attn = pair_ref[i, :, :D].astype(F32) + got_ref[1 - i, :, :D].astype(F32)
            residual = part[:, :D].astype(F32) + attn + bias_ref[...]
            if i == 0:
                residual_ref[...] = residual
            unit, scale = norm(residual)
            unit_ref[i] = unit
            scale_ref[i] = scale
            put_rows(a_ref, i, (unit * gain_ref[...] + shift_ref[...]).astype(BF16))

    two = (2, slots, D)
    outs = [((slots, D), F32), (two, F32), ((2, slots, 1), F32), (pair.shape, BF16)]
    return quick(
        kernel, outs, [pair, got, own, other, row(out_bias), row(gain), row(shift)]
    )


def mlp_up(pair, across, weight, bias):
    slots = pair.shape[1]

    def kernel(pair_ref, across_ref, weight_ref, bias_ref, all_ref, act_ref, slope_ref):
        for block in range(4):
            part = slice(block * slots, (block + 1) * slots)
            rows = (across_ref if block % 2 else pair_ref)[block // 2, :, :D]
            all_ref[part, :] = rows
            pre = dot(rows, weight_ref[...], 1, 0) + bias_ref[...]
            below = 0.5 * (1.0 + lax.erf(pre * 0.7071067811865476))
            act_ref[part, :] = (pre * below).astype(BF16)
            slope_ref[part, :] = below + pre * jnp.exp(-0.5 * pre * pre) * 0.3989422804014327

    shape = (4 * slots, D)
    outs = [(shape, BF16), (shape, BF16), (shape, F32)]
    return quick(kernel, outs, [pair, across, weight, row(bias)])


def mlp_down_back(grads, w_down, slope, w_up):
    rows = grads.shape[0]
    slots = rows // 4

    def kernel(
        grad_ref, down_ref, slope_ref, up_ref, low_ref, send_ref, keep_ref, sums_ref
    ):
        sums = jnp.zeros((1, D), F32)
        for block in range(4):
            part = slice(block * slots, (block + 1) * slots)
            pre = dot(grad_ref[part, :], down_ref[...], 1, 1) * slope_ref[part, :]
            low = pre.astype(BF16)
            low_ref[part, :] = low
            sums += jnp.sum(low.astype(F32), axis=0, keepdims=True)
            put_block(block, dot(low, up_ref[...], 1, 1), send_ref, keep_ref)
        sums_ref[...] = sums

    outs = [((rows, D), BF16)] + halves(slots) + [((1, D), F32)]
    return quick(kernel, outs, [grads, w_down, slope, w_up])


def norm_pull(unit, scale, gain, grad):
    lifted = grad * gain
    return scale * (
        lifted
        - jnp.mean(lifted, axis=-1, keepdims=True)
        - unit * jnp.mean(lifted * unit, axis=-1, keepdims=True)
    )


def second_norm_back(pair, got, unit, scale, gain, own_grad, other_grad):
    slots = own_grad.shape[0]

    def kernel(
        pair_ref, got_ref, unit_ref, scale_ref, gain_ref, own_ref, other_ref,
        resid_ref, low_ref, sums_ref,
    ):
        for i, part in enumerate((own_ref, other_ref)):
            grad = pair_ref[i, :, :D].astype(F32) + got_ref[1 - i, :, :D].astype(F32)
            back = norm_pull(unit_ref[i], scale_ref[i], gain_ref[...], grad)
            resid = part[:, :D].astype(F32) + back
            low = resid.astype(BF16)
            put_rows(low_ref, i, low)
            if i == 0:
                resid_ref[...] = resid
                sums_ref[0:1, :] = jnp.sum(grad * unit_ref[i], axis=0, keepdims=True)
                sums_ref[1:2, :] = jnp.sum(grad, axis=0, keepdims=True)
                sums_ref[2:3, :] = jnp.sum(low.astype(F32), axis=0, keepdims=True)
                sums_ref[3:4, :] = jnp.sum(part[...].astype(F32), axis=0, keepdims=True)

    outs = [((slots, D), F32), (pair.shape, BF16), ((8, D), F32)]
    return quick(kernel, outs, [pair, got, unit, scale, row(gain), own_grad, other_grad])


def first_norm_back(low, w_qkv, unit):
    rows = low.shape[0]
    slots = rows // 4

    def kernel(low_ref, w_ref, unit_ref, send_ref, keep_ref, sums_ref, bias_ref):
        gain = jnp.zeros((1, D), F32)
        shift = jnp.zeros((1, D), F32)
        bias = jnp.zeros((1, 3 * SPAN), F32)
        for block in range(4):
            part = slice(block * slots, (block + 1) * slots)
            low = low_ref[part, :]
            back = dot(low, w_ref[...], 1, 1)
            gain += jnp.sum(back * unit_ref[part, :], axis=0, keepdims=True)
            shift += jnp.sum(back, axis=0, keepdims=True)
            bias += jnp.sum(low.astype(F32), axis=0, keepdims=True)
            put_block(block, back, send_ref, keep_ref)
        sums_ref[0:1, :] = gain
        sums_ref[1:2, :] = shift
        bias_ref[...] = bias

    outs = halves(slots) + [((8, D), F32), ((1, 3 * SPAN), F32)]
    return quick(kernel, outs, [low, w_qkv, unit])


def attn_parts(a_one, low, out_back, small):
    count, rows = out_back.shape[0], D // out_back.shape[0]
    wide = 3 * SPAN + D // 4

    def kernel(a_ref, low_ref, out_ref, small_ref, parts_ref, total_ref):
        total_ref[...] = dot(a_ref[...], low_ref[...], 0, 0)
        for k in range(count):
            piece = total_ref[k * rows : (k + 1) * rows, :].astype(BF16)
            parts_ref[k, HEAD:, : 3 * SPAN] = piece
            parts_ref[k, HEAD:, 3 * SPAN :] = out_ref[k]
            parts_ref[k, :HEAD, :] = small_ref[k]

    scratch = [pltpu.VMEM((D, 3 * SPAN), F32)]
    outs = [((count, HEAD + rows, wide), BF16)]
    return quick(kernel, outs, [a_one, low, out_back, small], scratch=scratch)[0]


def core_sums(keep, across):
    def kernel(keep_ref, across_ref, near_ref, far_ref):
        near_ref[...] = keep_ref[0] + across_ref[0, :, :D].astype(F32)
        put_rows(far_ref, 0, (keep_ref[1] + across_ref[1, :, :D].astype(F32)).astype(BF16))

    outs = [(keep.shape[1:], F32), ((1,) + across.shape[1:], BF16)]
    return quick(kernel, outs, [keep, across])


def input_back(own, gain, near, got, resid):
    def kernel(own_ref, gain_ref, near_ref, got_ref, resid_ref, out_ref):
        unit, scale = norm(own_ref[...].astype(F32))
        grad = near_ref[...] + got_ref[0, :, :D].astype(F32)
        back = norm_pull(unit, scale, gain_ref[...], grad)
        out_ref[...] = (resid_ref[...] + back).astype(BF16)

    return quick(kernel, [(own.shape, BF16)], [own, row(gain), near, got, resid])[0]


def out_gradient(me, context, pair, across):
    slots, cols = pair.shape[1], D // 4

    def kernel(me_ref, context_ref, pair_ref, across_ref, *outs):
        total = jnp.zeros((SPAN, D), F32)
        for block in range(4):
            part = slice(block * slots, (block + 1) * slots)
            rows = (across_ref if block % 2 else pair_ref)[block // 2, :, :D]
            total += dot(context_ref[part, :], rows, 0, 0)
        low = total.astype(BF16)
        for m in range(4):

            @pl.when(me_ref[0] == m)
            def _():
                for r in range(4):
                    outs[r][...] = low[:, (m ^ r) * cols : ((m ^ r) + 1) * cols]

    ins = [me.reshape(1).astype(jnp.int32), context, pair, across]
    return quick(kernel, [((SPAN, cols), BF16)] * 4, ins, smem=1)


def attention_back(qkv, pair, across, w_out, logs, positions):
    rows = qkv.shape[0]
    slots = rows // 4

    def kernel(
        qkv_ref, pair_ref, across_ref, w_ref, log_ref, col_ref, row_ref, low_ref,
        keys_acc, values_acc,
    ):
        for block in range(4):
            part = slice(block * slots, (block + 1) * slots)
            mask = col_ref[part, :] >= row_ref[...]
            resid = (across_ref if block % 2 else pair_ref)[block // 2, :, :D]
            grads = dot(resid, w_ref[...], 1, 1).astype(BF16)
            heads = []
            for h in range(WINDOW):
                lo, hi = h * HD, (h + 1) * HD
                queries = qkv_ref[part, lo:hi]
                keys = qkv_ref[:, SPAN + lo : SPAN + hi]
                values = qkv_ref[:, 2 * SPAN + lo : 2 * SPAN + hi]
                grad = grads[:, lo:hi]
                scores = jnp.where(mask, dot(queries, keys, 1, 1) * 0.125, -1e30)
                probs = jnp.exp(scores - log_ref[part, h : h + 1])
                prob_grad = dot(grad, values, 1, 1)
                inner = jnp.sum(probs * prob_grad, axis=1, keepdims=True)
                score_low = (probs * (prob_grad - inner)).astype(BF16)
                heads.append(dot(score_low, keys, 1, 0) * 0.125)
                keys_grad = dot(score_low, queries, 0, 0) * 0.125
                values_grad = dot(probs.astype(BF16), grad, 0, 0)
                if block == 0:
                    keys_acc[h] = keys_grad
                    values_acc[h] = values_grad
                else:
                    keys_acc[h] += keys_grad
                    values_acc[h] += values_grad
            low_ref[part, :SPAN] = jnp.concatenate(heads, axis=1).astype(BF16)
        for i, acc in enumerate((keys_acc, values_acc)):
            joined = jnp.concatenate([acc[h] for h in range(WINDOW)], axis=1)
            low_ref[:, (i + 1) * SPAN : (i + 2) * SPAN] = joined.astype(BF16)

    scratch = [pltpu.VMEM((WINDOW, rows, HD), F32)] * 2
    ins = [qkv, pair, across, w_out, logs, positions.reshape(-1, 1), positions.reshape(1, -1)]
    return quick(kernel, [((rows, 3 * SPAN), BF16)], ins, scratch=scratch)[0]


def ring_add(ids, parts, flight, cut=None):
    count = len(parts)
    rows, cols = parts[0].shape[1:]
    half = flight[0].shape != (count, rows, cols)

    def kernel(ids_ref, *refs):
        ahead, back = refs[2 * count], refs[2 * count + 1]
        out_ahead, out_back = refs[2 * count + 2], refs[2 * count + 3]
        total = lambda a, b: (a.astype(F32) + b.astype(F32)).astype(BF16)
        mine = [refs[i][0] for i in range(2 * count)]
        if half and count == 2:
            out_ahead[0], out_ahead[1] = total(mine[0], ahead[...]), mine[1]
            out_back[0], out_back[1] = mine[2], total(mine[3], back[...])
        elif half:
            out_ahead[0, :cut] = total(mine[0][:cut], ahead[...])
            out_ahead[0, cut:] = mine[0][cut:]
            out_back[0, :cut] = mine[1][:cut]
            out_back[0, cut:] = total(mine[1][cut:], back[...])
        else:
            for i in range(count):
                out_ahead[i] = total(mine[i], ahead[i])
                out_back[i] = total(mine[count + i], back[i])

    pick = lambda n: pl.BlockSpec((1, rows, cols), lambda i, ids, n=n: (ids[n], 0, 0))
    whole = lambda v: pl.BlockSpec(v.shape, lambda i, ids, v=v: (0,) * v.ndim)
    out = jax.ShapeDtypeStruct((count, rows, cols), BF16)
    return pl.pallas_call(
        kernel,
        out_shape=[out] * 2,
        grid_spec=pltpu.PrefetchScalarGridSpec(
            num_scalar_prefetch=1,
            grid=(1,),
            in_specs=[pick(0)] * count + [pick(1)] * count + [whole(f) for f in flight],
            out_specs=[whole(out)] * 2,
        ),
        compiler_params=pltpu.CompilerParams(vmem_limit_bytes=MIB * 2**20),
        cost_estimate=pl.CostEstimate(flops=1000, bytes_accessed=1000, transcendentals=0),
    )(ids, *parts, *parts, *flight)


def ring_far(ids, parts, cut=None):
    rows, cols = parts[0].shape[1:]
    sizes = [rows] * 2 if cut is None else [cut, rows - cut]

    def kernel(ids_ref, *refs):
        outs = refs[len(parts) :]
        if cut is None:
            outs[0][...], outs[1][...] = refs[0][0], refs[1][0]
        else:
            outs[0][...], outs[1][...] = refs[0][0, :cut, :], refs[0][0, cut:, :]

    pick = pl.BlockSpec((1, rows, cols), lambda i, ids: (ids[0], 0, 0))
    return pl.pallas_call(
        kernel,
        out_shape=[jax.ShapeDtypeStruct((n, cols), BF16) for n in sizes],
        grid_spec=pltpu.PrefetchScalarGridSpec(
            num_scalar_prefetch=1,
            grid=(1,),
            in_specs=[pick] * len(parts),
            out_specs=[pl.BlockSpec((n, cols), lambda i, ids: (0, 0)) for n in sizes],
        ),
        compiler_params=pltpu.CompilerParams(vmem_limit_bytes=MIB * 2**20),
        cost_estimate=pl.CostEstimate(flops=1000, bytes_accessed=1000, transcendentals=0),
    )(ids, *parts)


def ring_total(ids, parts, flight):
    count = len(parts)
    rows, cols = parts[0].shape[1:]

    def kernel(ids_ref, *refs):
        for i in range(count):
            mine = refs[i][0].astype(F32) + refs[count][i].astype(F32)
            refs[count + 2 + i][...] = mine + refs[count + 1][i].astype(F32)

    pick = pl.BlockSpec((1, rows, cols), lambda i, ids: (ids[0], 0, 0))
    whole = pl.BlockSpec((count, rows, cols), lambda i, ids: (0, 0, 0))
    return pl.pallas_call(
        kernel,
        out_shape=[jax.ShapeDtypeStruct((rows, cols), F32)] * count,
        grid_spec=pltpu.PrefetchScalarGridSpec(
            num_scalar_prefetch=1,
            grid=(1,),
            in_specs=[pick] * count + [whole] * 2,
            out_specs=[pl.BlockSpec((rows, cols), lambda i, ids: (0, 0))] * count,
        ),
        compiler_params=pltpu.CompilerParams(vmem_limit_bytes=MIB * 2**20),
        cost_estimate=pl.CostEstimate(flops=1000, bytes_accessed=1000, transcendentals=0),
    )(ids, *parts, *flight)


def split_units(me, rows, dp_count):
    width = FF // dp_count // 4

    def kernel(me_ref, rows_ref, *outs):
        value = rows_ref[...]
        cut = lambda d, s: value[:, (4 * d + s) * width : (4 * d + s + 1) * width]
        four = [jnp.concatenate([cut(d, s) for d in range(dp_count)], axis=1) for s in range(4)]
        for m in range(4):

            @pl.when(me_ref[0] == m)
            def _():
                for r in range(4):
                    outs[r][...] = four[m ^ r]

    outs = [((rows.shape[0], D), BF16)] * 4
    return quick(kernel, outs, [me.reshape(1).astype(jnp.int32), rows], smem=1)


def join_units(four):
    rows = four[0].shape[0]
    blocks = FF // 128

    def kernel(*refs):
        parts, out_ref = [r[...].astype(F32) for r in refs[:4]], refs[4]
        width = 136
        pieces = []
        for d in range(D // width):
            pieces += [p[:, d * width : (d + 1) * width] for p in parts]
        joined = jnp.concatenate(pieces, axis=1)
        for t in range(blocks):
            out_ref[pl.ds(t, rows, stride=blocks), :] = joined[:, t * 128 : (t + 1) * 128]

    out = quick(kernel, [((rows * blocks, 128), F32)], four)[0]
    return out.reshape(-1)


class GatherAttn(Steps):
    def __init__(self, ring, chunk):
        self.ring, self.done = ring, 0
        self.flight = (chunk, chunk)
        self.chunks, self.order = [chunk], [0]
        self.cut = 80

    def move(self, step):
        ring, (ahead, back) = self.ring, self.flight
        last = step == ring.size // 2
        if last:
            ahead, back = cut_halves(ahead, back, self.cut)
        ahead = lax.ppermute(ahead, "dp", ring.ahead)
        back = lax.ppermute(back, "dp", ring.back)
        self.flight = (ahead, back)
        if not last:
            self.chunks += [ahead, back]
            self.order += [-step, step]

    def result(self):
        ids = [self.ring.member(k) for k in self.order + [self.ring.size // 2]]
        ids = jnp.stack(ids + [lax.axis_index("seq")])
        return place_attn(ids.astype(jnp.int32), self.chunks, self.flight, self.ring.size, self.cut)


class GatherTwo(Steps):
    def __init__(self, ring, first, second):
        self.ring, self.done = ring, 0
        chunk = jnp.stack([first, second])
        self.flight = (chunk, chunk)
        self.chunks, self.order = [chunk], [0]

    def move(self, step):
        ring, (ahead, back) = self.ring, self.flight
        last = step == ring.size // 2
        if last:
            ahead, back = cut_halves(ahead, back, None)
        ahead = lax.ppermute(ahead, "dp", ring.ahead)
        back = lax.ppermute(back, "dp", ring.back)
        self.flight = (ahead, back)
        if not last:
            self.chunks += [ahead, back]
            self.order += [-step, step]

    def result(self):
        ids = jnp.stack([self.ring.member(k) for k in self.order + [self.ring.size // 2]])
        return place_two(ids.astype(jnp.int32), self.chunks, self.flight, self.ring.size)


class Reduce(Steps):
    def __init__(self, ring, parts, cut=None):
        self.ring, self.parts, self.cut, self.done = ring, parts, cut, 0
        self.flight = tuple(ring_far(self.ids(ring.size // 2), parts, cut))

    def ids(self, *steps):
        return jnp.stack([self.ring.member(k) for k in steps]).astype(jnp.int32)

    def move(self, step):
        left = self.ring.size // 2 - step + 1
        ahead, back = self.flight
        if step > 1:
            ahead, back = ring_add(self.ids(left, -left), self.parts, self.flight, self.cut)
        self.flight = (
            lax.ppermute(ahead, "dp", self.ring.ahead),
            lax.ppermute(back, "dp", self.ring.back),
        )

    def result(self):
        return ring_total(self.ids(0), self.parts, self.flight)


class Whole:
    def gather_attn(self, chunk):
        got = lax.all_gather(chunk, "dp", axis=0)
        out = got[:, HEAD:, 3 * SPAN :].reshape(D, D // 4)
        sends = xor_order([out[s * HD : s * HD + SPAN] for s in STARTS], lax.axis_index("seq"))
        return Whole.Ready((got[:, HEAD:, : 3 * SPAN], got[:, :HEAD], sends), chunk)

    def gather_two(self, first, second):
        got = lax.all_gather(jnp.stack([first, second]), "dp", axis=0)
        return Whole.Ready([got[:, 0], got[:, 1]], first)

    def reduce(self, *parts, cut=None):
        got = [lax.psum_scatter(p, "dp", scatter_dimension=0, tiled=True)[0] for p in parts]
        return Whole.Ready([g.astype(F32) for g in got], got[0])

    class Ready(Steps):
        def __init__(self, value, flight):
            self.value, self.flight = value, flight

        def step(self, count=1):
            pass

        def finish(self):
            return self.value


def join_windows(four, axis):
    cut = lambda part, lo, hi: lax.slice_in_dim(part, lo, hi, axis=axis)
    return jnp.concatenate(
        [
            four[0],
            cut(four[1], 0, SPAN - HD),
            cut(four[2], 0, SPAN - HD),
            cut(four[3], HD, SPAN),
        ],
        axis=axis,
    )


def head_cols(rows):
    piece = lambda s, b: rows[:, b * D + s * HD : b * D + s * HD + SPAN]
    return [jnp.concatenate([piece(s, b) for b in range(3)], axis=1) for s in STARTS]


def join_head_cols(four):
    block = lambda b: join_windows([f[:, b * SPAN : (b + 1) * SPAN] for f in four], 1)
    return jnp.concatenate([block(b) for b in range(3)], axis=1)


def own_cols(rows):
    return [rows[:, s * (D // 4) : (s + 1) * (D // 4)] for s in range(4)]


def unit_cols(rows, dp_count):
    four = rows.reshape(rows.shape[0], dp_count, 4, -1)
    return [four[:, :, s].reshape(rows.shape[0], D) for s in range(4)]


def join_unit_cols(four, dp_count):
    if FF // dp_count // 4 == 136:
        return join_units(four)
    parts = [f.reshape(f.shape[0], dp_count, 1, -1) for f in four]
    return jnp.concatenate(parts, axis=2).reshape(four[0].shape[0], FF)


def split_rows(flats, widths, cols_of, me):
    if all(flat.shape[0] % width == 0 for flat, width in zip(flats, widths)):
        rows = [flat.reshape(-1, width) for flat, width in zip(flats, widths)]
        return jnp.concatenate(seq_exchange(cols_of(rows), me))
    rows = [
        lax.all_gather(flat, "seq", axis=0, tiled=True).reshape(-1, width)
        for flat, width in zip(flats, widths)
    ]
    return xor_order(cols_of(rows), me)[0]


def join_rows(rows, shares, widths, join_cols, me):
    low = rows.astype(BF16)
    count = rows.shape[0] // 4
    if all(share % width == 0 for share, width in zip(shares, widths)):
        got = seq_exchange([low[m * count : (m + 1) * count] for m in range(4)], me)
        return [part.astype(F32).reshape(-1) for part in join_cols(got)]
    got = join_cols(list(lax.all_gather(low, "seq", axis=0)))
    return [
        lax.dynamic_slice_in_dim(part.reshape(-1), me * share, share, 0).astype(F32)
        for part, share in zip(got, shares)
    ]


def body(tokens, order, cotangent, qkv_weight, out_weight, up_weight, down_weight, small_params):
    slots = tokens.shape[1]
    dp_count = lax.axis_size("dp")
    me = lax.axis_index("seq")
    units = FF // (dp_count * 4)
    block_rows = D // dp_count
    ring = Ring(dp_count) if dp_count == 8 else Whole()
    start = jnp.where(me == 0, 0, jnp.where(me == 3, 12, 4 * me + 1)) * HD

    small_len = small_params.shape[0]
    wide = 3 * SPAN + D // 4

    blank = jnp.zeros((HEAD - 4, wide), BF16)
    small_row = jnp.pad(small_params.reshape(1, -1), ((0, 0), (0, wide - small_len)))
    attn_cols = lambda r: [
        jnp.concatenate([q, o], axis=1) for q, o in zip(head_cols(r[0]), own_cols(r[1]))
    ]
    if qkv_weight.shape[0] % (3 * D) == 0 and out_weight.shape[0] % D == 0:
        blocks = attn_cols([qkv_weight.reshape(-1, 3 * D), out_weight.reshape(-1, D)])
        share = blocks[0].shape[0]
        got = seq_exchange([jnp.concatenate([block, small_row]) for block in blocks], me)
        attn_chunk = jnp.concatenate([g[share:] for g in got] + [blank] + [g[:share] for g in got])
    else:
        attn_rows = split_rows([qkv_weight, out_weight], [3 * D, D], attn_cols, me)
        small_rows = xor_order(list(seq_gather(small_row)), me)
        attn_chunk = jnp.concatenate(small_rows + [blank, attn_rows])
    attn_chunk, up_flat = tied(attn_chunk, up_weight)
    attn_ring = ring.gather_attn(attn_chunk)
    attn_ring.step()
    if block_rows == 136:
        up_four = split_units(me, up_flat.reshape(-1, FF), dp_count)
        up_rows = jnp.concatenate(xor_order(rel_exchange(up_four), me))
    else:
        up_rows = split_rows([up_flat], [FF], lambda r: unit_cols(r[0], dp_count), me)
    positions = jnp.concatenate(xor_order(order.reshape(4, slots), me))
    positions = attn_ring.tie(positions)
    attn_ring.step()
    own_tokens = tokens.reshape(-1, D)
    other_tokens, across_tokens = seq_blocks(widened(own_tokens))
    unit_one = first_norm(own_tokens, other_tokens, across_tokens)
    unit_one, up_rows = attn_ring.tie((unit_one, up_rows))
    own_grad = attn_ring.tie(cotangent.reshape(-1, D))
    attn_ring.step()
    mlp_rows = attn_ring.tie((up_rows, down_weight.reshape(-1, D)))
    mlp_ring = ring.gather_two(*mlp_rows)
    other_grad, across_grad = seq_blocks(widened(own_grad))
    grad_all = join_blocks(own_grad, other_grad, across_grad)
    w_qkv, small_all, out_sends = attn_ring.finish()
    mlp_ring.step()
    w_qkv = w_qkv.reshape(D, 3 * SPAN)
    small_full = small_all[:, :4, :small_len].reshape(-1).astype(F32)
    out_pieces = rel_exchange(out_sends)

    at = lambda i: small_full[i * D : (i + 1) * D]
    ln1_gain, ln1_bias, q_bias, v_bias, out_bias, ln2_gain, ln2_bias = [at(i) for i in range(7)]
    up_bias = small_full[7 * D : 7 * D + FF]
    down_bias = small_full[7 * D + FF : 8 * D + FF]

    window = lambda v: lax.dynamic_slice_in_dim(v, start, SPAN, 0)
    bias_qkv = jnp.concatenate([window(q_bias), jnp.zeros((SPAN,), F32), window(v_bias)])
    a_one, qkv_vals = qkv_kernel(unit_one, ln1_gain, ln1_bias, w_qkv, bias_qkv)
    a_one, qkv_vals = mlp_ring.tie((a_one, qkv_vals))
    mlp_ring.step()
    context, logs = mlp_ring.tie(attention(qkv_vals, positions))
    mlp_ring.step()
    w_out, send, keep = project(me, context, out_pieces)
    across = lax.ppermute(send, "seq", CORE_SWAP)
    pair, grad_all = tied(pair_sum(keep, across), grad_all)
    got = mlp_ring.tie(lax.ppermute(pair, "seq", CHIP_SWAP))
    w_up, w_down = (w.reshape(D, D) for w in mlp_ring.finish())
    residual, unit_two, scale_two, a_two = second_norm(
        pair, got, own_tokens, other_tokens, out_bias, ln2_gain, ln2_bias
    )
    a_across = lax.ppermute(a_two, "seq", CORE_SWAP)
    up_bias_own = lax.dynamic_index_in_dim(
        up_bias.reshape(dp_count, 4, units), me, 1, False
    ).reshape(-1)
    a_two_all, act_low, slope = mlp_up(a_two, a_across, w_up, up_bias_own)

    pre_low, send, keep, bias_cols = mlp_down_back(grad_all, w_down, slope, w_up)
    across = lax.ppermute(send, "seq", CORE_SWAP)
    down_grad = inner_rows(act_low, grad_all).astype(BF16)
    up_grad = inner_rows(a_two_all, pre_low).astype(BF16)
    pair, up_grad, down_grad = tied(pair_sum(keep, across), up_grad, down_grad)
    mlp_back = ring.reduce(
        down_grad.reshape(dp_count, units, D), up_grad.reshape(dp_count, block_rows, D)
    )
    mlp_back.step()
    got = mlp_back.tie(lax.ppermute(pair, "seq", CHIP_SWAP))
    mlp_back.step()
    resid, resid_low, sums_two = second_norm_back(
        pair, got, unit_two, scale_two, ln2_gain, own_grad, other_grad
    )

    resid_across = lax.ppermute(resid_low, "seq", CORE_SWAP)
    out_four = out_gradient(me, context, resid_low, resid_across)
    out_four, resid_low, resid_across = mlp_back.tie((out_four, resid_low, resid_across))
    mlp_back.step()
    out_back = join_windows(xor_order(rel_exchange(out_four), me), 0)
    qkv_low = attention_back(qkv_vals, resid_low, resid_across, w_out, logs, positions)
    qkv_low = mlp_back.tie(qkv_low)
    mlp_back.step()
    send, keep, sums_one, bias_sums = first_norm_back(qkv_low, w_qkv, unit_one)
    bias_sums = bias_sums.reshape(-1)
    placed = lambda v: lax.dynamic_update_slice(jnp.zeros((D,), F32), v, (start,))
    q_bias_grad = placed(bias_sums[:SPAN])
    v_bias_grad = placed(bias_sums[2 * SPAN :])

    up_bias_grad = lax.dynamic_update_slice(
        jnp.zeros((dp_count, 4, units), F32), bias_cols.reshape(dp_count, 1, units), (0, me, 0)
    ).reshape(-1)
    small_grad = jnp.concatenate(
        [
            sums_one[0],
            sums_one[1],
            q_bias_grad,
            v_bias_grad,
            sums_two[2],
            sums_two[0],
            sums_two[1],
            up_bias_grad,
            sums_two[3],
            jnp.zeros((small_full.shape[0] - 8 * D - FF,), F32),
        ]
    ).astype(BF16)
    small_grad = jnp.pad(
        small_grad.reshape(dp_count, 4, small_len), ((0, 0), (0, HEAD - 4), (0, wide - small_len))
    )
    out_back = out_back.reshape(dp_count, block_rows, D // 4)
    if block_rows == 136:
        parts = attn_parts(a_one, qkv_low, out_back, small_grad)
    else:
        qkv_grad = inner_rows(a_one, qkv_low).astype(BF16)
        parts = jnp.concatenate([qkv_grad.reshape(dp_count, block_rows, -1), out_back], axis=2)
        parts = jnp.concatenate([small_grad, parts], axis=1)
    attn_back = ring.reduce(parts, cut=80)
    attn_back.step()
    down_sum, up_sum = mlp_back.finish()
    down_sum, up_sum, send, keep, act_low = attn_back.tie(
        (down_sum, up_sum, send, keep, act_low)
    )
    attn_back.step()
    near, far = core_sums(keep, lax.ppermute(send, "seq", CORE_SWAP))
    got = lax.ppermute(far, "seq", CHIP_SWAP)
    input_grad = input_back(own_tokens, ln1_gain, near, got, resid).reshape(tokens.shape)
    (up_part,) = join_rows(
        up_sum, [up_weight.shape[0]], [FF], lambda four: (join_unit_cols(four, dp_count),), me
    )
    (attn_sum,) = attn_back.finish()
    small_got = seq_exchange(
        [attn_sum[m : m + 1, :small_len].astype(BF16) for m in range(4)],
        me,
    )
    small_part = sum(g.astype(F32) for g in small_got).reshape(-1)
    qkv_part, out_part = join_rows(
        attn_sum[HEAD:],
        [qkv_weight.shape[0], out_weight.shape[0]],
        [3 * D, D],
        lambda four: (
            join_head_cols([f[:, : 3 * SPAN] for f in four]),
            jnp.concatenate([f[:, 3 * SPAN :] for f in four], axis=1),
        ),
        me,
    )

    down_part = down_sum.reshape(-1)
    mlp_abs = jnp.concatenate(xor_order(mm(act_low, w_down).astype(BF16).reshape(4, slots, D), me))
    mlp_out = lax.psum_scatter(mlp_abs, "seq", scatter_dimension=0, tiled=True).astype(F32)
    mixed = (residual + mlp_out + down_bias).astype(BF16).reshape(tokens.shape)
    return (mixed, input_grad, qkv_part, out_part, up_part, down_part, small_part)


def solution(mesh):
    rows, flat = P("dp", "seq", None), P(("dp", "seq"))
    return jax.shard_map(
        body,
        mesh=mesh,
        in_specs=(rows, P("dp", None), rows, flat, flat, flat, flat, flat),
        out_specs=(rows, rows, flat, flat, flat, flat, flat),
        check_vma=False,
    )
```

```python
import jax
import jax.numpy as jnp
from jax import lax
from jax.experimental import pallas as pl
from jax.experimental.pallas import tpu as pltpu
from jax.sharding import PartitionSpec as P

D = 1088
FF = 4352
LANES = 1152
MIB = 16
HD = 64
HEADS = D // HD
LEN = 512
F32 = jnp.float32
BF16 = jnp.bfloat16

STARTS = (0, 5, 9, 12)
WINDOW = 5
SPAN = WINDOW * HD

CORE_SWAP = [(0, 1), (1, 0), (2, 3), (3, 2)]
CHIP_SWAP = [(0, 2), (2, 0), (1, 3), (3, 1)]
DIAG_SWAP = [(0, 3), (3, 0), (1, 2), (2, 1)]


def mm(left, right):
    return jnp.dot(left, right, preferred_element_type=F32)


def inner_rows(left, right):
    return lax.dot_general(left, right, (((0,), (0,)), ((), ())), preferred_element_type=F32)


def times_transposed(left, right):
    return lax.dot_general(left, right, (((1,), (1,)), ((), ())), preferred_element_type=F32)


def xor_order(four, me):
    core, chip = me % 2 == 1, me // 2 == 1
    a = [four[0], four[1], four[2], four[3]]
    a = [jnp.where(core, a[i ^ 1], a[i]) for i in range(4)]
    return [jnp.where(chip, a[i ^ 2], a[i]) for i in range(4)]


def seq_blocks(rows):
    other = lax.ppermute(rows, "seq", CHIP_SWAP)
    return other, lax.ppermute(jnp.stack([rows, other]), "seq", CORE_SWAP)


def seq_gather(rows):
    other, across = seq_blocks(rows)
    return jnp.stack([rows, across[0], other, across[1]])


def core_gather(pair):
    across = lax.ppermute(pair, "seq", CORE_SWAP)
    return jnp.stack([pair[0], across[0], pair[1], across[1]])


def core_reduce(blocks):
    low = blocks.astype(BF16)
    across = lax.ppermute(jnp.stack([low[1], low[3]]), "seq", CORE_SWAP).astype(F32)
    return blocks[0] + across[0], blocks[2] + across[1]


def seq_reduce(blocks):
    near, far = core_reduce(blocks)
    return near + lax.ppermute(far.astype(BF16), "seq", CHIP_SWAP).astype(F32)


def pair_reduce(blocks):
    near, far = core_reduce(blocks)
    pair = jnp.stack([near, far]).astype(BF16)
    got = lax.ppermute(pair, "seq", CHIP_SWAP).astype(F32)
    return pair.astype(F32) + jnp.stack([got[1], got[0]])


def seq_exchange(blocks, me):
    return xor_order(rel_exchange(xor_order(blocks, me)), me)


def rel_exchange(rel):
    return [
        rel[0],
        lax.ppermute(rel[1], "seq", CORE_SWAP),
        lax.ppermute(rel[2], "seq", CHIP_SWAP),
        lax.ppermute(rel[3], "seq", DIAG_SWAP),
    ]


def tied(*values):
    return lax.optimization_barrier(values)


class Ring:
    def __init__(self, size):
        self.size = size
        half = size // 2
        walk = [2 * i for i in range(half)] + [2 * i + 1 for i in range(half)][::-1]
        self.ahead = [(walk[i], walk[(i + 1) % size]) for i in range(size)]
        self.back = [(b, a) for a, b in self.ahead]
        index = lax.axis_index("dp")
        self.place = jnp.where(index % 2 == 0, index // 2, size - 1 - index // 2)

    def member(self, step):
        place = (self.place + step + self.size) % self.size
        return jnp.where(place < self.size // 2, 2 * place, 2 * (self.size - 1 - place) + 1)

    def gather_attn(self, chunk):
        return GatherAttn(self, chunk)

    def gather_two(self, first, second):
        return GatherTwo(self, first, second)

    def reduce(self, *parts, cut=None):
        return Reduce(self, parts, cut)


class Steps:
    def step(self, count=1):
        for _ in range(count):
            self.done += 1
            self.move(self.done)

    def tie(self, value):
        value, self.flight = tied(value, self.flight)
        return value

    def finish(self):
        self.step(self.ring.size // 2 - self.done)
        return self.result()


def quick(body, outs, ins, smem=0, scratch=(), mib=MIB):
    spec = lambda space: pl.BlockSpec(memory_space=space)
    return pl.pallas_call(
        body,
        out_shape=[jax.ShapeDtypeStruct(shape, kind) for shape, kind in outs],
        in_specs=[spec(pltpu.SMEM if i < smem else pltpu.VMEM) for i in range(len(ins))],
        out_specs=[spec(pltpu.VMEM)] * len(outs),
        scratch_shapes=list(scratch),
        compiler_params=pltpu.CompilerParams(vmem_limit_bytes=mib * 2**20),
        cost_estimate=pl.CostEstimate(flops=1000, bytes_accessed=1000, transcendentals=0),
    )(*ins)


def place_two(ids, chunks, halves, size):
    last = len(chunks)

    def kernel(ids_ref, *refs):
        sources, outs = refs[: last + 2], refs[last + 2 :]
        for k in range(last):
            for half in range(2):
                outs[half][ids_ref[k]] = sources[k][half]
        for half in range(2):
            outs[half][ids_ref[last]] = sources[last + half][...]

    outs = [((size,) + halves[0].shape, halves[0].dtype)] * 2
    return quick(kernel, outs, [ids, *chunks, *halves], smem=1)


HEAD = 16


def place_attn(ids, chunks, halves, size, cut):
    last = len(chunks)
    rows, cols = chunks[0].shape[0] - HEAD, D // 4

    def kernel(ids_ref, *refs):
        sources, (qkv, small, *sends, out) = refs[: last + 2], refs[last + 2 :]

        def put(place, lo, hi, part, head):
            qkv[place, lo:hi] = part[head:, : 3 * SPAN]
            at = pl.multiple_of(place * rows + lo, 8)
            out[pl.ds(at, hi - lo), :] = part[head:, 3 * SPAN :].astype(F32)

        for k in range(last):
            put(ids_ref[k], 0, rows, sources[k], HEAD)
            small[ids_ref[k]] = sources[k][:HEAD, :]
        place = ids_ref[last]
        put(place, 0, cut - HEAD, sources[last], HEAD)
        put(place, cut - HEAD, rows, sources[last + 1], 0)
        small[place] = sources[last][:HEAD, :]
        for m in range(4):

            @pl.when(ids_ref[last + 1] == m)
            def _():
                for r in range(4):
                    first = STARTS[m ^ r] * HD
                    sends[r][...] = out[first : first + SPAN, :].astype(BF16)

    outs = [((size, rows, 3 * SPAN), BF16), ((size, HEAD, chunks[0].shape[1]), BF16)]
    outs += [((SPAN, cols), BF16)] * 4
    scratch = [pltpu.VMEM((D, cols), F32)]
    got = quick(kernel, outs, [ids, *chunks, *halves], smem=1, scratch=scratch)
    return got[0], got[1], got[2:]


def cut_halves(ahead, back, cut):
    def kernel(ahead_ref, back_ref, first_ref, second_ref):
        if cut is None:
            first_ref[...], second_ref[...] = ahead_ref[0], back_ref[1]
        else:
            first_ref[...], second_ref[...] = ahead_ref[:cut, :], back_ref[cut:, :]

    rows, cols = ahead.shape[-2:]
    shapes = [(rows, cols)] * 2 if cut is None else [(cut, cols), (rows - cut, cols)]
    return quick(kernel, [(shape, BF16) for shape in shapes], [ahead, back])


def dot(left, right, left_dim, right_dim):
    return lax.dot_general(
        left, right, (((left_dim,), (right_dim,)), ((), ())), preferred_element_type=F32
    )


def qkv_kernel(unit, gain, shift, weight, bias):
    rows = unit.shape[0]

    def kernel(unit_ref, gain_ref, shift_ref, weight_ref, bias_ref, a_ref, qkv_ref):
        for at in range(0, rows, 128):
            part = slice(at, at + 128)
            a = (unit_ref[part, :] * gain_ref[...] + shift_ref[...]).astype(BF16)
            a_ref[part, :] = a
            qkv_ref[part, :] = (dot(a, weight_ref[...], 1, 0) + bias_ref[...]).astype(BF16)

    outs = [((rows, D), BF16), ((rows, 3 * SPAN), BF16)]
    row = lambda v: v.reshape(1, -1)
    return quick(kernel, outs, [unit, row(gain), row(shift), weight, row(bias)])


def put_rows(ref, at, rows):
    ref[at, :, :D] = rows
    ref[at, :, D:] = jnp.zeros((rows.shape[0], LANES - D), rows.dtype)


def put_block(block, product, send_ref, keep_ref):
    if block % 2 == 1:
        put_rows(send_ref, block // 2, product.astype(BF16))
    else:
        keep_ref[block // 2] = product


def halves(slots):
    return [((2, slots, LANES), BF16), ((2, slots, D), F32)]


def project(me, context, pieces):
    rows, cols = context.shape[0], D // 4
    slots = rows // 4

    def kernel(me_ref, context_ref, *refs):
        sources, (w_ref, send_ref, keep_ref) = refs[:4], refs[4:]
        for m in range(4):

            @pl.when(me_ref[0] == m)
            def _():
                for r in range(4):
                    w_ref[:, (m ^ r) * cols : ((m ^ r) + 1) * cols] = sources[r][...]
                if m > 0:
                    head = 0 if m == 3 else WINDOW - 1
                    w_ref[head * HD : (head + 1) * HD, :] = jnp.zeros((HD, D), BF16)

        for block in range(4):
            part = context_ref[block * slots : (block + 1) * slots, :]
            put_block(block, dot(part, w_ref[...], 1, 0), send_ref, keep_ref)

    ins = [me.reshape(1).astype(jnp.int32), context, *pieces]
    return quick(kernel, [((SPAN, D), BF16)] + halves(slots), ins, smem=1)


def attention(qkv, positions):
    rows = qkv.shape[0]
    slots = rows // 4

    def kernel(qkv_ref, col_ref, row_ref, context_ref, log_ref):
        for block in range(4):
            part = slice(block * slots, (block + 1) * slots)
            mask = col_ref[part, :] >= row_ref[...]
            heads = []
            for h in range(WINDOW):
                lo, hi = h * HD, (h + 1) * HD
                queries = qkv_ref[part, lo:hi]
                keys = qkv_ref[:, SPAN + lo : SPAN + hi]
                values = qkv_ref[:, 2 * SPAN + lo : 2 * SPAN + hi]
                scores = jnp.where(mask, dot(queries, keys, 1, 1) * 0.125, -1e30)
                peak = jnp.max(scores, axis=1, keepdims=True)
                exps = jnp.exp(scores - peak)
                total = jnp.sum(exps, axis=1, keepdims=True)
                heads.append(dot((exps * (1.0 / total)).astype(BF16), values, 1, 0))
                log_ref[part, h : h + 1] = peak + jnp.log(total)
            context_ref[part, :] = jnp.concatenate(heads, axis=1).astype(BF16)

    outs = [((rows, SPAN), BF16), ((rows, 8), F32)]
    return quick(kernel, outs, [qkv, positions.reshape(-1, 1), positions.reshape(1, -1)])


def widened(rows):
    return jnp.pad(rows, ((0, 0), (0, LANES - D)))


def row(vector):
    return vector.reshape(1, -1)


def norm(values):
    mean = jnp.mean(values, axis=-1, keepdims=True)
    centred = values - mean
    scale = lax.rsqrt(jnp.mean(centred * centred, axis=-1, keepdims=True) + 1e-05)
    return centred * scale, scale


def first_norm(own, other, across):
    slots = own.shape[0]

    def kernel(own_ref, other_ref, across_ref, unit_ref):
        for block, part in enumerate((own_ref, across_ref.at[0], other_ref, across_ref.at[1])):
            unit_ref[block * slots : (block + 1) * slots, :] = norm(part[:, :D].astype(F32))[0]

    return quick(kernel, [((4 * slots, D), F32)], [own, other, across])[0]


def join_blocks(own, other, across):
    slots = own.shape[0]

    def kernel(own_ref, other_ref, across_ref, out_ref):
        for block, part in enumerate((own_ref, across_ref.at[0], other_ref, across_ref.at[1])):
            out_ref[block * slots : (block + 1) * slots, :] = part[:, :D]

    return quick(kernel, [((4 * slots, D), own.dtype)], [own, other, across])[0]


def pair_sum(keep, across):
    def kernel(keep_ref, across_ref, out_ref):
        for i in range(2):
            put_rows(out_ref, i, (keep_ref[i] + across_ref[i, :, :D].astype(F32)).astype(BF16))

    return quick(kernel, [(across.shape, BF16)], [keep, across])[0]


def second_norm(pair, got, own, other, out_bias, gain, shift):
    slots = own.shape[0]

    def kernel(
        pair_ref, got_ref, own_ref, other_ref, bias_ref, gain_ref, shift_ref,
        residual_ref, unit_ref, scale_ref, a_ref,
    ):
        for i, part in enumerate((own_ref, other_ref)):
            attn = pair_ref[i, :, :D].astype(F32) + got_ref[1 - i, :, :D].astype(F32)
            residual = part[:, :D].astype(F32) + attn + bias_ref[...]
            if i == 0:
                residual_ref[...] = residual
            unit, scale = norm(residual)
            unit_ref[i] = unit
            scale_ref[i] = scale
            put_rows(a_ref, i, (unit * gain_ref[...] + shift_ref[...]).astype(BF16))

    two = (2, slots, D)
    outs = [((slots, D), F32), (two, F32), ((2, slots, 1), F32), (pair.shape, BF16)]
    return quick(
        kernel, outs, [pair, got, own, other, row(out_bias), row(gain), row(shift)]
    )


def mlp_up(pair, across, weight, bias):
    slots = pair.shape[1]

    def kernel(pair_ref, across_ref, weight_ref, bias_ref, all_ref, act_ref, slope_ref):
        for block in range(4):
            part = slice(block * slots, (block + 1) * slots)
            rows = (across_ref if block % 2 else pair_ref)[block // 2, :, :D]
            all_ref[part, :] = rows
            pre = dot(rows, weight_ref[...], 1, 0) + bias_ref[...]
            below = 0.5 * (1.0 + lax.erf(pre * 0.7071067811865476))
            act_ref[part, :] = (pre * below).astype(BF16)
            slope_ref[part, :] = below + pre * jnp.exp(-0.5 * pre * pre) * 0.3989422804014327

    shape = (4 * slots, D)
    outs = [(shape, BF16), (shape, BF16), (shape, F32)]
    return quick(kernel, outs, [pair, across, weight, row(bias)])


def mlp_down_back(grads, w_down, slope, w_up):
    rows = grads.shape[0]
    slots = rows // 4

    def kernel(
        grad_ref, down_ref, slope_ref, up_ref, low_ref, send_ref, keep_ref, sums_ref
    ):
        sums = jnp.zeros((1, D), F32)
        for block in range(4):
            part = slice(block * slots, (block + 1) * slots)
            pre = dot(grad_ref[part, :], down_ref[...], 1, 1) * slope_ref[part, :]
            low = pre.astype(BF16)
            low_ref[part, :] = low
            sums += jnp.sum(low.astype(F32), axis=0, keepdims=True)
            put_block(block, dot(low, up_ref[...], 1, 1), send_ref, keep_ref)
        sums_ref[...] = sums

    outs = [((rows, D), BF16)] + halves(slots) + [((1, D), F32)]
    return quick(kernel, outs, [grads, w_down, slope, w_up])


def norm_pull(unit, scale, gain, grad):
    lifted = grad * gain
    return scale * (
        lifted
        - jnp.mean(lifted, axis=-1, keepdims=True)
        - unit * jnp.mean(lifted * unit, axis=-1, keepdims=True)
    )


def second_norm_back(pair, got, unit, scale, gain, own_grad, other_grad):
    slots = own_grad.shape[0]

    def kernel(
        pair_ref, got_ref, unit_ref, scale_ref, gain_ref, own_ref, other_ref,
        resid_ref, low_ref, sums_ref,
    ):
        for i, part in enumerate((own_ref, other_ref)):
            grad = pair_ref[i, :, :D].astype(F32) + got_ref[1 - i, :, :D].astype(F32)
            back = norm_pull(unit_ref[i], scale_ref[i], gain_ref[...], grad)
            resid = part[:, :D].astype(F32) + back
            low = resid.astype(BF16)
            put_rows(low_ref, i, low)
            if i == 0:
                resid_ref[...] = resid
                sums_ref[0:1, :] = jnp.sum(grad * unit_ref[i], axis=0, keepdims=True)
                sums_ref[1:2, :] = jnp.sum(grad, axis=0, keepdims=True)
                sums_ref[2:3, :] = jnp.sum(low.astype(F32), axis=0, keepdims=True)
                sums_ref[3:4, :] = jnp.sum(part[...].astype(F32), axis=0, keepdims=True)

    outs = [((slots, D), F32), (pair.shape, BF16), ((8, D), F32)]
    return quick(kernel, outs, [pair, got, unit, scale, row(gain), own_grad, other_grad])


def first_norm_back(low, w_qkv, unit):
    rows = low.shape[0]
    slots = rows // 4

    def kernel(low_ref, w_ref, unit_ref, send_ref, keep_ref, sums_ref, bias_ref):
        gain = jnp.zeros((1, D), F32)
        shift = jnp.zeros((1, D), F32)
        bias = jnp.zeros((1, 3 * SPAN), F32)
        for block in range(4):
            part = slice(block * slots, (block + 1) * slots)
            low = low_ref[part, :]
            back = dot(low, w_ref[...], 1, 1)
            gain += jnp.sum(back * unit_ref[part, :], axis=0, keepdims=True)
            shift += jnp.sum(back, axis=0, keepdims=True)
            bias += jnp.sum(low.astype(F32), axis=0, keepdims=True)
            put_block(block, back, send_ref, keep_ref)
        sums_ref[0:1, :] = gain
        sums_ref[1:2, :] = shift
        bias_ref[...] = bias

    outs = halves(slots) + [((8, D), F32), ((1, 3 * SPAN), F32)]
    return quick(kernel, outs, [low, w_qkv, unit])


def attn_parts(a_one, low, out_back, small):
    count, rows = out_back.shape[0], D // out_back.shape[0]
    wide = 3 * SPAN + D // 4

    def kernel(a_ref, low_ref, out_ref, small_ref, parts_ref, total_ref):
        total_ref[...] = dot(a_ref[...], low_ref[...], 0, 0)
        for k in range(count):
            piece = total_ref[k * rows : (k + 1) * rows, :].astype(BF16)
            parts_ref[k, HEAD:, : 3 * SPAN] = piece
            parts_ref[k, HEAD:, 3 * SPAN :] = out_ref[k]
            parts_ref[k, :HEAD, :] = small_ref[k]

    scratch = [pltpu.VMEM((D, 3 * SPAN), F32)]
    outs = [((count, HEAD + rows, wide), BF16)]
    return quick(kernel, outs, [a_one, low, out_back, small], scratch=scratch)[0]


def core_sums(keep, across):
    def kernel(keep_ref, across_ref, near_ref, far_ref):
        near_ref[...] = keep_ref[0] + across_ref[0, :, :D].astype(F32)
        put_rows(far_ref, 0, (keep_ref[1] + across_ref[1, :, :D].astype(F32)).astype(BF16))

    outs = [(keep.shape[1:], F32), ((1,) + across.shape[1:], BF16)]
    return quick(kernel, outs, [keep, across])


def input_back(own, gain, near, got, resid):
    def kernel(own_ref, gain_ref, near_ref, got_ref, resid_ref, out_ref):
        unit, scale = norm(own_ref[...].astype(F32))
        grad = near_ref[...] + got_ref[0, :, :D].astype(F32)
        back = norm_pull(unit, scale, gain_ref[...], grad)
        out_ref[...] = (resid_ref[...] + back).astype(BF16)

    return quick(kernel, [(own.shape, BF16)], [own, row(gain), near, got, resid])[0]


def out_gradient(me, context, pair, across):
    slots, cols = pair.shape[1], D // 4

    def kernel(me_ref, context_ref, pair_ref, across_ref, *outs):
        total = jnp.zeros((SPAN, D), F32)
        for block in range(4):
            part = slice(block * slots, (block + 1) * slots)
            rows = (across_ref if block % 2 else pair_ref)[block // 2, :, :D]
            total += dot(context_ref[part, :], rows, 0, 0)
        low = total.astype(BF16)
        for m in range(4):

            @pl.when(me_ref[0] == m)
            def _():
                for r in range(4):
                    outs[r][...] = low[:, (m ^ r) * cols : ((m ^ r) + 1) * cols]

    ins = [me.reshape(1).astype(jnp.int32), context, pair, across]
    return quick(kernel, [((SPAN, cols), BF16)] * 4, ins, smem=1)


def attention_back(qkv, pair, across, w_out, logs, positions, first, last, done=None):
    rows = qkv.shape[0]
    slots = rows // 4
    count = last - first
    size = count * HD
    before = first * HD

    def kernel(
        qkv_ref, pair_ref, across_ref, w_ref, log_ref, col_ref, row_ref, *refs
    ):
        low_ref, keys_acc, values_acc = refs[-3:]
        span = before + size

        def put(part, i, grads):
            low_ref[part, i * span + before : (i + 1) * span] = grads.astype(BF16)

        for block in range(4):
            part = slice(block * slots, (block + 1) * slots)
            mask = col_ref[part, :] >= row_ref[...]
            resid = (across_ref if block % 2 else pair_ref)[block // 2, :, :D]
            grads = dot(resid, w_ref[before:span, :], 1, 1).astype(BF16)
            heads = []
            for h in range(count):
                lo, hi = before + h * HD, before + (h + 1) * HD
                queries = qkv_ref[part, lo:hi]
                keys = qkv_ref[:, SPAN + lo : SPAN + hi]
                values = qkv_ref[:, 2 * SPAN + lo : 2 * SPAN + hi]
                grad = grads[:, h * HD : (h + 1) * HD]
                scores = jnp.where(mask, dot(queries, keys, 1, 1) * 0.125, -1e30)
                probs = jnp.exp(scores - log_ref[part, first + h : first + h + 1])
                prob_grad = dot(grad, values, 1, 1)
                inner = jnp.sum(probs * prob_grad, axis=1, keepdims=True)
                score_low = (probs * (prob_grad - inner)).astype(BF16)
                heads.append(dot(score_low, keys, 1, 0) * 0.125)
                keys_grad = dot(score_low, queries, 0, 0) * 0.125
                values_grad = dot(probs.astype(BF16), grad, 0, 0)
                if block == 0:
                    keys_acc[h] = keys_grad
                    values_acc[h] = values_grad
                else:
                    keys_acc[h] += keys_grad
                    values_acc[h] += values_grad
            put(part, 0, jnp.concatenate(heads, axis=1))
        for i, acc in enumerate((keys_acc, values_acc)):
            put(slice(0, rows), i + 1, jnp.concatenate([acc[h] for h in range(count)], axis=1))
        if first:
            for i in range(3):
                low_ref[:, i * span : i * span + before] = refs[0][
                    :, i * before : (i + 1) * before
                ]

    scratch = [pltpu.VMEM((count, rows, HD), F32)] * 2
    ins = [qkv, pair, across, w_out, logs, positions.reshape(-1, 1), positions.reshape(1, -1)]
    ins += [done] if first else []
    return quick(kernel, [((rows, 3 * last * HD), BF16)], ins, scratch=scratch)[0]


def ring_add(ids, parts, flight, cut=None):
    count = len(parts)
    rows, cols = parts[0].shape[1:]
    half = flight[0].shape != (count, rows, cols)

    def kernel(ids_ref, *refs):
        ahead, back = refs[2 * count], refs[2 * count + 1]
        out_ahead, out_back = refs[2 * count + 2], refs[2 * count + 3]
        total = lambda a, b: (a.astype(F32) + b.astype(F32)).astype(BF16)
        mine = [refs[i][0] for i in range(2 * count)]
        if half and count == 2:
            out_ahead[0], out_ahead[1] = total(mine[0], ahead[...]), mine[1]
            out_back[0], out_back[1] = mine[2], total(mine[3], back[...])
        elif half:
            out_ahead[0, :cut] = total(mine[0][:cut], ahead[...])
            out_ahead[0, cut:] = mine[0][cut:]
            out_back[0, :cut] = mine[1][:cut]
            out_back[0, cut:] = total(mine[1][cut:], back[...])
        else:
            for i in range(count):
                out_ahead[i] = total(mine[i], ahead[i])
                out_back[i] = total(mine[count + i], back[i])

    pick = lambda n: pl.BlockSpec((1, rows, cols), lambda i, ids, n=n: (ids[n], 0, 0))
    whole = lambda v: pl.BlockSpec(v.shape, lambda i, ids, v=v: (0,) * v.ndim)
    out = jax.ShapeDtypeStruct((count, rows, cols), BF16)
    return pl.pallas_call(
        kernel,
        out_shape=[out] * 2,
        grid_spec=pltpu.PrefetchScalarGridSpec(
            num_scalar_prefetch=1,
            grid=(1,),
            in_specs=[pick(0)] * count + [pick(1)] * count + [whole(f) for f in flight],
            out_specs=[whole(out)] * 2,
        ),
        compiler_params=pltpu.CompilerParams(vmem_limit_bytes=MIB * 2**20),
        cost_estimate=pl.CostEstimate(flops=1000, bytes_accessed=1000, transcendentals=0),
    )(ids, *parts, *parts, *flight)


def ring_far(ids, parts, cut=None):
    rows, cols = parts[0].shape[1:]
    sizes = [rows] * 2 if cut is None else [cut, rows - cut]

    def kernel(ids_ref, *refs):
        outs = refs[len(parts) :]
        if cut is None:
            outs[0][...], outs[1][...] = refs[0][0], refs[1][0]
        else:
            outs[0][...], outs[1][...] = refs[0][0, :cut, :], refs[0][0, cut:, :]

    pick = pl.BlockSpec((1, rows, cols), lambda i, ids: (ids[0], 0, 0))
    return pl.pallas_call(
        kernel,
        out_shape=[jax.ShapeDtypeStruct((n, cols), BF16) for n in sizes],
        grid_spec=pltpu.PrefetchScalarGridSpec(
            num_scalar_prefetch=1,
            grid=(1,),
            in_specs=[pick] * len(parts),
            out_specs=[pl.BlockSpec((n, cols), lambda i, ids: (0, 0)) for n in sizes],
        ),
        compiler_params=pltpu.CompilerParams(vmem_limit_bytes=MIB * 2**20),
        cost_estimate=pl.CostEstimate(flops=1000, bytes_accessed=1000, transcendentals=0),
    )(ids, *parts)


def ring_total(ids, parts, flight):
    count = len(parts)
    rows, cols = parts[0].shape[1:]

    def kernel(ids_ref, *refs):
        for i in range(count):
            mine = refs[i][0].astype(F32) + refs[count][i].astype(F32)
            refs[count + 2 + i][...] = mine + refs[count + 1][i].astype(F32)

    pick = pl.BlockSpec((1, rows, cols), lambda i, ids: (ids[0], 0, 0))
    whole = pl.BlockSpec((count, rows, cols), lambda i, ids: (0, 0, 0))
    return pl.pallas_call(
        kernel,
        out_shape=[jax.ShapeDtypeStruct((rows, cols), F32)] * count,
        grid_spec=pltpu.PrefetchScalarGridSpec(
            num_scalar_prefetch=1,
            grid=(1,),
            in_specs=[pick] * count + [whole] * 2,
            out_specs=[pl.BlockSpec((rows, cols), lambda i, ids: (0, 0))] * count,
        ),
        compiler_params=pltpu.CompilerParams(vmem_limit_bytes=MIB * 2**20),
        cost_estimate=pl.CostEstimate(flops=1000, bytes_accessed=1000, transcendentals=0),
    )(ids, *parts, *flight)


def split_units(me, rows, dp_count):
    width = FF // dp_count // 4

    def kernel(me_ref, rows_ref, *outs):
        value = rows_ref[...]
        cut = lambda d, s: value[:, (4 * d + s) * width : (4 * d + s + 1) * width]
        four = [jnp.concatenate([cut(d, s) for d in range(dp_count)], axis=1) for s in range(4)]
        for m in range(4):

            @pl.when(me_ref[0] == m)
            def _():
                for r in range(4):
                    outs[r][...] = four[m ^ r]

    outs = [((rows.shape[0], D), BF16)] * 4
    return quick(kernel, outs, [me.reshape(1).astype(jnp.int32), rows], smem=1)


def join_units(four):
    rows = four[0].shape[0]
    blocks = FF // 128

    def kernel(*refs):
        parts, out_ref = [r[...].astype(F32) for r in refs[:4]], refs[4]
        width = 136
        pieces = []
        for d in range(D // width):
            pieces += [p[:, d * width : (d + 1) * width] for p in parts]
        joined = jnp.concatenate(pieces, axis=1)
        for t in range(blocks):
            out_ref[pl.ds(t, rows, stride=blocks), :] = joined[:, t * 128 : (t + 1) * 128]

    out = quick(kernel, [((rows * blocks, 128), F32)], four)[0]
    return out.reshape(-1)


class GatherAttn(Steps):
    def __init__(self, ring, chunk):
        self.ring, self.done = ring, 0
        self.flight = (chunk, chunk)
        self.chunks, self.order = [chunk], [0]
        self.cut = 80

    def move(self, step):
        ring, (ahead, back) = self.ring, self.flight
        last = step == ring.size // 2
        if last:
            ahead, back = cut_halves(ahead, back, self.cut)
        ahead = lax.ppermute(ahead, "dp", ring.ahead)
        back = lax.ppermute(back, "dp", ring.back)
        self.flight = (ahead, back)
        if not last:
            self.chunks += [ahead, back]
            self.order += [-step, step]

    def result(self):
        ids = [self.ring.member(k) for k in self.order + [self.ring.size // 2]]
        ids = jnp.stack(ids + [lax.axis_index("seq")])
        return place_attn(ids.astype(jnp.int32), self.chunks, self.flight, self.ring.size, self.cut)


class GatherTwo(Steps):
    def __init__(self, ring, first, second):
        self.ring, self.done = ring, 0
        chunk = jnp.stack([first, second])
        self.flight = (chunk, chunk)
        self.chunks, self.order = [chunk], [0]

    def move(self, step):
        ring, (ahead, back) = self.ring, self.flight
        last = step == ring.size // 2
        if last:
            ahead, back = cut_halves(ahead, back, None)
        ahead = lax.ppermute(ahead, "dp", ring.ahead)
        back = lax.ppermute(back, "dp", ring.back)
        self.flight = (ahead, back)
        if not last:
            self.chunks += [ahead, back]
            self.order += [-step, step]

    def result(self):
        ids = jnp.stack([self.ring.member(k) for k in self.order + [self.ring.size // 2]])
        return place_two(ids.astype(jnp.int32), self.chunks, self.flight, self.ring.size)


class Reduce(Steps):
    def __init__(self, ring, parts, cut=None):
        self.ring, self.parts, self.cut, self.done = ring, parts, cut, 0
        self.flight = tuple(ring_far(self.ids(ring.size // 2), parts, cut))

    def ids(self, *steps):
        return jnp.stack([self.ring.member(k) for k in steps]).astype(jnp.int32)

    def move(self, step):
        left = self.ring.size // 2 - step + 1
        ahead, back = self.flight
        if step > 1:
            ahead, back = ring_add(self.ids(left, -left), self.parts, self.flight, self.cut)
        self.flight = (
            lax.ppermute(ahead, "dp", self.ring.ahead),
            lax.ppermute(back, "dp", self.ring.back),
        )

    def result(self):
        return ring_total(self.ids(0), self.parts, self.flight)


class Whole:
    def gather_attn(self, chunk):
        got = lax.all_gather(chunk, "dp", axis=0)
        out = got[:, HEAD:, 3 * SPAN :].reshape(D, D // 4)
        sends = xor_order([out[s * HD : s * HD + SPAN] for s in STARTS], lax.axis_index("seq"))
        return Whole.Ready((got[:, HEAD:, : 3 * SPAN], got[:, :HEAD], sends), chunk)

    def gather_two(self, first, second):
        got = lax.all_gather(jnp.stack([first, second]), "dp", axis=0)
        return Whole.Ready([got[:, 0], got[:, 1]], first)

    def reduce(self, *parts, cut=None):
        got = [lax.psum_scatter(p, "dp", scatter_dimension=0, tiled=True)[0] for p in parts]
        return Whole.Ready([g.astype(F32) for g in got], got[0])

    class Ready(Steps):
        def __init__(self, value, flight):
            self.value, self.flight = value, flight

        def step(self, count=1):
            pass

        def finish(self):
            return self.value


def join_windows(four, axis):
    cut = lambda part, lo, hi: lax.slice_in_dim(part, lo, hi, axis=axis)
    return jnp.concatenate(
        [
            four[0],
            cut(four[1], 0, SPAN - HD),
            cut(four[2], 0, SPAN - HD),
            cut(four[3], HD, SPAN),
        ],
        axis=axis,
    )


def head_cols(rows):
    piece = lambda s, b: rows[:, b * D + s * HD : b * D + s * HD + SPAN]
    return [jnp.concatenate([piece(s, b) for b in range(3)], axis=1) for s in STARTS]


def join_head_cols(four):
    block = lambda b: join_windows([f[:, b * SPAN : (b + 1) * SPAN] for f in four], 1)
    return jnp.concatenate([block(b) for b in range(3)], axis=1)


def own_cols(rows):
    return [rows[:, s * (D // 4) : (s + 1) * (D // 4)] for s in range(4)]


def unit_cols(rows, dp_count):
    four = rows.reshape(rows.shape[0], dp_count, 4, -1)
    return [four[:, :, s].reshape(rows.shape[0], D) for s in range(4)]


def join_unit_cols(four, dp_count):
    if FF // dp_count // 4 == 136:
        return join_units(four)
    parts = [f.reshape(f.shape[0], dp_count, 1, -1) for f in four]
    return jnp.concatenate(parts, axis=2).reshape(four[0].shape[0], FF)


def split_rows(flats, widths, cols_of, me):
    if all(flat.shape[0] % width == 0 for flat, width in zip(flats, widths)):
        rows = [flat.reshape(-1, width) for flat, width in zip(flats, widths)]
        return jnp.concatenate(seq_exchange(cols_of(rows), me))
    rows = [
        lax.all_gather(flat, "seq", axis=0, tiled=True).reshape(-1, width)
        for flat, width in zip(flats, widths)
    ]
    return xor_order(cols_of(rows), me)[0]


def join_rows(rows, shares, widths, join_cols, me):
    low = rows.astype(BF16)
    count = rows.shape[0] // 4
    if all(share % width == 0 for share, width in zip(shares, widths)):
        got = seq_exchange([low[m * count : (m + 1) * count] for m in range(4)], me)
        return [part.astype(F32).reshape(-1) for part in join_cols(got)]
    got = join_cols(list(lax.all_gather(low, "seq", axis=0)))
    return [
        lax.dynamic_slice_in_dim(part.reshape(-1), me * share, share, 0).astype(F32)
        for part, share in zip(got, shares)
    ]


def body(tokens, order, cotangent, qkv_weight, out_weight, up_weight, down_weight, small_params):
    slots = tokens.shape[1]
    dp_count = lax.axis_size("dp")
    me = lax.axis_index("seq")
    units = FF // (dp_count * 4)
    block_rows = D // dp_count
    ring = Ring(dp_count) if dp_count == 8 else Whole()
    start = jnp.where(me == 0, 0, jnp.where(me == 3, 12, 4 * me + 1)) * HD

    small_len = small_params.shape[0]
    wide = 3 * SPAN + D // 4

    blank = jnp.zeros((HEAD - 4, wide), BF16)
    small_row = jnp.pad(small_params.reshape(1, -1), ((0, 0), (0, wide - small_len)))
    attn_cols = lambda r: [
        jnp.concatenate([q, o], axis=1) for q, o in zip(head_cols(r[0]), own_cols(r[1]))
    ]
    if qkv_weight.shape[0] % (3 * D) == 0 and out_weight.shape[0] % D == 0:
        blocks = attn_cols([qkv_weight.reshape(-1, 3 * D), out_weight.reshape(-1, D)])
        share = blocks[0].shape[0]
        got = seq_exchange([jnp.concatenate([block, small_row]) for block in blocks], me)
        attn_chunk = jnp.concatenate([g[share:] for g in got] + [blank] + [g[:share] for g in got])
    else:
        attn_rows = split_rows([qkv_weight, out_weight], [3 * D, D], attn_cols, me)
        small_rows = xor_order(list(seq_gather(small_row)), me)
        attn_chunk = jnp.concatenate(small_rows + [blank, attn_rows])
    attn_chunk, up_flat = tied(attn_chunk, up_weight)
    attn_ring = ring.gather_attn(attn_chunk)
    attn_ring.step()
    if block_rows == 136:
        up_four = split_units(me, up_flat.reshape(-1, FF), dp_count)
        up_rows = jnp.concatenate(xor_order(rel_exchange(up_four), me))
    else:
        up_rows = split_rows([up_flat], [FF], lambda r: unit_cols(r[0], dp_count), me)
    positions = jnp.concatenate(xor_order(order.reshape(4, slots), me))
    positions = attn_ring.tie(positions)
    attn_ring.step()
    own_tokens = tokens.reshape(-1, D)
    other_tokens, across_tokens = seq_blocks(widened(own_tokens))
    unit_one = first_norm(own_tokens, other_tokens, across_tokens)
    unit_one, up_rows = attn_ring.tie((unit_one, up_rows))
    own_grad = attn_ring.tie(cotangent.reshape(-1, D))
    attn_ring.step()
    other_grad = lax.ppermute(widened(own_grad), "seq", CHIP_SWAP)
    other_grad, *mlp_rows = attn_ring.tie((other_grad, up_rows, down_weight.reshape(-1, D)))
    mlp_ring = ring.gather_two(*mlp_rows)
    across_grad = jnp.stack([widened(own_grad), other_grad])
    across_grad = lax.ppermute(across_grad, "seq", CORE_SWAP)
    grad_all = join_blocks(own_grad, other_grad, across_grad)
    w_qkv, small_all, out_sends = attn_ring.finish()
    mlp_ring.step()
    w_qkv = w_qkv.reshape(D, 3 * SPAN)
    small_full = small_all[:, :4, :small_len].reshape(-1).astype(F32)
    out_pieces = rel_exchange(out_sends)

    at = lambda i: small_full[i * D : (i + 1) * D]
    ln1_gain, ln1_bias, q_bias, v_bias, out_bias, ln2_gain, ln2_bias = [at(i) for i in range(7)]
    up_bias = small_full[7 * D : 7 * D + FF]
    down_bias = small_full[7 * D + FF : 8 * D + FF]

    window = lambda v: lax.dynamic_slice_in_dim(v, start, SPAN, 0)
    bias_qkv = jnp.concatenate([window(q_bias), jnp.zeros((SPAN,), F32), window(v_bias)])
    a_one, qkv_vals = qkv_kernel(unit_one, ln1_gain, ln1_bias, w_qkv, bias_qkv)
    a_one, qkv_vals = mlp_ring.tie((a_one, qkv_vals))
    mlp_ring.step()
    context, logs = mlp_ring.tie(attention(qkv_vals, positions))
    mlp_ring.step()
    w_out, send, keep = project(me, context, out_pieces)
    across = lax.ppermute(send, "seq", CORE_SWAP)
    pair, grad_all = tied(pair_sum(keep, across), grad_all)
    got = mlp_ring.tie(lax.ppermute(pair, "seq", CHIP_SWAP))
    w_up, w_down = (w.reshape(D, D) for w in mlp_ring.finish())
    residual, unit_two, scale_two, a_two = second_norm(
        pair, got, own_tokens, other_tokens, out_bias, ln2_gain, ln2_bias
    )
    a_across = lax.ppermute(a_two, "seq", CORE_SWAP)
    up_bias_own = lax.dynamic_index_in_dim(
        up_bias.reshape(dp_count, 4, units), me, 1, False
    ).reshape(-1)
    a_two_all, act_low, slope = mlp_up(a_two, a_across, w_up, up_bias_own)

    pre_low, send, keep, bias_cols = mlp_down_back(grad_all, w_down, slope, w_up)
    across = lax.ppermute(send, "seq", CORE_SWAP)
    pair, act_low, pre_low = tied(pair_sum(keep, across), act_low, pre_low)
    down_grad = inner_rows(act_low, grad_all).astype(BF16)
    up_grad = inner_rows(a_two_all, pre_low).astype(BF16)
    mlp_back = ring.reduce(
        down_grad.reshape(dp_count, units, D), up_grad.reshape(dp_count, block_rows, D)
    )
    mlp_back.step()
    up_bias_grad = lax.dynamic_update_slice(
        jnp.zeros((dp_count, 4, units), BF16),
        bias_cols.astype(BF16).reshape(dp_count, 1, units),
        (0, me, 0),
    ).reshape(-1)
    got, up_bias_grad = mlp_back.tie((lax.ppermute(pair, "seq", CHIP_SWAP), up_bias_grad))
    mlp_back.step()
    resid, resid_low, sums_two = second_norm_back(
        pair, got, unit_two, scale_two, ln2_gain, own_grad, other_grad
    )

    resid_across = lax.ppermute(resid_low, "seq", CORE_SWAP)
    out_four = out_gradient(me, context, resid_low, resid_across)
    back_ins = (w_out, logs, positions)
    qkv_low = attention_back(qkv_vals, resid_low, resid_across, *back_ins, 0, 2)
    out_four, resid_low, resid_across, qkv_low = mlp_back.tie(
        (out_four, resid_low, resid_across, qkv_low)
    )
    mlp_back.step()
    out_back = join_windows(xor_order(rel_exchange(out_four), me), 0)
    qkv_low = attention_back(qkv_vals, resid_low, resid_across, *back_ins, 2, WINDOW, qkv_low)
    qkv_low = mlp_back.tie(qkv_low)
    mlp_back.step()
    send, keep, sums_one, bias_sums = first_norm_back(qkv_low, w_qkv, unit_one)
    bias_sums = bias_sums.reshape(-1)
    placed = lambda v: lax.dynamic_update_slice(jnp.zeros((D,), F32), v, (start,))
    q_bias_grad = placed(bias_sums[:SPAN])
    v_bias_grad = placed(bias_sums[2 * SPAN :])

    small_grad = jnp.concatenate(
        [
            sums_one[0].astype(BF16),
            sums_one[1].astype(BF16),
            q_bias_grad.astype(BF16),
            v_bias_grad.astype(BF16),
            sums_two[2].astype(BF16),
            sums_two[0].astype(BF16),
            sums_two[1].astype(BF16),
            up_bias_grad,
            sums_two[3].astype(BF16),
            jnp.zeros((small_full.shape[0] - 8 * D - FF,), BF16),
        ]
    )
    small_grad = jnp.pad(
        small_grad.reshape(dp_count, 4, small_len), ((0, 0), (0, HEAD - 4), (0, wide - small_len))
    )
    out_back = out_back.reshape(dp_count, block_rows, D // 4)
    if block_rows == 136:
        parts = attn_parts(a_one, qkv_low, out_back, small_grad)
    else:
        qkv_grad = inner_rows(a_one, qkv_low).astype(BF16)
        parts = jnp.concatenate([qkv_grad.reshape(dp_count, block_rows, -1), out_back], axis=2)
        parts = jnp.concatenate([small_grad, parts], axis=1)
    attn_back = ring.reduce(parts, cut=80)
    attn_back.step()
    down_sum, up_sum = mlp_back.finish()
    down_sum, up_sum, send, keep, act_low = attn_back.tie(
        (down_sum, up_sum, send, keep, act_low)
    )
    attn_back.step()
    near, far = core_sums(keep, lax.ppermute(send, "seq", CORE_SWAP))
    got = lax.ppermute(far, "seq", CHIP_SWAP)
    input_grad = input_back(own_tokens, ln1_gain, near, got, resid).reshape(tokens.shape)
    (up_part,) = join_rows(
        up_sum, [up_weight.shape[0]], [FF], lambda four: (join_unit_cols(four, dp_count),), me
    )
    (attn_sum,) = attn_back.finish()
    down_part = down_sum.reshape(-1)
    mlp_abs = jnp.concatenate(xor_order(mm(act_low, w_down).astype(BF16).reshape(4, slots, D), me))
    mlp_out = lax.psum_scatter(mlp_abs, "seq", scatter_dimension=0, tiled=True).astype(F32)
    mixed = (residual + mlp_out + down_bias).astype(BF16).reshape(tokens.shape)
    join_attn = lambda four: (
        join_head_cols([f[:, : 3 * SPAN] for f in four]),
        jnp.concatenate([f[:, 3 * SPAN :] for f in four], axis=1),
    )
    low = attn_sum.astype(BF16)
    if qkv_weight.shape[0] % (3 * D) == 0 and out_weight.shape[0] % D == 0:
        share = block_rows // 4
        got = seq_exchange(
            [
                jnp.concatenate([low[HEAD + m * share : HEAD + (m + 1) * share], low[m : m + 1]])
                for m in range(4)
            ],
            me,
        )
        *got, mixed = tied(*got, mixed)
        small_got = [g[share:, :small_len] for g in got]
        qkv_part, out_part = (
            part.astype(F32).reshape(-1) for part in join_attn([g[:share] for g in got])
        )
    else:
        small_got = seq_exchange([low[m : m + 1, :small_len] for m in range(4)], me)
        qkv_part, out_part = join_rows(
            attn_sum[HEAD:],
            [qkv_weight.shape[0], out_weight.shape[0]],
            [3 * D, D],
            join_attn,
            me,
        )
    small_part = sum(g.astype(F32) for g in small_got).reshape(-1)
    return (mixed, input_grad, qkv_part, out_part, up_part, down_part, small_part)


def solution(mesh):
    rows, flat = P("dp", "seq", None), P(("dp", "seq"))
    return jax.shard_map(
        body,
        mesh=mesh,
        in_specs=(rows, P("dp", None), rows, flat, flat, flat, flat, flat),
        out_specs=(rows, rows, flat, flat, flat, flat, flat),
        check_vma=False,
    )
```

```python
import jax
import jax.numpy as jnp
from jax import lax
from jax.experimental import pallas as pl
from jax.experimental.pallas import tpu as pltpu
from jax.sharding import PartitionSpec as P

D = 1088
FF = 4352
LANES = 1152
MIB = 16
HD = 64
HEADS = D // HD
LEN = 512
F32 = jnp.float32
BF16 = jnp.bfloat16

STARTS = (0, 5, 9, 12)
WINDOW = 5
SPAN = WINDOW * HD

CORE_SWAP = [(0, 1), (1, 0), (2, 3), (3, 2)]
CHIP_SWAP = [(0, 2), (2, 0), (1, 3), (3, 1)]
DIAG_SWAP = [(0, 3), (3, 0), (1, 2), (2, 1)]


def mm(left, right):
    return jnp.dot(left, right, preferred_element_type=F32)


def inner_rows(left, right):
    return lax.dot_general(left, right, (((0,), (0,)), ((), ())), preferred_element_type=F32)


def times_transposed(left, right):
    return lax.dot_general(left, right, (((1,), (1,)), ((), ())), preferred_element_type=F32)


def xor_order(four, me):
    core, chip = me % 2 == 1, me // 2 == 1
    a = [four[0], four[1], four[2], four[3]]
    a = [jnp.where(core, a[i ^ 1], a[i]) for i in range(4)]
    return [jnp.where(chip, a[i ^ 2], a[i]) for i in range(4)]


def seq_blocks(rows):
    other = lax.ppermute(rows, "seq", CHIP_SWAP)
    return other, lax.ppermute(jnp.stack([rows, other]), "seq", CORE_SWAP)


def seq_gather(rows):
    other, across = seq_blocks(rows)
    return jnp.stack([rows, across[0], other, across[1]])


def core_gather(pair):
    across = lax.ppermute(pair, "seq", CORE_SWAP)
    return jnp.stack([pair[0], across[0], pair[1], across[1]])


def core_reduce(blocks):
    low = blocks.astype(BF16)
    across = lax.ppermute(jnp.stack([low[1], low[3]]), "seq", CORE_SWAP).astype(F32)
    return blocks[0] + across[0], blocks[2] + across[1]


def seq_reduce(blocks):
    near, far = core_reduce(blocks)
    return near + lax.ppermute(far.astype(BF16), "seq", CHIP_SWAP).astype(F32)


def pair_reduce(blocks):
    near, far = core_reduce(blocks)
    pair = jnp.stack([near, far]).astype(BF16)
    got = lax.ppermute(pair, "seq", CHIP_SWAP).astype(F32)
    return pair.astype(F32) + jnp.stack([got[1], got[0]])


def seq_exchange(blocks, me):
    return xor_order(rel_exchange(xor_order(blocks, me)), me)


def rel_exchange(rel):
    return [
        rel[0],
        lax.ppermute(rel[1], "seq", CORE_SWAP),
        lax.ppermute(rel[2], "seq", CHIP_SWAP),
        lax.ppermute(rel[3], "seq", DIAG_SWAP),
    ]


def tied(*values):
    return lax.optimization_barrier(values)


class Ring:
    def __init__(self, size):
        self.size = size
        half = size // 2
        walk = [2 * i for i in range(half)] + [2 * i + 1 for i in range(half)][::-1]
        self.ahead = [(walk[i], walk[(i + 1) % size]) for i in range(size)]
        self.back = [(b, a) for a, b in self.ahead]
        index = lax.axis_index("dp")
        self.place = jnp.where(index % 2 == 0, index // 2, size - 1 - index // 2)

    def member(self, step):
        place = (self.place + step + self.size) % self.size
        return jnp.where(place < self.size // 2, 2 * place, 2 * (self.size - 1 - place) + 1)

    def gather_attn(self, chunk):
        return GatherAttn(self, chunk)

    def gather_two(self, first, second):
        return GatherTwo(self, first, second)

    def reduce(self, *parts, cut=None):
        return Reduce(self, parts, cut)


class Steps:
    def step(self, count=1):
        for _ in range(count):
            self.done += 1
            self.move(self.done)

    def tie(self, value):
        value, self.flight = tied(value, self.flight)
        return value

    def finish(self):
        self.step(self.ring.size // 2 - self.done)
        return self.result()


def quick(body, outs, ins, smem=0, scratch=(), mib=MIB):
    spec = lambda space: pl.BlockSpec(memory_space=space)
    return pl.pallas_call(
        body,
        out_shape=[jax.ShapeDtypeStruct(shape, kind) for shape, kind in outs],
        in_specs=[spec(pltpu.SMEM if i < smem else pltpu.VMEM) for i in range(len(ins))],
        out_specs=[spec(pltpu.VMEM)] * len(outs),
        scratch_shapes=list(scratch),
        compiler_params=pltpu.CompilerParams(vmem_limit_bytes=mib * 2**20),
        cost_estimate=pl.CostEstimate(flops=1000, bytes_accessed=1000, transcendentals=0),
    )(*ins)


def place_two(ids, chunks, halves, size):
    last = len(chunks)

    def kernel(ids_ref, *refs):
        sources, outs = refs[: last + 2], refs[last + 2 :]
        for k in range(last):
            for half in range(2):
                outs[half][ids_ref[k]] = sources[k][half]
        for half in range(2):
            outs[half][ids_ref[last]] = sources[last + half][...]

    outs = [((size,) + halves[0].shape, halves[0].dtype)] * 2
    return quick(kernel, outs, [ids, *chunks, *halves], smem=1)


HEAD = 16


def place_attn(ids, chunks, halves, size, cut):
    last = len(chunks)
    rows, cols = chunks[0].shape[0] - HEAD, D // 4

    def kernel(ids_ref, *refs):
        sources, (qkv, small, *sends, out) = refs[: last + 2], refs[last + 2 :]

        def put(place, lo, hi, part, head):
            qkv[place, lo:hi] = part[head:, : 3 * SPAN]
            at = pl.multiple_of(place * rows + lo, 8)
            out[pl.ds(at, hi - lo), :] = part[head:, 3 * SPAN :].astype(F32)

        for k in range(last):
            put(ids_ref[k], 0, rows, sources[k], HEAD)
            small[ids_ref[k]] = sources[k][:HEAD, :]
        place = ids_ref[last]
        put(place, 0, cut - HEAD, sources[last], HEAD)
        put(place, cut - HEAD, rows, sources[last + 1], 0)
        small[place] = sources[last][:HEAD, :]
        for m in range(4):

            @pl.when(ids_ref[last + 1] == m)
            def _():
                for r in range(4):
                    first = STARTS[m ^ r] * HD
                    sends[r][...] = out[first : first + SPAN, :].astype(BF16)

    outs = [((size, rows, 3 * SPAN), BF16), ((size, HEAD, chunks[0].shape[1]), BF16)]
    outs += [((SPAN, cols), BF16)] * 4
    scratch = [pltpu.VMEM((D, cols), F32)]
    got = quick(kernel, outs, [ids, *chunks, *halves], smem=1, scratch=scratch)
    return got[0], got[1], got[2:]


def cut_halves(ahead, back, cut):
    def kernel(ahead_ref, back_ref, first_ref, second_ref):
        if cut is None:
            first_ref[...], second_ref[...] = ahead_ref[0], back_ref[1]
        else:
            first_ref[...], second_ref[...] = ahead_ref[:cut, :], back_ref[cut:, :]

    rows, cols = ahead.shape[-2:]
    shapes = [(rows, cols)] * 2 if cut is None else [(cut, cols), (rows - cut, cols)]
    return quick(kernel, [(shape, BF16) for shape in shapes], [ahead, back])


def dot(left, right, left_dim, right_dim):
    return lax.dot_general(
        left, right, (((left_dim,), (right_dim,)), ((), ())), preferred_element_type=F32
    )


def qkv_kernel(unit, gain, shift, weight, bias):
    rows = unit.shape[0]

    def kernel(unit_ref, gain_ref, shift_ref, weight_ref, bias_ref, a_ref, qkv_ref):
        for at in range(0, rows, 128):
            part = slice(at, at + 128)
            a = (unit_ref[part, :] * gain_ref[...] + shift_ref[...]).astype(BF16)
            a_ref[part, :] = a
            qkv_ref[part, :] = (dot(a, weight_ref[...], 1, 0) + bias_ref[...]).astype(BF16)

    outs = [((rows, D), BF16), ((rows, 3 * SPAN), BF16)]
    row = lambda v: v.reshape(1, -1)
    return quick(kernel, outs, [unit, row(gain), row(shift), weight, row(bias)])


def put_rows(ref, at, rows):
    ref[at, :, :D] = rows
    ref[at, :, D:] = jnp.zeros((rows.shape[0], LANES - D), rows.dtype)


def put_block(block, product, send_ref, keep_ref):
    if block % 2 == 1:
        put_rows(send_ref, block // 2, product.astype(BF16))
    else:
        keep_ref[block // 2] = product


def halves(slots):
    return [((2, slots, LANES), BF16), ((2, slots, D), F32)]


def project(me, context, pieces):
    rows, cols = context.shape[0], D // 4
    slots = rows // 4

    def kernel(me_ref, context_ref, *refs):
        sources, (w_ref, send_ref, keep_ref) = refs[:4], refs[4:]
        for m in range(4):

            @pl.when(me_ref[0] == m)
            def _():
                for r in range(4):
                    w_ref[:, (m ^ r) * cols : ((m ^ r) + 1) * cols] = sources[r][...]
                if m > 0:
                    head = 0 if m == 3 else WINDOW - 1
                    w_ref[head * HD : (head + 1) * HD, :] = jnp.zeros((HD, D), BF16)

        for block in range(4):
            part = context_ref[block * slots : (block + 1) * slots, :]
            put_block(block, dot(part, w_ref[...], 1, 0), send_ref, keep_ref)

    ins = [me.reshape(1).astype(jnp.int32), context, *pieces]
    return quick(kernel, [((SPAN, D), BF16)] + halves(slots), ins, smem=1)


def attention(qkv, positions):
    rows = qkv.shape[0]
    slots = rows // 4

    def kernel(qkv_ref, col_ref, row_ref, context_ref, log_ref):
        for block in range(4):
            part = slice(block * slots, (block + 1) * slots)
            mask = col_ref[part, :] >= row_ref[...]
            heads = []
            for h in range(WINDOW):
                lo, hi = h * HD, (h + 1) * HD
                queries = qkv_ref[part, lo:hi]
                keys = qkv_ref[:, SPAN + lo : SPAN + hi]
                values = qkv_ref[:, 2 * SPAN + lo : 2 * SPAN + hi]
                scores = jnp.where(mask, dot(queries, keys, 1, 1) * 0.125, -1e30)
                peak = jnp.max(scores, axis=1, keepdims=True)
                exps = jnp.exp(scores - peak)
                total = jnp.sum(exps, axis=1, keepdims=True)
                heads.append(dot((exps * (1.0 / total)).astype(BF16), values, 1, 0))
                log_ref[part, h : h + 1] = peak + jnp.log(total)
            context_ref[part, :] = jnp.concatenate(heads, axis=1).astype(BF16)

    outs = [((rows, SPAN), BF16), ((rows, 8), F32)]
    return quick(kernel, outs, [qkv, positions.reshape(-1, 1), positions.reshape(1, -1)])


def widened(rows):
    return jnp.pad(rows, ((0, 0), (0, LANES - D)))


def row(vector):
    return vector.reshape(1, -1)


def norm(values):
    mean = jnp.mean(values, axis=-1, keepdims=True)
    centred = values - mean
    scale = lax.rsqrt(jnp.mean(centred * centred, axis=-1, keepdims=True) + 1e-05)
    return centred * scale, scale


def first_norm(own, other, across):
    slots = own.shape[0]

    def kernel(own_ref, other_ref, across_ref, unit_ref):
        for block, part in enumerate((own_ref, across_ref.at[0], other_ref, across_ref.at[1])):
            unit_ref[block * slots : (block + 1) * slots, :] = norm(part[:, :D].astype(F32))[0]

    return quick(kernel, [((4 * slots, D), F32)], [own, other, across])[0]


def join_blocks(own, other, across):
    slots = own.shape[0]

    def kernel(own_ref, other_ref, across_ref, out_ref):
        for block, part in enumerate((own_ref, across_ref.at[0], other_ref, across_ref.at[1])):
            out_ref[block * slots : (block + 1) * slots, :] = part[:, :D]

    return quick(kernel, [((4 * slots, D), own.dtype)], [own, other, across])[0]


def pair_sum(keep, across):
    def kernel(keep_ref, across_ref, out_ref):
        for i in range(2):
            put_rows(out_ref, i, (keep_ref[i] + across_ref[i, :, :D].astype(F32)).astype(BF16))

    return quick(kernel, [(across.shape, BF16)], [keep, across])[0]


def second_norm(pair, got, own, other, out_bias, gain, shift):
    slots = own.shape[0]

    def kernel(
        pair_ref, got_ref, own_ref, other_ref, bias_ref, gain_ref, shift_ref,
        residual_ref, unit_ref, scale_ref, a_ref,
    ):
        for i, part in enumerate((own_ref, other_ref)):
            attn = pair_ref[i, :, :D].astype(F32) + got_ref[1 - i, :, :D].astype(F32)
            residual = part[:, :D].astype(F32) + attn + bias_ref[...]
            if i == 0:
                residual_ref[...] = residual
            unit, scale = norm(residual)
            unit_ref[i] = unit
            scale_ref[i] = scale
            put_rows(a_ref, i, (unit * gain_ref[...] + shift_ref[...]).astype(BF16))

    two = (2, slots, D)
    outs = [((slots, D), F32), (two, F32), ((2, slots, 1), F32), (pair.shape, BF16)]
    return quick(
        kernel, outs, [pair, got, own, other, row(out_bias), row(gain), row(shift)]
    )


def mlp_up(pair, across, weight, bias):
    slots = pair.shape[1]

    def kernel(pair_ref, across_ref, weight_ref, bias_ref, all_ref, act_ref, slope_ref):
        for block in range(4):
            part = slice(block * slots, (block + 1) * slots)
            rows = (across_ref if block % 2 else pair_ref)[block // 2, :, :D]
            all_ref[part, :] = rows
            pre = dot(rows, weight_ref[...], 1, 0) + bias_ref[...]
            below = 0.5 * (1.0 + lax.erf(pre * 0.7071067811865476))
            act_ref[part, :] = (pre * below).astype(BF16)
            slope_ref[part, :] = below + pre * jnp.exp(-0.5 * pre * pre) * 0.3989422804014327

    shape = (4 * slots, D)
    outs = [(shape, BF16), (shape, BF16), (shape, F32)]
    return quick(kernel, outs, [pair, across, weight, row(bias)])


def mlp_down_back(grads, w_down, slope, w_up):
    rows = grads.shape[0]
    slots = rows // 4

    def kernel(
        grad_ref, down_ref, slope_ref, up_ref, low_ref, send_ref, keep_ref, sums_ref
    ):
        sums = jnp.zeros((1, D), F32)
        for block in range(4):
            part = slice(block * slots, (block + 1) * slots)
            pre = dot(grad_ref[part, :], down_ref[...], 1, 1) * slope_ref[part, :]
            low = pre.astype(BF16)
            low_ref[part, :] = low
            sums += jnp.sum(low.astype(F32), axis=0, keepdims=True)
            put_block(block, dot(low, up_ref[...], 1, 1), send_ref, keep_ref)
        sums_ref[...] = sums

    outs = [((rows, D), BF16)] + halves(slots) + [((1, D), F32)]
    return quick(kernel, outs, [grads, w_down, slope, w_up])


def norm_pull(unit, scale, gain, grad):
    lifted = grad * gain
    return scale * (
        lifted
        - jnp.mean(lifted, axis=-1, keepdims=True)
        - unit * jnp.mean(lifted * unit, axis=-1, keepdims=True)
    )


def second_norm_back(pair, got, unit, scale, gain, own_grad, other_grad):
    slots = own_grad.shape[0]

    def kernel(
        pair_ref, got_ref, unit_ref, scale_ref, gain_ref, own_ref, other_ref,
        resid_ref, low_ref, sums_ref,
    ):
        for i, part in enumerate((own_ref, other_ref)):
            grad = pair_ref[i, :, :D].astype(F32) + got_ref[1 - i, :, :D].astype(F32)
            back = norm_pull(unit_ref[i], scale_ref[i], gain_ref[...], grad)
            resid = part[:, :D].astype(F32) + back
            low = resid.astype(BF16)
            put_rows(low_ref, i, low)
            if i == 0:
                resid_ref[...] = resid
                sums_ref[0:1, :] = jnp.sum(grad * unit_ref[i], axis=0, keepdims=True)
                sums_ref[1:2, :] = jnp.sum(grad, axis=0, keepdims=True)
                sums_ref[2:3, :] = jnp.sum(low.astype(F32), axis=0, keepdims=True)
                sums_ref[3:4, :] = jnp.sum(part[...].astype(F32), axis=0, keepdims=True)

    outs = [((slots, D), F32), (pair.shape, BF16), ((8, D), F32)]
    return quick(kernel, outs, [pair, got, unit, scale, row(gain), own_grad, other_grad])


def first_norm_back(low, w_qkv, unit):
    rows = low.shape[0]
    slots = rows // 4

    def kernel(low_ref, w_ref, unit_ref, send_ref, keep_ref, sums_ref, bias_ref):
        gain = jnp.zeros((1, D), F32)
        shift = jnp.zeros((1, D), F32)
        bias = jnp.zeros((1, 3 * SPAN), F32)
        for block in range(4):
            part = slice(block * slots, (block + 1) * slots)
            low = low_ref[part, :]
            back = dot(low, w_ref[...], 1, 1)
            gain += jnp.sum(back * unit_ref[part, :], axis=0, keepdims=True)
            shift += jnp.sum(back, axis=0, keepdims=True)
            bias += jnp.sum(low.astype(F32), axis=0, keepdims=True)
            put_block(block, back, send_ref, keep_ref)
        sums_ref[0:1, :] = gain
        sums_ref[1:2, :] = shift
        bias_ref[...] = bias

    outs = halves(slots) + [((8, D), F32), ((1, 3 * SPAN), F32)]
    return quick(kernel, outs, [low, w_qkv, unit])


def attn_parts(a_one, low, out_back, small):
    count, rows = out_back.shape[0], D // out_back.shape[0]
    wide = 3 * SPAN + D // 4

    def kernel(a_ref, low_ref, out_ref, small_ref, parts_ref, total_ref):
        total_ref[...] = dot(a_ref[...], low_ref[...], 0, 0)
        for k in range(count):
            piece = total_ref[k * rows : (k + 1) * rows, :].astype(BF16)
            parts_ref[k, HEAD:, : 3 * SPAN] = piece
            parts_ref[k, HEAD:, 3 * SPAN :] = out_ref[k]
            parts_ref[k, :HEAD, :] = small_ref[k]

    scratch = [pltpu.VMEM((D, 3 * SPAN), F32)]
    outs = [((count, HEAD + rows, wide), BF16)]
    return quick(kernel, outs, [a_one, low, out_back, small], scratch=scratch)[0]


def core_sums(keep, across):
    def kernel(keep_ref, across_ref, near_ref, far_ref):
        near_ref[...] = keep_ref[0] + across_ref[0, :, :D].astype(F32)
        put_rows(far_ref, 0, (keep_ref[1] + across_ref[1, :, :D].astype(F32)).astype(BF16))

    outs = [(keep.shape[1:], F32), ((1,) + across.shape[1:], BF16)]
    return quick(kernel, outs, [keep, across])


def input_back(own, gain, near, got, resid):
    def kernel(own_ref, gain_ref, near_ref, got_ref, resid_ref, out_ref):
        unit, scale = norm(own_ref[...].astype(F32))
        grad = near_ref[...] + got_ref[0, :, :D].astype(F32)
        back = norm_pull(unit, scale, gain_ref[...], grad)
        out_ref[...] = (resid_ref[...] + back).astype(BF16)

    return quick(kernel, [(own.shape, BF16)], [own, row(gain), near, got, resid])[0]


def out_gradient(me, context, pair, across):
    slots, cols = pair.shape[1], D // 4

    def kernel(me_ref, context_ref, pair_ref, across_ref, *outs):
        total = jnp.zeros((SPAN, D), F32)
        for block in range(4):
            part = slice(block * slots, (block + 1) * slots)
            rows = (across_ref if block % 2 else pair_ref)[block // 2, :, :D]
            total += dot(context_ref[part, :], rows, 0, 0)
        low = total.astype(BF16)
        for m in range(4):

            @pl.when(me_ref[0] == m)
            def _():
                for r in range(4):
                    outs[r][...] = low[:, (m ^ r) * cols : ((m ^ r) + 1) * cols]

    ins = [me.reshape(1).astype(jnp.int32), context, pair, across]
    return quick(kernel, [((SPAN, cols), BF16)] * 4, ins, smem=1)


def attention_back(qkv, pair, across, w_out, logs, positions, first, last, done=None):
    rows = qkv.shape[0]
    slots = rows // 4
    count = last - first
    size = count * HD
    before = first * HD

    def kernel(
        qkv_ref, pair_ref, across_ref, w_ref, log_ref, col_ref, row_ref, *refs
    ):
        low_ref, keys_acc, values_acc = refs[-3:]
        span = before + size

        def put(part, i, grads):
            low_ref[part, i * span + before : (i + 1) * span] = grads.astype(BF16)

        for block in range(4):
            part = slice(block * slots, (block + 1) * slots)
            mask = col_ref[part, :] >= row_ref[...]
            resid = (across_ref if block % 2 else pair_ref)[block // 2, :, :D]
            grads = dot(resid, w_ref[before:span, :], 1, 1).astype(BF16)
            heads = []
            for h in range(count):
                lo, hi = before + h * HD, before + (h + 1) * HD
                queries = qkv_ref[part, lo:hi]
                keys = qkv_ref[:, SPAN + lo : SPAN + hi]
                values = qkv_ref[:, 2 * SPAN + lo : 2 * SPAN + hi]
                grad = grads[:, h * HD : (h + 1) * HD]
                scores = jnp.where(mask, dot(queries, keys, 1, 1) * 0.125, -1e30)
                probs = jnp.exp(scores - log_ref[part, first + h : first + h + 1])
                prob_grad = dot(grad, values, 1, 1)
                inner = jnp.sum(probs * prob_grad, axis=1, keepdims=True)
                score_low = (probs * (prob_grad - inner)).astype(BF16)
                heads.append(dot(score_low, keys, 1, 0) * 0.125)
                keys_grad = dot(score_low, queries, 0, 0) * 0.125
                values_grad = dot(probs.astype(BF16), grad, 0, 0)
                if block == 0:
                    keys_acc[h] = keys_grad
                    values_acc[h] = values_grad
                else:
                    keys_acc[h] += keys_grad
                    values_acc[h] += values_grad
            put(part, 0, jnp.concatenate(heads, axis=1))
        for i, acc in enumerate((keys_acc, values_acc)):
            put(slice(0, rows), i + 1, jnp.concatenate([acc[h] for h in range(count)], axis=1))
        if first:
            for i in range(3):
                low_ref[:, i * span : i * span + before] = refs[0][
                    :, i * before : (i + 1) * before
                ]

    scratch = [pltpu.VMEM((count, rows, HD), F32)] * 2
    ins = [qkv, pair, across, w_out, logs, positions.reshape(-1, 1), positions.reshape(1, -1)]
    ins += [done] if first else []
    return quick(kernel, [((rows, 3 * last * HD), BF16)], ins, scratch=scratch)[0]


def ring_add(ids, parts, flight, cut=None):
    count = len(parts)
    rows, cols = parts[0].shape[1:]
    half = flight[0].shape != (count, rows, cols)

    def kernel(ids_ref, *refs):
        ahead, back = refs[2 * count], refs[2 * count + 1]
        out_ahead, out_back = refs[2 * count + 2], refs[2 * count + 3]
        total = lambda a, b: (a.astype(F32) + b.astype(F32)).astype(BF16)
        mine = [refs[i][0] for i in range(2 * count)]
        if half and count == 2:
            out_ahead[0], out_ahead[1] = total(mine[0], ahead[...]), mine[1]
            out_back[0], out_back[1] = mine[2], total(mine[3], back[...])
        elif half:
            out_ahead[0, :cut] = total(mine[0][:cut], ahead[...])
            out_ahead[0, cut:] = mine[0][cut:]
            out_back[0, :cut] = mine[1][:cut]
            out_back[0, cut:] = total(mine[1][cut:], back[...])
        else:
            for i in range(count):
                out_ahead[i] = total(mine[i], ahead[i])
                out_back[i] = total(mine[count + i], back[i])

    pick = lambda n: pl.BlockSpec((1, rows, cols), lambda i, ids, n=n: (ids[n], 0, 0))
    whole = lambda v: pl.BlockSpec(v.shape, lambda i, ids, v=v: (0,) * v.ndim)
    out = jax.ShapeDtypeStruct((count, rows, cols), BF16)
    return pl.pallas_call(
        kernel,
        out_shape=[out] * 2,
        grid_spec=pltpu.PrefetchScalarGridSpec(
            num_scalar_prefetch=1,
            grid=(1,),
            in_specs=[pick(0)] * count + [pick(1)] * count + [whole(f) for f in flight],
            out_specs=[whole(out)] * 2,
        ),
        compiler_params=pltpu.CompilerParams(vmem_limit_bytes=MIB * 2**20),
        cost_estimate=pl.CostEstimate(flops=1000, bytes_accessed=1000, transcendentals=0),
    )(ids, *parts, *parts, *flight)


def ring_far(ids, parts, cut=None):
    rows, cols = parts[0].shape[1:]
    sizes = [rows] * 2 if cut is None else [cut, rows - cut]

    def kernel(ids_ref, *refs):
        outs = refs[len(parts) :]
        if cut is None:
            outs[0][...], outs[1][...] = refs[0][0], refs[1][0]
        else:
            outs[0][...], outs[1][...] = refs[0][0, :cut, :], refs[0][0, cut:, :]

    pick = pl.BlockSpec((1, rows, cols), lambda i, ids: (ids[0], 0, 0))
    return pl.pallas_call(
        kernel,
        out_shape=[jax.ShapeDtypeStruct((n, cols), BF16) for n in sizes],
        grid_spec=pltpu.PrefetchScalarGridSpec(
            num_scalar_prefetch=1,
            grid=(1,),
            in_specs=[pick] * len(parts),
            out_specs=[pl.BlockSpec((n, cols), lambda i, ids: (0, 0)) for n in sizes],
        ),
        compiler_params=pltpu.CompilerParams(vmem_limit_bytes=MIB * 2**20),
        cost_estimate=pl.CostEstimate(flops=1000, bytes_accessed=1000, transcendentals=0),
    )(ids, *parts)


def ring_total(ids, parts, flight):
    count = len(parts)
    rows, cols = parts[0].shape[1:]

    def kernel(ids_ref, *refs):
        for i in range(count):
            mine = refs[i][0].astype(F32) + refs[count][i].astype(F32)
            refs[count + 2 + i][...] = mine + refs[count + 1][i].astype(F32)

    pick = pl.BlockSpec((1, rows, cols), lambda i, ids: (ids[0], 0, 0))
    whole = pl.BlockSpec((count, rows, cols), lambda i, ids: (0, 0, 0))
    return pl.pallas_call(
        kernel,
        out_shape=[jax.ShapeDtypeStruct((rows, cols), F32)] * count,
        grid_spec=pltpu.PrefetchScalarGridSpec(
            num_scalar_prefetch=1,
            grid=(1,),
            in_specs=[pick] * count + [whole] * 2,
            out_specs=[pl.BlockSpec((rows, cols), lambda i, ids: (0, 0))] * count,
        ),
        compiler_params=pltpu.CompilerParams(vmem_limit_bytes=MIB * 2**20),
        cost_estimate=pl.CostEstimate(flops=1000, bytes_accessed=1000, transcendentals=0),
    )(ids, *parts, *flight)


def split_units(me, rows, dp_count):
    width = FF // dp_count // 4

    def kernel(me_ref, rows_ref, *outs):
        value = rows_ref[...]
        cut = lambda d, s: value[:, (4 * d + s) * width : (4 * d + s + 1) * width]
        four = [jnp.concatenate([cut(d, s) for d in range(dp_count)], axis=1) for s in range(4)]
        for m in range(4):

            @pl.when(me_ref[0] == m)
            def _():
                for r in range(4):
                    outs[r][...] = four[m ^ r]

    outs = [((rows.shape[0], D), BF16)] * 4
    return quick(kernel, outs, [me.reshape(1).astype(jnp.int32), rows], smem=1)


def join_units(four):
    rows = four[0].shape[0]
    blocks = FF // 128

    def kernel(*refs):
        parts, out_ref = [r[...].astype(F32) for r in refs[:4]], refs[4]
        width = 136
        pieces = []
        for d in range(D // width):
            pieces += [p[:, d * width : (d + 1) * width] for p in parts]
        joined = jnp.concatenate(pieces, axis=1)
        for t in range(blocks):
            out_ref[pl.ds(t, rows, stride=blocks), :] = joined[:, t * 128 : (t + 1) * 128]

    out = quick(kernel, [((rows * blocks, 128), F32)], four)[0]
    return out.reshape(-1)


class GatherAttn(Steps):
    def __init__(self, ring, chunk):
        self.ring, self.done = ring, 0
        self.flight = (chunk, chunk)
        self.chunks, self.order = [chunk], [0]
        self.cut = 80

    def move(self, step):
        ring, (ahead, back) = self.ring, self.flight
        last = step == ring.size // 2
        if last:
            ahead, back = cut_halves(ahead, back, self.cut)
        ahead = lax.ppermute(ahead, "dp", ring.ahead)
        back = lax.ppermute(back, "dp", ring.back)
        self.flight = (ahead, back)
        if not last:
            self.chunks += [ahead, back]
            self.order += [-step, step]

    def result(self):
        ids = [self.ring.member(k) for k in self.order + [self.ring.size // 2]]
        ids = jnp.stack(ids + [lax.axis_index("seq")])
        return place_attn(ids.astype(jnp.int32), self.chunks, self.flight, self.ring.size, self.cut)


class GatherTwo(Steps):
    def __init__(self, ring, first, second):
        self.ring, self.done = ring, 0
        chunk = jnp.stack([first, second])
        self.flight = (chunk, chunk)
        self.chunks, self.order = [chunk], [0]

    def cut(self):
        self.flight = tuple(cut_halves(*self.flight, None))

    def move(self, step):
        ring, (ahead, back) = self.ring, self.flight
        last = step == ring.size // 2
        if last and ahead.ndim == 3:
            self.cut()
            ahead, back = self.flight
        ahead = lax.ppermute(ahead, "dp", ring.ahead)
        back = lax.ppermute(back, "dp", ring.back)
        self.flight = (ahead, back)
        if not last:
            self.chunks += [ahead, back]
            self.order += [-step, step]

    def result(self):
        ids = jnp.stack([self.ring.member(k) for k in self.order + [self.ring.size // 2]])
        return place_two(ids.astype(jnp.int32), self.chunks, self.flight, self.ring.size)


class Reduce(Steps):
    def __init__(self, ring, parts, cut=None):
        self.ring, self.parts, self.cut, self.done = ring, parts, cut, 0
        self.flight = tuple(ring_far(self.ids(ring.size // 2), parts, cut))

    def ids(self, *steps):
        return jnp.stack([self.ring.member(k) for k in steps]).astype(jnp.int32)

    def move(self, step):
        left = self.ring.size // 2 - step + 1
        ahead, back = self.flight
        if step > 1:
            ahead, back = ring_add(self.ids(left, -left), self.parts, self.flight, self.cut)
        self.flight = (
            lax.ppermute(ahead, "dp", self.ring.ahead),
            lax.ppermute(back, "dp", self.ring.back),
        )

    def result(self):
        return ring_total(self.ids(0), self.parts, self.flight)


class Whole:
    def gather_attn(self, chunk):
        got = lax.all_gather(chunk, "dp", axis=0)
        out = got[:, HEAD:, 3 * SPAN :].reshape(D, D // 4)
        sends = xor_order([out[s * HD : s * HD + SPAN] for s in STARTS], lax.axis_index("seq"))
        return Whole.Ready((got[:, HEAD:, : 3 * SPAN], got[:, :HEAD], sends), chunk)

    def gather_two(self, first, second):
        got = lax.all_gather(jnp.stack([first, second]), "dp", axis=0)
        return Whole.Ready([got[:, 0], got[:, 1]], first)

    def reduce(self, *parts, cut=None):
        got = [lax.psum_scatter(p, "dp", scatter_dimension=0, tiled=True)[0] for p in parts]
        return Whole.Ready([g.astype(F32) for g in got], got[0])

    class Ready(Steps):
        def __init__(self, value, flight):
            self.value, self.flight = value, flight

        def step(self, count=1):
            pass

        def cut(self):
            pass

        def finish(self):
            return self.value


def join_windows(four, axis):
    cut = lambda part, lo, hi: lax.slice_in_dim(part, lo, hi, axis=axis)
    return jnp.concatenate(
        [
            four[0],
            cut(four[1], 0, SPAN - HD),
            cut(four[2], 0, SPAN - HD),
            cut(four[3], HD, SPAN),
        ],
        axis=axis,
    )


def head_cols(rows):
    piece = lambda s, b: rows[:, b * D + s * HD : b * D + s * HD + SPAN]
    return [jnp.concatenate([piece(s, b) for b in range(3)], axis=1) for s in STARTS]


def join_head_cols(four):
    block = lambda b: join_windows([f[:, b * SPAN : (b + 1) * SPAN] for f in four], 1)
    return jnp.concatenate([block(b) for b in range(3)], axis=1)


def own_cols(rows):
    return [rows[:, s * (D // 4) : (s + 1) * (D // 4)] for s in range(4)]


def unit_cols(rows, dp_count):
    four = rows.reshape(rows.shape[0], dp_count, 4, -1)
    return [four[:, :, s].reshape(rows.shape[0], D) for s in range(4)]


def join_unit_cols(four, dp_count):
    if FF // dp_count // 4 == 136:
        return join_units(four)
    parts = [f.reshape(f.shape[0], dp_count, 1, -1) for f in four]
    return jnp.concatenate(parts, axis=2).reshape(four[0].shape[0], FF)


def split_rows(flats, widths, cols_of, me):
    if all(flat.shape[0] % width == 0 for flat, width in zip(flats, widths)):
        rows = [flat.reshape(-1, width) for flat, width in zip(flats, widths)]
        return jnp.concatenate(seq_exchange(cols_of(rows), me))
    rows = [
        lax.all_gather(flat, "seq", axis=0, tiled=True).reshape(-1, width)
        for flat, width in zip(flats, widths)
    ]
    return xor_order(cols_of(rows), me)[0]


def join_rows(rows, shares, widths, join_cols, me):
    low = rows.astype(BF16)
    count = rows.shape[0] // 4
    if all(share % width == 0 for share, width in zip(shares, widths)):
        got = seq_exchange([low[m * count : (m + 1) * count] for m in range(4)], me)
        return [part.astype(F32).reshape(-1) for part in join_cols(got)]
    got = join_cols(list(lax.all_gather(low, "seq", axis=0)))
    return [
        lax.dynamic_slice_in_dim(part.reshape(-1), me * share, share, 0).astype(F32)
        for part, share in zip(got, shares)
    ]


def body(tokens, order, cotangent, qkv_weight, out_weight, up_weight, down_weight, small_params):
    slots = tokens.shape[1]
    dp_count = lax.axis_size("dp")
    me = lax.axis_index("seq")
    units = FF // (dp_count * 4)
    block_rows = D // dp_count
    ring = Ring(dp_count) if dp_count == 8 else Whole()
    start = jnp.where(me == 0, 0, jnp.where(me == 3, 12, 4 * me + 1)) * HD

    small_len = small_params.shape[0]
    wide = 3 * SPAN + D // 4

    blank = jnp.zeros((HEAD - 4, wide), BF16)
    small_row = jnp.pad(small_params.reshape(1, -1), ((0, 0), (0, wide - small_len)))
    attn_cols = lambda r: [
        jnp.concatenate([q, o], axis=1) for q, o in zip(head_cols(r[0]), own_cols(r[1]))
    ]
    if qkv_weight.shape[0] % (3 * D) == 0 and out_weight.shape[0] % D == 0:
        blocks = attn_cols([qkv_weight.reshape(-1, 3 * D), out_weight.reshape(-1, D)])
        share = blocks[0].shape[0]
        got = seq_exchange([jnp.concatenate([block, small_row]) for block in blocks], me)
        attn_chunk = jnp.concatenate([g[share:] for g in got] + [blank] + [g[:share] for g in got])
    else:
        attn_rows = split_rows([qkv_weight, out_weight], [3 * D, D], attn_cols, me)
        small_rows = xor_order(list(seq_gather(small_row)), me)
        attn_chunk = jnp.concatenate(small_rows + [blank, attn_rows])
    attn_chunk, up_flat = tied(attn_chunk, up_weight)
    attn_ring = ring.gather_attn(attn_chunk)
    attn_ring.step()
    if block_rows == 136:
        up_four = split_units(me, up_flat.reshape(-1, FF), dp_count)
        up_rows = jnp.concatenate(xor_order(rel_exchange(up_four), me))
    else:
        up_rows = split_rows([up_flat], [FF], lambda r: unit_cols(r[0], dp_count), me)
    positions = jnp.concatenate(xor_order(order.reshape(4, slots), me))
    positions = attn_ring.tie(positions)
    attn_ring.step()
    own_tokens = tokens.reshape(-1, D)
    other_tokens, across_tokens = seq_blocks(widened(own_tokens))
    unit_one = first_norm(own_tokens, other_tokens, across_tokens)
    unit_one, up_rows = attn_ring.tie((unit_one, up_rows))
    own_grad = attn_ring.tie(cotangent.reshape(-1, D))
    attn_ring.step()
    other_grad = lax.ppermute(widened(own_grad), "seq", CHIP_SWAP)
    other_grad, *mlp_rows = attn_ring.tie((other_grad, up_rows, down_weight.reshape(-1, D)))
    mlp_ring = ring.gather_two(*mlp_rows)
    across_grad = jnp.stack([widened(own_grad), other_grad])
    across_grad = lax.ppermute(across_grad, "seq", CORE_SWAP)
    grad_all = join_blocks(own_grad, other_grad, across_grad)
    w_qkv, small_all, out_sends = attn_ring.finish()
    mlp_ring.step()
    w_qkv = w_qkv.reshape(D, 3 * SPAN)
    small_full = small_all[:, :4, :small_len].reshape(-1).astype(F32)
    out_pieces = rel_exchange(out_sends)

    at = lambda i: small_full[i * D : (i + 1) * D]
    ln1_gain, ln1_bias, q_bias, v_bias, out_bias, ln2_gain, ln2_bias = [at(i) for i in range(7)]
    up_bias = small_full[7 * D : 7 * D + FF]
    down_bias = small_full[7 * D + FF : 8 * D + FF]

    window = lambda v: lax.dynamic_slice_in_dim(v, start, SPAN, 0)
    bias_qkv = jnp.concatenate([window(q_bias), jnp.zeros((SPAN,), F32), window(v_bias)])
    a_one, qkv_vals = qkv_kernel(unit_one, ln1_gain, ln1_bias, w_qkv, bias_qkv)
    a_one, qkv_vals = mlp_ring.tie((a_one, qkv_vals))
    mlp_ring.step()
    context, logs = mlp_ring.tie(attention(qkv_vals, positions))
    mlp_ring.step()
    w_out, send, keep = project(me, context, out_pieces)
    across = lax.ppermute(send, "seq", CORE_SWAP)
    pair, grad_all = tied(pair_sum(keep, across), grad_all)
    got = mlp_ring.tie(lax.ppermute(pair, "seq", CHIP_SWAP))
    mlp_ring.cut()
    got = mlp_ring.tie(got)
    w_up, w_down = (w.reshape(D, D) for w in mlp_ring.finish())
    residual, unit_two, scale_two, a_two = second_norm(
        pair, got, own_tokens, other_tokens, out_bias, ln2_gain, ln2_bias
    )
    a_across = lax.ppermute(a_two, "seq", CORE_SWAP)
    up_bias_own = lax.dynamic_index_in_dim(
        up_bias.reshape(dp_count, 4, units), me, 1, False
    ).reshape(-1)
    a_two_all, act_low, slope = mlp_up(a_two, a_across, w_up, up_bias_own)

    pre_low, send, keep, bias_cols = mlp_down_back(grad_all, w_down, slope, w_up)
    across = lax.ppermute(send, "seq", CORE_SWAP)
    pair, act_low, pre_low = tied(pair_sum(keep, across), act_low, pre_low)
    down_grad = inner_rows(act_low, grad_all).astype(BF16)
    up_grad = inner_rows(a_two_all, pre_low).astype(BF16)
    mlp_back = ring.reduce(
        down_grad.reshape(dp_count, units, D), up_grad.reshape(dp_count, block_rows, D)
    )
    mlp_back.step()
    up_bias_grad = lax.dynamic_update_slice(
        jnp.zeros((dp_count, 4, units), BF16),
        bias_cols.astype(BF16).reshape(dp_count, 1, units),
        (0, me, 0),
    ).reshape(-1)
    got, up_bias_grad = mlp_back.tie((lax.ppermute(pair, "seq", CHIP_SWAP), up_bias_grad))
    mlp_back.step()
    resid, resid_low, sums_two = second_norm_back(
        pair, got, unit_two, scale_two, ln2_gain, own_grad, other_grad
    )

    resid_across = lax.ppermute(resid_low, "seq", CORE_SWAP)
    out_four = out_gradient(me, context, resid_low, resid_across)
    back_ins = (w_out, logs, positions)
    qkv_low = attention_back(qkv_vals, resid_low, resid_across, *back_ins, 0, 2)
    out_four, resid_low, resid_across, qkv_low, act_low = mlp_back.tie(
        (out_four, resid_low, resid_across, qkv_low, act_low)
    )
    mlp_back.step()
    mlp_part = mm(act_low, w_down).astype(BF16).reshape(4, slots, D)
    mlp_abs = jnp.concatenate(xor_order(mlp_part, me))
    out_back = join_windows(xor_order(rel_exchange(out_four), me), 0)
    qkv_low = attention_back(qkv_vals, resid_low, resid_across, *back_ins, 2, WINDOW, qkv_low)
    qkv_low, mlp_abs, out_back = mlp_back.tie((qkv_low, mlp_abs, out_back))
    mlp_back.step()
    mlp_out = lax.psum_scatter(mlp_abs, "seq", scatter_dimension=0, tiled=True).astype(F32)
    mixed = (residual + mlp_out + down_bias).astype(BF16).reshape(tokens.shape)
    send, keep, sums_one, bias_sums = first_norm_back(qkv_low, w_qkv, unit_one)
    bias_sums = bias_sums.reshape(-1)
    placed = lambda v: lax.dynamic_update_slice(jnp.zeros((D,), F32), v, (start,))
    q_bias_grad = placed(bias_sums[:SPAN])
    v_bias_grad = placed(bias_sums[2 * SPAN :])

    small_grad = jnp.concatenate(
        [
            sums_one[0].astype(BF16),
            sums_one[1].astype(BF16),
            q_bias_grad.astype(BF16),
            v_bias_grad.astype(BF16),
            sums_two[2].astype(BF16),
            sums_two[0].astype(BF16),
            sums_two[1].astype(BF16),
            up_bias_grad,
            sums_two[3].astype(BF16),
            jnp.zeros((small_full.shape[0] - 8 * D - FF,), BF16),
        ]
    )
    small_grad = jnp.pad(
        small_grad.reshape(dp_count, 4, small_len), ((0, 0), (0, HEAD - 4), (0, wide - small_len))
    )
    out_back = out_back.reshape(dp_count, block_rows, D // 4)
    if block_rows == 136:
        parts = attn_parts(a_one, qkv_low, out_back, small_grad)
    else:
        qkv_grad = inner_rows(a_one, qkv_low).astype(BF16)
        parts = jnp.concatenate([qkv_grad.reshape(dp_count, block_rows, -1), out_back], axis=2)
        parts = jnp.concatenate([small_grad, parts], axis=1)
    attn_back = ring.reduce(parts, cut=80)
    attn_back.step()
    down_sum, up_sum = mlp_back.finish()
    near, far = core_sums(keep, lax.ppermute(send, "seq", CORE_SWAP))
    down_sum, up_sum, near, far = attn_back.tie((down_sum, up_sum, near, far))
    attn_back.step()
    got = attn_back.tie(lax.ppermute(far, "seq", CHIP_SWAP))
    attn_back.step()
    mixed = attn_back.tie(mixed)
    input_grad = input_back(own_tokens, ln1_gain, near, got, resid).reshape(tokens.shape)
    (up_part,) = join_rows(
        up_sum, [up_weight.shape[0]], [FF], lambda four: (join_unit_cols(four, dp_count),), me
    )
    (attn_sum,) = attn_back.finish()
    down_part = down_sum.reshape(-1)
    join_attn = lambda four: (
        join_head_cols([f[:, : 3 * SPAN] for f in four]),
        jnp.concatenate([f[:, 3 * SPAN :] for f in four], axis=1),
    )
    low = attn_sum.astype(BF16)
    if qkv_weight.shape[0] % (3 * D) == 0 and out_weight.shape[0] % D == 0:
        share = block_rows // 4
        got = seq_exchange(
            [
                jnp.concatenate([low[HEAD + m * share : HEAD + (m + 1) * share], low[m : m + 1]])
                for m in range(4)
            ],
            me,
        )
        small_got = [g[share:, :small_len] for g in got]
        qkv_part, out_part = (
            part.astype(F32).reshape(-1) for part in join_attn([g[:share] for g in got])
        )
    else:
        small_got = seq_exchange([low[m : m + 1, :small_len] for m in range(4)], me)
        qkv_part, out_part = join_rows(
            attn_sum[HEAD:],
            [qkv_weight.shape[0], out_weight.shape[0]],
            [3 * D, D],
            join_attn,
            me,
        )
    small_part = sum(g.astype(F32) for g in small_got).reshape(-1)
    return (mixed, input_grad, qkv_part, out_part, up_part, down_part, small_part)


def solution(mesh):
    rows, flat = P("dp", "seq", None), P(("dp", "seq"))
    return jax.shard_map(
        body,
        mesh=mesh,
        in_specs=(rows, P("dp", None), rows, flat, flat, flat, flat, flat),
        out_specs=(rows, rows, flat, flat, flat, flat, flat),
        check_vma=False,
    )
```
